128 devices in a mesh: wide: 32 (over y, z, core), narrow: 4 (over x).
Axes of the slice: x: 4, y: 4, z: 4, core: 2. Of those that a mesh axis runs over, the one named last changes fastest.
Arguments:
- tokens: bfloat16 [4096, 2048], P('wide', 'narrow'), may hold values from -6 to 6
- ln_gain: float32 [2048], P('narrow'), may hold values from 0.5 to 1.5
- ln_bias: float32 [2048], P('narrow'), may hold values from -4 to 4
- w_query: bfloat16 [2048, 2048], P('narrow', 'wide'), may hold values from -0.125 to 0.125
- b_query: bfloat16 [2048], P('wide'), may hold values from -4 to 4
- w_key: bfloat16 [2048, 2048], P('narrow', 'wide'), may hold values from -0.125 to 0.125
- b_key: bfloat16 [2048], P('wide'), may hold values from -4 to 4
- w_value: bfloat16 [2048, 2048], P('narrow', 'wide'), may hold values from -0.125 to 0.125
- b_value: bfloat16 [2048], P('wide'), may hold values from -4 to 4
- w_out: bfloat16 [2048, 2048], P('wide', 'narrow'), may hold values from -0.75 to 0.75
- b_out: bfloat16 [2048], P('narrow'), may hold values from -4 to 4
- w_fc1: bfloat16 [2048, 8192], P('narrow', 'wide'), may hold values from -0.125 to 0.125
- b_fc1: bfloat16 [8192], P('wide'), may hold values from -4 to 4
- w_fc2: bfloat16 [8192, 2048], P('wide', 'narrow'), may hold values from -0.0625 to 0.0625
- b_fc2: bfloat16 [2048], P('narrow'), may hold values from -4 to 4
- cotangent: bfloat16 [4096, 2048], P('wide', 'narrow'), may hold values from -6 to 6
- lengths: int32 [2], replicated, may hold values from 1024 to 2048, as said below
- dealing: int32 [32], replicated, may hold values from 0 to 31, as said below
Outputs:
- block_output: bfloat16 [4096, 2048], P('wide', 'narrow')
- input_grad: float32 [4096, 2048], P('wide', 'narrow')
- grad_ln_gain: float32 [2048], P('narrow')
- grad_ln_bias: float32 [2048], P('narrow')
- grad_w_query: float32 [2048, 2048], P('narrow', 'wide')
- grad_b_query: float32 [2048], P('wide')
- grad_w_key: float32 [2048, 2048], P('narrow', 'wide')
- grad_b_key: float32 [2048], P('wide')
- grad_w_value: float32 [2048, 2048], P('narrow', 'wide')
- grad_b_value: float32 [2048], P('wide')
- grad_w_out: float32 [2048, 2048], P('wide', 'narrow')
- grad_b_out: float32 [2048], P('narrow')
- grad_w_fc1: float32 [2048, 8192], P('narrow', 'wide')
- grad_b_fc1: float32 [8192], P('wide')
- grad_w_fc2: float32 [8192, 2048], P('wide', 'narrow')
- grad_b_fc2: float32 [2048], P('narrow')
The draws below stay inside these ranges and needn't reach their ends.
Inputs may be any that keep to these rules, and one draw needn't show every extreme that they name: `lengths`: each sequence holds at least 1024 tokens; one sequence holds exactly 2048. `dealing`: a permutation of the 32 logical blocks.
All inputs are finite; a program needn't handle non-finite values.
Results may differ from the reference program's by a relative error of at most 0.015.
Values may be sent and summed in bfloat16 or wider, within the bound.
A program may use at most 128 MiB of HBM per device.

```python
import jax
import jax.numpy as jnp
from jax import lax

D = 2048
HEADS = 32
HEAD_DIM = 64
ROT = 32
FF = 8192
BLOCK = 128
MAXLEN = 2048
TOKENS = 4096
NSEQ = 2
NBLK = 32


def draw_lengths(key, part):
    key = jax.random.fold_in(key, 11)
    pick_key, length_key = jax.random.split(key)
    drawn = jax.random.randint(length_key, (NSEQ,), MAXLEN // 2, MAXLEN + 1)
    chosen = jax.random.randint(pick_key, (), 0, NSEQ)
    return jnp.where(jnp.arange(NSEQ) == chosen, MAXLEN, drawn).astype(jnp.int32)


def draw_dealing(key, part):
    key = jax.random.fold_in(key, 23)
    return jax.random.permutation(key, NBLK).astype(jnp.int32)


def block_scale(key, extent, pieces, low, high):
    factor_of, own = 1.0, jax.random.fold_in(key, 6)
    for dim, parts in pieces:
        draws = jnp.exp(jax.random.uniform(jax.random.fold_in(own, dim), (parts,), jnp.float32, low / len(pieces), high / len(pieces)))
        factor_of = factor_of * jnp.repeat(draws, extent[dim] // parts).reshape([-1 if axis == dim else 1 for axis in range(len(extent))])
    return factor_of


def bell_draw(key, shape, deviation, most, cuts=(), held_as=jnp.bfloat16):
    level = block_scale(key, shape, cuts, -0.22, 0.18) if cuts else 1.0
    values = jax.random.normal(key, shape, jnp.float32) * deviation * level
    return jnp.minimum(jnp.maximum(values, -most), most).astype(held_as)


def setup_inputs(seed: int = 0) -> dict:
    seeds = jax.random.split(jax.random.key(seed), 19)
    tokens = bell_draw(seeds[0], (TOKENS, D), 1.0, 6.0, ((0, 32), (1, 4)))
    ln_gain = jnp.clip(1.0 + 0.1 * jax.random.normal(seeds[1], (D,), jnp.float32), 0.5, 1.5)
    ln_bias = bell_draw(seeds[2], (D,), 0.3, 4.0, ((0, 4),), jnp.float32)
    w_query = bell_draw(seeds[3], (D, D), D ** -0.5, 0.125, ((0, 4), (1, 32)))
    b_query = bell_draw(seeds[4], (D,), 0.3, 4.0, ((0, 32),))
    w_key = bell_draw(seeds[5], (D, D), D ** -0.5, 0.125, ((0, 4), (1, 32)))
    b_key = bell_draw(seeds[6], (D,), 0.3, 4.0, ((0, 32),))
    w_value = bell_draw(seeds[7], (D, D), D ** -0.5, 0.125, ((0, 4), (1, 32)))
    b_value = bell_draw(seeds[8], (D,), 0.3, 4.0, ((0, 32),))
    w_out = bell_draw(seeds[9], (D, D), (D // 32) ** -0.5, 0.75, ((0, 32), (1, 4)))
    b_out = bell_draw(seeds[10], (D,), 0.3, 4.0, ((0, 4),))
    w_fc1 = bell_draw(seeds[11], (D, FF), D ** -0.5, 0.125, ((0, 4), (1, 32)))
    b_fc1 = bell_draw(seeds[12], (FF,), 0.3, 4.0, ((0, 32),))
    w_fc2 = bell_draw(seeds[13], (FF, D), FF ** -0.5, 0.0625, ((0, 32), (1, 4)))
    b_fc2 = bell_draw(seeds[14], (D,), 0.3, 4.0, ((0, 4),))
    cotangent = bell_draw(seeds[15], (TOKENS, D), 1.0, 6.0, ((0, 32), (1, 4)))
    lengths = draw_lengths(jax.random.fold_in(seeds[18], 71), 0)
    dealing = draw_dealing(jax.random.fold_in(seeds[18], 71), 0)
    return {"tokens": tokens, "ln_gain": ln_gain, "ln_bias": ln_bias, "w_query": w_query, "b_query": b_query, "w_key": w_key, "b_key": b_key, "w_value": w_value, "b_value": b_value, "w_out": w_out, "b_out": b_out, "w_fc1": w_fc1, "b_fc1": b_fc1, "w_fc2": w_fc2, "b_fc2": b_fc2, "cotangent": cotangent, "lengths": lengths, "dealing": dealing}


epsilon = 1e-05
highest = lax.Precision.HIGHEST

@jax.custom_vjp
def low(v):
    return lax.optimization_barrier(v.astype(jnp.bfloat16)).astype(jnp.float32)

@jax.custom_vjp
def low_back(v):
    return v

def low_keep(v):
    return (low(v), None)

def low_pass(kept, grad):
    return (grad,)

def back_keep(v):
    return (v, None)

def back_low(kept, grad):
    return (low(grad),)
low.defvjp(low_keep, low_pass)
low_back.defvjp(back_keep, back_low)

def rotate(matrix, position, direction):
    halfway = ROT // 2
    inverse_freq = 10000.0 ** (-(jnp.arange(halfway, dtype=jnp.float32) * 2.0 / ROT))
    angles = position.astype(jnp.float32)[:, None] * inverse_freq[None, :]
    cosine = jnp.cos(angles)[:, None, :]
    sine_part = direction * jnp.sin(angles)[:, None, :]
    first_half = matrix[..., :halfway]
    second = matrix[..., halfway:ROT]
    return jnp.concatenate([first_half * cosine - second * sine_part, second * cosine + first_half * sine_part, matrix[..., ROT:]], -1)

def reference(tokens, ln_gain, ln_bias, w_query, b_query, w_key, b_key, w_value, b_value, w_out, b_out, w_fc1, b_fc1, w_fc2, b_fc2, cotangent, lengths, dealing):
    blocks = dealing.shape[0]
    inverse = jnp.zeros((blocks,), jnp.int32).at[dealing].set(jnp.arange(blocks, dtype=jnp.int32))

    def to_logical(array):
        return array.reshape(blocks, BLOCK, -1)[inverse].reshape(NSEQ, MAXLEN, -1)

    def to_slots(array):
        return array.reshape(blocks, BLOCK, -1)[dealing].reshape(NSEQ * MAXLEN, -1)
    position = jnp.arange(MAXLEN, dtype=jnp.int32)
    valid = (position[None, :] < lengths[:, None]).astype(jnp.float32)
    scale = HEAD_DIM ** (-0.5)

    def attend(args):
        query_lin, key_lin, value_lin, length = args
        queries = low(rotate(query_lin.reshape(MAXLEN, HEADS, HEAD_DIM), position, 1.0))
        keys_low = low(rotate(key_lin.reshape(MAXLEN, HEADS, HEAD_DIM), position, 1.0))
        values_low = low(value_lin.reshape(MAXLEN, HEADS, HEAD_DIM))
        raw_scores = low_back(jnp.einsum('qhd,khd->hqk', queries, keys_low, precision=highest))
        allowed = (position[None, :] <= position[:, None]) & (position[None, :] < length)
        scores = jnp.where(allowed[None], raw_scores * scale, -1e+30)
        maxima = lax.optimization_barrier(jnp.max(scores, -1, keepdims=True))
        expo = jnp.exp(scores - maxima)
        probs = low(expo / lax.optimization_barrier(jnp.sum(expo, -1, keepdims=True)))
        mixed = jnp.einsum('hqk,khd->qhd', probs, values_low, precision=highest)
        return mixed.reshape(MAXLEN, D)

    def forward(inputs, gain, shift, query_w, query_b, key_w, key_b, value_w, value_b, out_w, out_b, up_w, up_b, down_w, down_b):
        row_mean = lax.optimization_barrier(jnp.mean(inputs, -1, keepdims=True))
        row_var = lax.optimization_barrier(jnp.mean(inputs * inputs, -1, keepdims=True)) - row_mean * row_mean
        normed = (inputs - row_mean) * lax.rsqrt(row_var + epsilon)
        ln_low = low(normed * gain + shift)

        def project(weight, bias):
            return jnp.einsum('std,de->ste', ln_low, weight, precision=highest) + bias
        query_lin = low_back(project(query_w, query_b))
        key_lin = low_back(project(key_w, key_b))
        value_lin = low_back(project(value_w, value_b))
        units = low_back(project(up_w, up_b))
        hidden = low(jax.nn.gelu(units, approximate=True))
        attended = lax.map(jax.checkpoint(attend), (query_lin, key_lin, value_lin, lengths))
        attended = low(low_back(attended))
        branch = jnp.einsum('std,de->ste', attended, out_w, precision=highest) + out_b
        branch = branch + jnp.einsum('stf,fd->std', hidden, down_w, precision=highest) + down_b
        return inputs + valid[..., None] * branch
    params = (ln_gain, ln_bias, w_query, b_query, w_key, b_key, w_value, b_value, w_out, b_out, w_fc1, b_fc1, w_fc2, b_fc2)
    floats = [param.astype(jnp.float32) for param in params]
    inputs = to_logical(tokens.astype(jnp.float32))
    result, pullback = jax.vjp(forward, inputs, *floats)
    grads = pullback(to_logical(cotangent.astype(jnp.float32)))
    return (to_slots(result).astype(jnp.bfloat16), to_slots(grads[0]), grads[1], grads[2], grads[3], grads[4], grads[5], grads[6], grads[7], grads[8], grads[9], grads[10], grads[11], grads[12], grads[13], grads[14])
```

```python
import functools

import jax
import jax.numpy as jnp
import numpy as np
from jax import lax
from jax.experimental import pallas as pl
from jax.experimental.pallas import tpu as pltpu
from jax.sharding import PartitionSpec as P

MESH = pl.DeviceIdType.MESH
D = 2048
HEAD_DIM = 64
ROT = 32
BLOCK = 128
MAXLEN = 2048
NBLK = 32
PART = 32
ROWS = NBLK * PART
COLS = 512
UNITS = 256
EPS = 1e-05
BF16 = jnp.bfloat16
F32 = jnp.float32


def rope_tables():
    half = ROT // 2
    inverse = (10000.0 ** (-(np.arange(half, dtype=np.float32) * np.float32(2.0) / np.float32(ROT)))).astype(np.float32)
    angles = (np.arange(MAXLEN, dtype=np.float32)[:, None] * inverse[None, :]).astype(np.float64)
    cosine = np.ones((MAXLEN, 128), np.float32)
    sine = np.zeros((MAXLEN, 128), np.float32)
    cosine[:, :half] = np.cos(angles)
    cosine[:, half:ROT] = np.cos(angles)
    sine[:, :half] = -np.sin(angles)
    sine[:, half:ROT] = np.sin(angles)
    return cosine, sine


class Net:
    def __init__(self, send, recv):
        self.send, self.recv, self.used, self.open = send, recv, 0, []

    def copy(self, src, dst, device):
        i = self.used
        self.used += 1
        c = pltpu.make_async_remote_copy(
            src_ref=src,
            dst_ref=dst,
            send_sem=self.send.at[i],
            recv_sem=self.recv.at[i],
            device_id=device,
            device_id_type=MESH,
        )
        c.start()
        self.open.append(c)
        return c

    def drain(self):
        for c in self.open:
            c.wait_send()


class Ring:
    def __init__(self, net, me, device, unit, half):
        self.net, self.unit, self.half = net, unit, half
        self.right, self.left = (me + 1) % 4, (me + 3) % 4
        self.to_right, self.to_left = device(self.right), device(self.left)
        self.me = me

    def start(self):
        own = self.unit(self.me)
        self.a = self.net.copy(own, own, self.to_right)
        self.b = self.net.copy(own, own, self.to_left)

    def forward(self):
        self.a.wait_recv()
        x = self.half(self.left, 0)
        self.c = self.net.copy(x, x, self.to_right)
        self.b.wait_recv()
        x = self.half(self.right, 1)
        self.d = self.net.copy(x, x, self.to_left)

    def finish(self):
        self.c.wait_recv()
        self.d.wait_recv()


def coords():
    w, n = lax.axis_index("wide"), lax.axis_index("narrow")
    return w // 8, (w // 2) % 4, w % 2, n


def wide_of(y, z, c):
    return (y * 4 + z) * 2 + c


def aligned(x, m):
    return pl.multiple_of(x, m)


def slot_a(c, z, y):
    return aligned(((c * 4 + z) * 4 + y) * 16, 16)


def slot_b(c, y, z):
    return aligned((32 + (c * 4 + y) * 4 + z) * 16, 16)


class WideGather:
    def __init__(self, net, buf, y, z, c, n):
        self.net, self.buf, self.y, self.z, self.c = net, buf, y, z, c

        def dev(y, z, c):
            return (wide_of(y, z, c), n)

        def rows(start, count):
            return buf.at[pl.ds(start, count)]

        def cols(start, h):
            return buf.at[pl.ds(start, 16), pl.ds(h * 1024, 1024)]

        def half(start, h):
            return buf.at[pl.ds(aligned(start + 32 * h, 16), 32)]

        self.rows = rows
        self.other = dev(y, z, 1 - c)
        self.one = (
            Ring(net, y, lambda i: dev(i, z, c), lambda i: rows(slot_a(c, z, i), 16), lambda i, h: cols(slot_a(c, z, i), h)),
            Ring(net, z, lambda i: dev(y, i, c), lambda i: rows(slot_b(c, y, i), 16), lambda i, h: cols(slot_b(c, y, i), h)),
        )
        self.two = (
            Ring(net, z, lambda i: dev(y, i, c), lambda i: rows(slot_a(c, i, 0), 64), lambda i, h: half(slot_a(c, i, 0), h)),
            Ring(net, y, lambda i: dev(i, z, c), lambda i: rows(slot_b(c, i, 0), 64), lambda i, h: half(slot_b(c, i, 0), h)),
        )
        self.cross = []

    def _cross(self, i):
        for part, slot in ((0, slot_a), (1, slot_b)):
            me = (self.z, self.y)[part]
            x = self.rows(slot(self.c, (me + i) % 4, 0), 64)
            self.cross.append(self.net.copy(x, x, self.other))

    def start(self):
        for r in self.one:
            r.start()

    def forward(self):
        for r in self.one:
            r.forward()

    def second(self):
        for r in self.one:
            r.finish()
        for r in self.two:
            r.start()
        self._cross(0)

    def forward_second(self):
        for r in self.two:
            r.forward()
        self._cross(1)
        self._cross(3)

    def finish(self):
        for r in self.two:
            r.finish()
        self._cross(2)
        for x in self.cross:
            x.wait_recv()


def greet(y, z, c, n):
    peers = [
        (wide_of((y + 1) % 4, z, c), n),
        (wide_of((y + 3) % 4, z, c), n),
        (wide_of(y, (z + 1) % 4, c), n),
        (wide_of(y, (z + 3) % 4, c), n),
        (wide_of(y, z, 1 - c), n),
        (wide_of(y, z, c), (n + 1) % 4),
        (wide_of(y, z, c), (n + 2) % 4),
        (wide_of(y, z, c), (n + 3) % 4),
    ]
    barrier = pltpu.get_barrier_semaphore()
    for p in peers:
        pl.semaphore_signal(barrier, inc=1, device_id=p, device_id_type=MESH)
    pl.semaphore_wait(barrier, len(peers))


def nt(a, b):
    return lax.dot_general(a, b, (((1,), (1,)), ((), ())), preferred_element_type=F32)


GELU_A = float(np.sqrt(2.0 / np.pi))
GELU_B = 0.044715


def first_kernel(
    chunk_ref, tok, cot, wq, wk, wv, wu, wo, wd, gb, bias, cosine, sine,
    ln, g, w, wm, xhat, q_log, do_log, kv, h_out, du_out,
    xs, gbs, pre, qp, dop, u, send, recv, local,
):
    y, z, c, n = coords()
    net = Net(send, recv)
    my_cols = pl.ds(aligned(n * COLS, COLS), COLS)
    my_rows = pl.ds(aligned(n * PART, PART), PART)
    me = wide_of(y, z, c)
    own_a, own_b = slot_a(c, z, y), slot_b(c, y, z)

    w[0:64, my_cols] = wk[...].T
    w[64:128, my_cols] = wv[...].T
    w[128:192, my_cols] = wq[...].T
    w[192:448, my_cols] = wu[...].T
    wm[0:64, my_cols] = wo[...]
    wm[64:320, my_cols] = wd[...]
    gbs[n] = gb[...]
    xs[:, my_cols] = tok[my_rows, :]
    g[pl.ds(own_a, 16), my_cols] = cot[pl.ds(aligned(n * PART, 16), 16), :]
    g[pl.ds(own_b, 16), my_cols] = cot[pl.ds(aligned(n * PART + 16, 16), 16), :]
    greet(y, z, c, n)

    def to(m):
        return (me, m)

    early, late = [], []
    for j in (1, 3, 2):
        m = (n + j) % 4
        early.append(net.copy(gbs.at[n], gbs.at[n], to(m)))
        early.append(net.copy(tok.at[pl.ds(aligned(m * PART, PART), PART)], xs.at[:, my_cols], to(m)))
    for j in (1, 3, 2):
        m = (n + j) % 4
        late.append(net.copy(cot.at[pl.ds(aligned(m * PART, 16), 16)], g.at[pl.ds(own_a, 16), my_cols], to(m)))
        late.append(net.copy(cot.at[pl.ds(aligned(m * PART + 16, 16), 16)], g.at[pl.ds(own_b, 16), my_cols], to(m)))

    def w_cols(i):
        return pl.ds(aligned(i * COLS, COLS), COLS)

    w_ring = Ring(net, n, to, lambda i: w.at[pl.ds(0, 448), w_cols(i)], lambda i, h: w.at[pl.ds(h * 224, 224), w_cols(i)])
    o_ring = Ring(net, n, to, lambda i: wm.at[pl.ds(0, 64), w_cols(i)], lambda i, h: wm.at[pl.ds(h * 32, 32), w_cols(i)])
    d_ring = Ring(net, n, to, lambda i: wm.at[pl.ds(64, 256), w_cols(i)], lambda i, h: wm.at[pl.ds(64 + h * 128, 128), w_cols(i)])
    w_ring.start()

    for x in early:
        x.wait_recv()
    x = xs[...].astype(F32)
    mean = jnp.sum(x, 1, keepdims=True) / D
    var = jnp.sum(x * x, 1, keepdims=True) / D - mean * mean
    inv = lax.rsqrt(var + EPS)
    xhat[...] = (x - mean) * inv
    for i in range(4):
        cs = slice(i * COLS, (i + 1) * COLS)
        low = (xhat[:, cs] * gbs[i, 0:1, :] + gbs[i, 1:2, :]).astype(BF16)
        ln[pl.ds(own_a, 16), cs] = low[0:16]
        ln[pl.ds(own_b, 16), cs] = low[16:32]

    lg = WideGather(net, ln, y, z, c, n)
    gg = WideGather(net, g, y, z, c, n)
    lg.start()
    for x in late:
        x.wait_recv()
    lg.forward()
    gg.start()
    lg.second()
    gg.forward()
    w_ring.forward()
    lg.forward_second()
    gg.second()
    o_ring.start()
    lg.finish()
    w_ring.finish()
    o_ring.forward()
    gg.forward_second()

    w[448:640, :] = w[0:192, :]
    w[640:656, :] = w[144:160, :]
    w[656:672, :] = w[128:144, :]
    w[672:688, :] = w[16:32, :]
    w[688:704, :] = w[0:16, :]

    def project(i, _):
        r = pl.ds(aligned(i * 256, 256), 256)
        x = ln[r, :]
        pre[pl.ds(i * 16, 16)] = (nt(x, w[448:704, :]) + bias[:, 0:256]).reshape(16, 16, 256)
        return 0

    lax.fori_loop(0, 4, project, 0)
    def arrange(i, _):
        both = pre[chunk_ref[i]]
        r = pl.ds(aligned(i * 16, 16), 16)
        tab = pl.ds(aligned((i % 32) * 16, 16), 16)
        a, b = both[:, 0:128], both[:, 128:256]
        cs, sn = cosine[tab, :], sine[tab, :]
        kv[n, r, :] = (a * cs + pltpu.roll(b, 32, 1) * sn).astype(BF16)
        q_log[r, :] = (b * cs + pltpu.roll(b, 64, 1) * sn).astype(BF16)
        return 0

    lax.fori_loop(0, 64, arrange, 0)
    kv_ring = Ring(net, n, to, lambda i: kv.at[i], lambda i, h: kv.at[i, pl.ds(h * 512, 512)])
    kv_ring.start()
    d_ring.start()

    def project_up(i, _):
        r = pl.ds(aligned(i * 256, 256), 256)
        u[r, :] = nt(ln[r, :], w[192:448, :]) + bias[:, 256:512]
        return 0

    lax.fori_loop(0, 4, project_up, 0)
    gg.finish()
    o_ring.finish()

    def grad_o(i, _):
        r = pl.ds(aligned(i * 256, 256), 256)
        dop[pl.ds(i * 16, 16)] = nt(g[r, :], wm[0:64, :]).reshape(16, 16, 64)
        return 0

    lax.fori_loop(0, 4, grad_o, 0)

    def arrange_do(i, _):
        do_log[pl.ds(aligned(i * 16, 16), 16), :] = dop[chunk_ref[i]].astype(BF16)
        return 0

    lax.fori_loop(0, 64, arrange_do, 0)
    kv_ring.forward()
    d_ring.forward()
    kv_ring.finish()
    d_ring.finish()

    def units(i, _):
        r = pl.ds(aligned(i * 256, 256), 256)
        v = u[r, :]
        dh = nt(g[r, :], wm[64:320, :])
        t = jnp.tanh(GELU_A * (v + GELU_B * (v * v * v)))
        h_out[r, :] = (0.5 * v * (1.0 + t)).astype(BF16)
        slope = 0.5 * (1.0 + t) + 0.5 * v * (1.0 - t * t) * (GELU_A * (1.0 + 3.0 * GELU_B * (v * v)))
        du_out[r, :] = (dh * slope).astype(BF16)
        return 0

    lax.fori_loop(0, 4, units, 0)
    net.drain()


def call_first(chunk, tok, cot, wq, wk, wv, wu, wo, wd, gb, bias, cosine, sine):
    vmem = pl.BlockSpec(memory_space=pltpu.VMEM)
    shape = jax.ShapeDtypeStruct
    return pl.pallas_call(
        first_kernel,
        out_shape=(
            shape((ROWS, D), BF16),
            shape((ROWS, D), BF16),
            shape((704, D), BF16),
            shape((320, D), BF16),
            shape((PART, D), F32),
            shape((ROWS, 128), BF16),
            shape((ROWS, 64), BF16),
            shape((4, ROWS, 128), BF16),
            shape((ROWS, UNITS), BF16),
            shape((ROWS, UNITS), BF16),
        ),
        in_specs=[pl.BlockSpec(memory_space=pltpu.SMEM)] + [vmem] * 12,
        out_specs=(vmem,) * 10,
        scratch_shapes=[
            pltpu.VMEM((PART, D), BF16),
            pltpu.VMEM((4, 8, COLS), F32),
            pltpu.VMEM((64, 16, 256), F32),
            pltpu.VMEM((8, 128), F32),
            pltpu.VMEM((64, 16, 64), F32),
            pltpu.VMEM((ROWS, UNITS), F32),
            pltpu.SemaphoreType.DMA((80,)),
            pltpu.SemaphoreType.DMA((80,)),
            pltpu.SemaphoreType.DMA((2,)),
        ],
        compiler_params=pltpu.CompilerParams(collective_id=0, has_side_effects=True, vmem_limit_bytes=56 * 2**20),
    )(chunk, tok, cot, wq, wk, wv, wu, wo, wd, gb, bias, cosine, sine)


def rotate_back(x, cosine, sine):
    half = ROT // 2
    swapped = jnp.concatenate([x[:, half:ROT], x[:, :half], x[:, ROT:]], 1)
    return x * cosine - swapped * sine


def on_device(
    tokens, ln_gain, ln_bias, w_query, b_query, w_key, b_key, w_value, b_value, w_out, b_out,
    w_fc1, b_fc1, w_fc2, b_fc2, cotangent, lengths, dealing,
):
    n, wide = lax.axis_index("narrow"), lax.axis_index("wide")
    per_seq = MAXLEN // BLOCK
    blocks = jnp.arange(NBLK, dtype=jnp.int32)
    inverse = jnp.sum(jnp.where(dealing[None, :] == blocks[:, None], blocks[None, :], 0), 1)
    iy, iz, ic = inverse // 8, (inverse // 2) % 4, inverse % 2
    starts = jnp.stack([((ic * 4 + iz) * 4 + iy) * 16, (32 + (ic * 4 + iy) * 4 + iz) * 16], 1).reshape(-1)

    mine = jnp.sum(jnp.where(blocks == wide, dealing, 0))
    limit = jnp.where(mine // per_seq == 0, lengths[0], lengths[1])
    valid_local = mine % per_seq * BLOCK + jnp.arange(BLOCK, dtype=jnp.int32) < limit
    cot_masked = jnp.where(valid_local[:, None], cotangent, jnp.zeros_like(cotangent))

    half = ROT // 2
    zero = jnp.zeros((6, COLS), F32)
    gb = jnp.concatenate([ln_gain[None], ln_bias[None], zero], 0)
    bias = jnp.concatenate(
        [
            b_key, b_value, b_query, b_query[half:ROT], b_query[:half], b_key[half:ROT], b_key[:half], b_fc1,
        ]
    ).astype(F32)[None]
    cosine, sine = rope_tables()
    shares = [t.reshape(per_seq, 4, PART, 128) for t in (cosine, sine)]
    cos_n, sin_n = (lax.dynamic_index_in_dim(jnp.asarray(t), n, 1, False).reshape(-1, 128) for t in shares)
    ln, g, w, wm, xhat, q, do, kv, h, du = call_first(
        starts // 16, tokens, cot_masked, w_query, w_key, w_value, w_fc1, w_out, w_fc2, gb, bias, cos_n, sin_n
    )

    q = q[:, :64]
    offset = jnp.arange(PART, dtype=jnp.int32)
    seq_q = jnp.repeat(blocks // per_seq, PART)
    pos_q = (blocks[:, None] % per_seq * BLOCK + n * PART + offset[None]).reshape(-1)
    keys = kv.reshape(4, NBLK, PART, 128).transpose(1, 0, 2, 3).reshape(-1, 128)
    k, v = keys[:, :64], keys[:, 64:]
    pos_k = jnp.tile(jnp.arange(MAXLEN, dtype=jnp.int32), 2)
    seq_k = jnp.repeat(jnp.arange(2, dtype=jnp.int32), MAXLEN)
    valid_k = pos_k < jnp.where(seq_k == 0, lengths[0], lengths[1])
    allowed = (seq_q[:, None] == seq_k[None]) & (pos_k[None] <= pos_q[:, None]) & valid_k[None]
    scale = HEAD_DIM**-0.5
    s = jnp.where(allowed, jnp.dot(q, k.T, preferred_element_type=F32) * scale, -1e30)
    p = jax.nn.softmax(s, -1)
    pb = p.astype(BF16)
    o = jnp.dot(pb, v, preferred_element_type=F32).astype(BF16)
    dp = jnp.dot(do, v.T, preferred_element_type=F32)
    ds = (p * (dp - jnp.sum(p * dp, -1, keepdims=True)) * scale).astype(BF16)
    dq = jnp.dot(ds, k, preferred_element_type=F32)
    dk = jnp.dot(ds.T, q, preferred_element_type=F32)
    dv = jnp.dot(pb.T, do, preferred_element_type=F32)
    dkv = jnp.concatenate([dk, dv], 1).reshape(NBLK, 4, PART, 128).transpose(1, 0, 2, 3)
    dkv = lax.psum_scatter(dkv, "narrow", scatter_dimension=0, tiled=True).reshape(ROWS, 128)
    c64 = jnp.tile(cos_n[:, :64], (2, 1))
    s64 = jnp.tile(sin_n[:, :64], (2, 1))
    dq = rotate_back(dq, c64, s64).astype(BF16)
    dk = rotate_back(dkv[:, :64], c64, s64).astype(BF16)
    logical = jnp.concatenate([dk, dkv[:, 64:].astype(BF16), dq, o], 1).reshape(64, 16, 256)
    chunks = jnp.arange(64, dtype=jnp.int32)
    back = jnp.sum(jnp.where((starts // 16)[None, :] == chunks[:, None], chunks[None, :], 0), 1)
    phys = logical[back].reshape(ROWS, 256)
    dqkv, o = phys[:, :192], phys[:, 192:]
    ones = jnp.ones((ROWS, 64), BF16)

    def by_device(x):
        a = x[:512].reshape(2, 4, 4, 16, D).transpose(2, 1, 0, 3, 4).reshape(32, 16, D)
        b = x[512:].reshape(2, 4, 4, 16, D).transpose(1, 2, 0, 3, 4).reshape(32, 16, D)
        return jnp.concatenate([a, b], 1).reshape(ROWS, D)

    def scatter_rows(x):
        return lax.psum_scatter(by_device(x.astype(BF16)), "wide", scatter_dimension=0, tiled=True)

    def turn(x):
        return lax.all_to_all(x, "narrow", 1, 0, tiled=True)

    branch = turn(scatter_rows(jnp.dot(jnp.concatenate([o, h], 1), wm, preferred_element_type=F32))).astype(F32)
    out_bias = b_out.astype(F32) + b_fc2.astype(F32)
    result = tokens.astype(F32) + valid_local[:, None].astype(F32) * (branch + out_bias)

    def gathered(x):
        return lax.psum_scatter(x, "narrow", scatter_dimension=1, tiled=True)

    grad_mix = gathered(lax.dot_general(jnp.concatenate([o, h, ones], 1), g, (((0,), (0,)), ((), ())), preferred_element_type=F32))
    dpre = jnp.concatenate([dqkv, du], 1)
    grad_in = gathered(lax.dot_general(dpre, ln, (((0,), (0,)), ((), ())), preferred_element_type=F32)).T
    grad_b_in = lax.psum(jnp.sum(dpre, 0, dtype=F32), "narrow")
    dln = scatter_rows(jnp.dot(dpre, w[:448], preferred_element_type=F32)).astype(F32)
    gain = lax.all_gather(ln_gain, "narrow", axis=0, tiled=True)
    e = dln * gain
    x = lax.all_gather(jnp.sum(tokens.astype(F32), 1), "narrow", axis=0)
    x2 = lax.all_gather(jnp.sum(tokens.astype(F32) ** 2, 1), "narrow", axis=0)
    mean = jnp.sum(x, 0) / D
    inv = lax.rsqrt(jnp.sum(x2, 0) / D - mean * mean + EPS)
    core = e - jnp.mean(e, 1, keepdims=True) - xhat * jnp.mean(e * xhat, 1, keepdims=True)
    input_grad = cotangent.astype(F32) + inv[:, None] * turn(core)
    sums = lax.psum(jnp.stack([jnp.sum(dln * xhat, 0), jnp.sum(dln, 0)]), "wide")
    sums = lax.psum_scatter(sums, "narrow", scatter_dimension=1, tiled=True)
    grad_b_out = grad_mix[320]
    return (
        result.astype(BF16),
        input_grad,
        sums[0],
        sums[1],
        grad_in[:, 128:192],
        grad_b_in[128:192],
        grad_in[:, 0:64],
        grad_b_in[0:64],
        grad_in[:, 64:128],
        grad_b_in[64:128],
        grad_mix[:64],
        grad_b_out,
        grad_in[:, 192:],
        grad_b_in[192:],
        grad_mix[64:320],
        grad_b_out,
    )


def solution(mesh):
    rows, col, units = P("wide", "narrow"), P("narrow"), P("wide")
    weight, out = P("narrow", "wide"), P("wide", "narrow")
    placed = (
        rows, col, col, weight, units, weight, units, weight, units, out, col, weight, units, out, col, rows, P(), P(),
    )
    given = (
        rows, rows, col, col, weight, units, weight, units, weight, units, out, col, weight, units, out, col,
    )
    return jax.shard_map(on_device, mesh=mesh, in_specs=placed, out_specs=given, check_vma=False)
```

```python
import jax
import jax.numpy as jnp
import numpy as np
from jax import lax
from jax.experimental import pallas as pl
from jax.experimental.pallas import tpu as pltpu
from jax.sharding import PartitionSpec as P

MESH = pl.DeviceIdType.MESH
D = 2048
HEAD_DIM = 64
ROT = 32
BLOCK = 128
MAXLEN = 2048
NBLK = 32
PART = 32
ROWS = NBLK * PART
COLS = 512
UNITS = 256
EPS = 1e-05
BF16 = jnp.bfloat16
F32 = jnp.float32


def rope_tables():
    half = ROT // 2
    inverse = (10000.0 ** (-(np.arange(half, dtype=np.float32) * np.float32(2.0) / np.float32(ROT)))).astype(np.float32)
    angles = (np.arange(MAXLEN, dtype=np.float32)[:, None] * inverse[None, :]).astype(np.float64)
    cosine = np.ones((MAXLEN, 128), np.float32)
    sine = np.zeros((MAXLEN, 128), np.float32)
    cosine[:, :half] = np.cos(angles)
    cosine[:, half:ROT] = np.cos(angles)
    sine[:, :half] = -np.sin(angles)
    sine[:, half:ROT] = np.sin(angles)
    return cosine, sine


class Net:
    def __init__(self, send, recv):
        self.send, self.recv, self.used, self.open = send, recv, 0, []

    def copy(self, src, dst, device):
        i = self.used
        self.used += 1
        c = pltpu.make_async_remote_copy(
            src_ref=src,
            dst_ref=dst,
            send_sem=self.send.at[i],
            recv_sem=self.recv.at[i],
            device_id=device,
            device_id_type=MESH,
        )
        c.start()
        self.open.append(c)
        return c

    def drain(self):
        for c in self.open:
            c.wait_send()


class Ring:
    def __init__(self, net, me, device, unit, half):
        self.net, self.unit, self.half = net, unit, half
        self.right, self.left = (me + 1) % 4, (me + 3) % 4
        self.to_right, self.to_left = device(self.right), device(self.left)
        self.me = me

    def start(self):
        own = self.unit(self.me)
        self.a = self.net.copy(own, own, self.to_right)
        self.b = self.net.copy(own, own, self.to_left)

    def forward(self):
        self.a.wait_recv()
        x = self.half(self.left, 0)
        self.c = self.net.copy(x, x, self.to_right)
        self.b.wait_recv()
        x = self.half(self.right, 1)
        self.d = self.net.copy(x, x, self.to_left)

    def finish(self):
        self.c.wait_recv()
        self.d.wait_recv()


def coords():
    w, n = lax.axis_index("wide"), lax.axis_index("narrow")
    return w // 8, (w // 2) % 4, w % 2, n


def wide_of(y, z, c):
    return (y * 4 + z) * 2 + c


def aligned(x, m):
    return pl.multiple_of(x, m)


def slot_a(c, z, y):
    return aligned(((c * 4 + z) * 4 + y) * 16, 16)


def slot_b(c, y, z):
    return aligned((32 + (c * 4 + y) * 4 + z) * 16, 16)


class WideGather:
    def __init__(self, net, buf, y, z, c, n):
        self.net, self.buf, self.y, self.z, self.c = net, buf, y, z, c

        def dev(y, z, c):
            return (wide_of(y, z, c), n)

        def rows(start, count):
            return buf.at[pl.ds(start, count)]

        def cols(start, h):
            return buf.at[pl.ds(start, 16), pl.ds(h * 1024, 1024)]

        def half(start, h):
            return buf.at[pl.ds(aligned(start + 32 * h, 16), 32)]

        self.rows = rows
        self.other = dev(y, z, 1 - c)
        self.one = (
            Ring(net, y, lambda i: dev(i, z, c), lambda i: rows(slot_a(c, z, i), 16), lambda i, h: cols(slot_a(c, z, i), h)),
            Ring(net, z, lambda i: dev(y, i, c), lambda i: rows(slot_b(c, y, i), 16), lambda i, h: cols(slot_b(c, y, i), h)),
        )
        self.two = (
            Ring(net, z, lambda i: dev(y, i, c), lambda i: rows(slot_a(c, i, 0), 64), lambda i, h: half(slot_a(c, i, 0), h)),
            Ring(net, y, lambda i: dev(i, z, c), lambda i: rows(slot_b(c, i, 0), 64), lambda i, h: half(slot_b(c, i, 0), h)),
        )
        self.cross = []

    def _cross(self, i):
        for part, slot in ((0, slot_a), (1, slot_b)):
            me = (self.z, self.y)[part]
            x = self.rows(slot(self.c, (me + i) % 4, 0), 64)
            self.cross.append(self.net.copy(x, x, self.other))

    def start(self):
        for r in self.one:
            r.start()

    def forward(self):
        for r in self.one:
            r.forward()

    def second(self):
        for r in self.one:
            r.finish()
        for r in self.two:
            r.start()
        self._cross(0)

    def forward_second(self):
        for r in self.two:
            r.forward()
        self._cross(1)
        self._cross(3)

    def finish(self):
        for r in self.two:
            r.finish()
        self._cross(2)
        for x in self.cross:
            x.wait_recv()


class Scatter:
    def __init__(self, net, me, device, part, rh, rl, rr):
        self.net, self.part, self.rh, self.rl, self.rr = net, part, rh, rl, rr
        self.me, self.right, self.left = me, (me + 1) % 4, (me + 3) % 4
        self.to_right, self.to_left = device(self.right), device(self.left)

    def start(self):
        copy, far = self.net.copy, (self.me + 2) % 4
        self.s0 = copy(self.part(far, 0), self.rh[0], self.to_right)
        self.s1 = copy(self.part(far, 1), self.rh[1], self.to_left)
        self.a0 = copy(self.part(self.right, 1), self.rl(1), self.to_right)
        self.a1 = copy(self.part(self.left, 0), self.rr(0), self.to_left)

    def step(self):
        self.s0.wait_recv()
        p = self.part(self.right, 0)
        p[...] = (p[...].astype(F32) + self.rh[0][...].astype(F32)).astype(BF16)
        self.b0 = self.net.copy(p, self.rl(0), self.to_right)
        self.s1.wait_recv()
        p = self.part(self.left, 1)
        p[...] = (p[...].astype(F32) + self.rh[1][...].astype(F32)).astype(BF16)
        self.b1 = self.net.copy(p, self.rr(1), self.to_left)

    def finish(self):
        for x in (self.a0, self.a1, self.b0, self.b1):
            x.wait_recv()

    def half(self, h):
        return self.part(self.me, h)[...].astype(F32) + (self.rl(h)[...].astype(F32) + self.rr(h)[...].astype(F32))


class WideScatter:
    def __init__(self, net, tile, out, got, own, acc, r1, r2, y, z, c, n):
        self.net, self.tile, self.out, self.got, self.own, self.acc, self.c = net, tile, out, got, own, acc, c

        def dev(y, z, c):
            return (wide_of(y, z, c), n)

        self.other = dev(y, z, 1 - c)

        def rows(ref, start, count):
            return ref.at[pl.ds(aligned(start, 16), count)]

        def first(base, k):
            return dict(
                part=lambda i, h: rows(acc, base + i * 64 + h * 32, 32),
                rh=(r1.at[k, pl.ds(0, 32)], r1.at[k, pl.ds(32, 32)]),
                rl=lambda h: r1.at[k, pl.ds(64 + 32 * h, 32)],
                rr=lambda h: r1.at[k, pl.ds(128 + 32 * h, 32)],
            )

        def cols(ref, start, h):
            return ref.at[pl.ds(aligned(start, 16), 16), pl.ds(h * 1024, 1024)]

        def second(base, me, k):
            return dict(
                part=lambda i, h: cols(acc, base + me * 64 + i * 16, h),
                rh=(cols(r2, k * 48, 0), cols(r2, k * 48, 1)),
                rl=lambda h: cols(r2, k * 48 + 16, h),
                rr=lambda h: cols(r2, k * 48 + 32, h),
            )

        self.one = (
            Scatter(net, z, lambda i: dev(y, i, c), **first(0, 0)),
            Scatter(net, y, lambda i: dev(i, z, c), **first(256, 1)),
        )
        self.two = (
            Scatter(net, y, lambda i: dev(i, z, c), **second(0, z, 0)),
            Scatter(net, z, lambda i: dev(y, i, c), **second(256, y, 1)),
        )

    def exchange(self):
        self.cross = []
        for p in range(2):
            mine = pl.ds(p * 256, 256)
            for i in range(4):
                cs = slice(i * COLS, (i + 1) * COLS)
                self.out[mine, cs] = self.tile(aligned(p * 512 + (1 - self.c) * 256, 256), cs).astype(BF16)
            self.cross.append(self.net.copy(self.out.at[mine], self.got.at[mine], self.other))
        for p in range(2):
            for i in range(4):
                cs = slice(i * COLS, (i + 1) * COLS)
                self.own[p * 256 : p * 256 + 256, cs] = self.tile(aligned(p * 512 + self.c * 256, 256), cs)

    def start(self):
        for p in range(2):
            self.cross[p].wait_recv()

            def add(i, _, p=p):
                r = pl.ds(aligned(p * 256 + i * 64, 64), 64)
                self.acc[r, :] = (self.own[r, :] + self.got[r, :].astype(F32)).astype(BF16)
                return 0

            lax.fori_loop(0, 4, add, 0)
            self.one[p].start()

    def step(self):
        for r in self.one:
            r.step()

    def second(self):
        for r, t in zip(self.one, self.two):
            r.finish()
            for h in range(2):
                r.part(r.me, h)[...] = r.half(h).astype(BF16)
            t.start()

    def second_step(self):
        for r in self.two:
            r.step()

    def finish(self):
        for r in self.two:
            r.finish()

    def result(self, i, cs):
        return self.two[i].half(cs)


def greet(y, z, c, n):
    peers = [
        (wide_of((y + 1) % 4, z, c), n),
        (wide_of((y + 3) % 4, z, c), n),
        (wide_of(y, (z + 1) % 4, c), n),
        (wide_of(y, (z + 3) % 4, c), n),
        (wide_of((y + 2) % 4, z, c), n),
        (wide_of(y, (z + 2) % 4, c), n),
        (wide_of(y, z, 1 - c), n),
        (wide_of(y, z, c), (n + 1) % 4),
        (wide_of(y, z, c), (n + 2) % 4),
        (wide_of(y, z, c), (n + 3) % 4),
    ]
    barrier = pltpu.get_barrier_semaphore()
    for p in peers:
        pl.semaphore_signal(barrier, inc=1, device_id=p, device_id_type=MESH)
    pl.semaphore_wait(barrier, len(peers))


def nt(a, b):
    return lax.dot_general(a, b, (((1,), (1,)), ((), ())), preferred_element_type=F32)


GELU_A = float(np.sqrt(2.0 / np.pi))
GELU_B = 0.044715


def dot(a, b):
    return jnp.dot(a, b, preferred_element_type=F32)


def lanes(shape):
    return lax.broadcasted_iota(jnp.int32, shape, len(shape) - 1)


def swap(x):
    return jnp.where(lanes(x.shape) < ROT // 2, pltpu.roll(x, 128 - ROT // 2, 1), pltpu.roll(x, ROT // 2, 1))


def block_kernel(
    meta, tok, cot, wq, wk, wv, wu, wo, wd, gb, bias, cos_all, sin_all,
    res, ig, grad_l, grad_u, grad_f, small,
    ln, g, w, wm, wmo, xs, gbs, xhat, cosine, sine, pre, slope, hb, dpre, kv, kk, xq, xd, od, dkvt, dkv, dkvp,
    rdkv, sum_f, sum_u, sum_l, r_f, r_u, r_l, out_1, got_1, acc_1, r1_1, r2_1, out_2, got_2, acc_2, r1_2, r2_2, own,
    trans, cmask, bsend, bfin, csend, cfin, ssend, srecv, brecv, yrecv, zrecv, crecv, kpos, send, recv, local,
):
    y, z, c, n = coords()
    net = Net(send, recv)
    my_cols = pl.ds(aligned(n * COLS, COLS), COLS)
    me = wide_of(y, z, c)
    own_a, own_b = slot_a(c, z, y), slot_b(c, y, z)

    def to(m):
        return (me, m)

    def w_cols(i):
        return pl.ds(aligned(i * COLS, COLS), COLS)

    def share(i):
        return pl.ds(aligned(i * PART, PART), PART)

    tables = [
        pltpu.make_async_copy(cos_all.at[n], cosine, local.at[0]),
        pltpu.make_async_copy(sin_all.at[n], sine, local.at[1]),
    ]
    for t in tables:
        t.start()
    w[256:320, my_cols] = wk[...]
    w[320:384, my_cols] = wv[...]
    w[384:448, my_cols] = wq[...]
    w[0:256, my_cols] = wu[...].T
    wm[0:256, my_cols] = wd[...]
    wm[256:320, my_cols] = wo[...]
    gbs[n] = gb[...]
    xs[:, my_cols] = tok[share(n), :]
    row = lax.broadcasted_iota(jnp.int32, (BLOCK, COLS), 0)
    valid = meta[128] + row < meta[129]
    cmask[...] = jnp.where(valid, cot[...], jnp.zeros_like(cot))
    mine = cmask[share(n), :]
    g[pl.ds(own_a, 16), my_cols] = mine[0:16]
    g[pl.ds(own_b, 16), my_cols] = mine[16:32]
    greet(y, z, c, n)

    early, late = [], []
    for j in (1, 3, 2):
        m = (n + j) % 4
        early.append(net.copy(gbs.at[n], gbs.at[n], to(m)))
        early.append(net.copy(tok.at[share(m)], xs.at[:, my_cols], to(m)))
    w_ring = Ring(net, n, to, lambda i: w.at[pl.ds(0, 448), w_cols(i)], lambda i, h: w.at[pl.ds(h * 224, 224), w_cols(i)])
    d_ring = Ring(net, n, to, lambda i: wm.at[pl.ds(0, 256), w_cols(i)], lambda i, h: wm.at[pl.ds(h * 128, 128), w_cols(i)])
    o_ring = Ring(net, n, to, lambda i: wm.at[pl.ds(256, 64), w_cols(i)], lambda i, h: wm.at[pl.ds(256 + h * 32, 32), w_cols(i)])
    kv_ring = Ring(net, n, to, lambda i: kv.at[i], lambda i, h: kv.at[i, pl.ds(h * 512, 512)])
    w_ring.start()
    for j in (1, 3, 2):
        m = (n + j) % 4
        late.append(net.copy(cmask.at[pl.ds(aligned(m * PART, 16), 16)], g.at[pl.ds(own_a, 16), my_cols], to(m)))
        late.append(net.copy(cmask.at[pl.ds(aligned(m * PART + 16, 16), 16)], g.at[pl.ds(own_b, 16), my_cols], to(m)))
    o_ring.start()

    for x in early:
        x.wait_recv()
    x = xs[...].astype(F32)
    mean = jnp.sum(x, 1, keepdims=True) / D
    var = jnp.sum(x * x, 1, keepdims=True) / D - mean * mean
    inv = lax.rsqrt(var + EPS)
    xhat[...] = (x - mean) * inv
    for i in range(4):
        cs = slice(i * COLS, (i + 1) * COLS)
        low = (xhat[:, cs] * gbs[i, 0:1, :] + gbs[i, 1:2, :]).astype(BF16)
        ln[pl.ds(own_a, 16), cs] = low[0:16]
        ln[pl.ds(own_b, 16), cs] = low[16:32]

    lg = WideGather(net, ln, y, z, c, n)
    gg = WideGather(net, g, y, z, c, n)
    lg.start()
    for x in late:
        x.wait_recv()
    for t in tables:
        t.wait()
    for s in range(2):
        at = lanes((8, MAXLEN))
        kpos[s] = jnp.where(at < meta[130 + s], at, 1 << 20)
    wmo[0:64, :] = jnp.zeros((64, D), BF16)
    lg.forward()
    gg.start()
    lg.second()
    gg.forward()
    w_ring.forward()
    o_ring.forward()
    lg.forward_second()
    gg.second()
    w_ring.finish()
    lg.finish()
    gg.forward_second()

    w[448:640, :] = w[256:448, :]
    w[640:656, :] = w[400:416, :]
    w[656:672, :] = w[384:400, :]
    w[672:688, :] = w[272:288, :]
    w[688:704, :] = w[256:272, :]

    def project(i, _):
        r = pl.ds(aligned(i * 256, 256), 256)
        pre[pl.ds(i * 16, 16)] = (nt(ln[r, :], w[448:704, :]) + bias[:, 256:512]).reshape(16, 16, 256)
        return 0

    lax.fori_loop(0, 4, project, 0)

    def arrange(i, _):
        both = pre[meta[i]]
        r = pl.ds(aligned(i * 16, 16), 16)
        tab = pl.ds(aligned((i % 32) * 16, 16), 16)
        a, b = both[:, 0:128], both[:, 128:256]
        cs, sn = cosine[tab, :], sine[tab, :]
        kv[n, r, :] = (a * cs + pltpu.roll(b, 32, 1) * sn).astype(BF16)
        q = (b * cs + pltpu.roll(b, 64, 1) * sn) * (HEAD_DIM**-0.5)
        xq[r, :] = jnp.where(lanes((16, 128)) < HEAD_DIM, q, 0.0).astype(BF16)
        return 0

    lax.fori_loop(0, 64, arrange, 0)
    kv_ring.start()
    d_ring.start()

    def units(i, _):
        r = pl.ds(aligned(i * 256, 256), 256)
        v = nt(ln[r, :], w[0:256, :]) + bias[:, 0:256]
        t = jnp.tanh(GELU_A * (v + GELU_B * (v * v * v)))
        hb[r, :] = (0.5 * v * (1.0 + t)).astype(BF16)
        slope[r, :] = 0.5 * (1.0 + t) + 0.5 * v * (1.0 - t * t) * (GELU_A * (1.0 + 3.0 * GELU_B * (v * v)))
        return 0

    lax.fori_loop(0, 4, units, 0)
    o_ring.finish()
    wmo[64:128, :] = wm[256:320, :]
    gg.finish()

    def grad_o(i, _):
        r = pl.ds(aligned(i * 256, 256), 256)
        pre[pl.ds(i * 16, 16), :, 0:128] = nt(g[r, :], wmo[...]).reshape(16, 16, 128)
        return 0

    lax.fori_loop(0, 4, grad_o, 0)

    def arrange_do(i, _):
        xd[pl.ds(aligned(i * 16, 16), 16), :] = pre[meta[i], :, 0:128].astype(BF16)
        return 0

    lax.fori_loop(0, 64, arrange_do, 0)

    def scatter_cols(buf, count, r):
        half = count // 2
        return Scatter(
            net, n, to,
            lambda i, h: buf.at[pl.ds(h * half, half), w_cols(i)],
            (r.at[0, pl.ds(0, half)], r.at[0, pl.ds(half, half)]),
            lambda h: r.at[1, pl.ds(h * half, half)],
            lambda h: r.at[2, pl.ds(h * half, half)],
        )

    f_sum = scatter_cols(sum_f, 288, r_f)
    u_sum = scatter_cols(sum_u, 256, r_u)
    l_sum = scatter_cols(sum_l, 256, r_l)

    trans[...] = hb[...].T

    def weight_f(i, _):
        cs = pl.ds(aligned(i * COLS, COLS), COLS)
        sum_f[0:256, cs] = dot(trans[...], g[:, cs]).astype(BF16)
        sum_f[256:288, cs] = dot(jnp.ones((32, ROWS), BF16), g[:, cs]).astype(BF16)
        return 0

    lax.fori_loop(0, 4, weight_f, 0)
    f_sum.start()
    kv_ring.forward()
    d_ring.forward()
    kv_ring.finish()

    def gather_keys(i, _):
        for m in range(4):
            kk[pl.ds(aligned(i * BLOCK + m * PART, PART), PART), :] = kv[m, share(i), :]
        return 0

    lax.fori_loop(0, NBLK, gather_keys, 0)

    def attend(s, t):
        keys = 512 * (t + 1)
        r = pl.ds(s * 512 + t * 128, 128)
        x = jnp.concatenate([xq[r, :], xd[r, :]], 0)
        near = kk[pl.ds(s * MAXLEN, keys), :]
        both = nt(x, near)
        i = lax.broadcasted_iota(jnp.int32, (128, 1), 0)
        qpos = (4 * t + i // PART) * BLOCK + n * PART + i % PART
        scores = jnp.where(kpos[s, 0:1, 0:keys] <= qpos, both[0:128], -1e30)
        e = jnp.exp(scores - jnp.max(scores, 1, keepdims=True))
        p = e * (1.0 / jnp.sum(e, 1, keepdims=True))
        dp = both[128:256]
        ds = p * (dp - jnp.sum(p * dp, 1, keepdims=True))
        yy = jnp.concatenate([ds.astype(BF16), p.astype(BF16)], 0)
        back = dot(yy, near)
        od[pl.ds(s * 32 + t * 8, 8)] = jnp.where(lanes((128, 128)) < HEAD_DIM, back[0:128] * (HEAD_DIM**-0.5), back[128:256]).reshape(8, 16, 128)
        grads = dot(x.T, yy)
        if t == 3:
            dkvt[s, :, 0:keys] = grads
        else:
            dkvt[s, :, 0:keys] += grads

    attend(0, 3)
    attend(1, 3)
    f_sum.step()
    attend(0, 2)
    d_ring.finish()

    def grad_units(i, _):
        r = pl.ds(aligned(i * 256, 256), 256)
        dpre[r, 0:256] = (nt(g[r, :], wm[0:256, :]) * slope[r, :]).astype(BF16)
        return 0

    lax.fori_loop(0, 4, grad_units, 0)
    trans[...] = dpre[:, 0:256].T

    def weight_u(i, _):
        cs = pl.ds(aligned(i * COLS, COLS), COLS)
        sum_u[:, cs] = dot(trans[...], ln[:, cs]).astype(BF16)
        return 0

    lax.fori_loop(0, 4, weight_u, 0)
    u_sum.start()
    attend(1, 2)
    attend(0, 1)
    attend(1, 1)
    attend(0, 0)
    attend(1, 0)

    for s in range(2):

        def turn_keys(i, _, s=s):
            t = dkvt[s, :, pl.ds(aligned(i * BLOCK, BLOCK), BLOCK)].T.astype(BF16)
            for m in range(4):
                dkv[m, pl.ds(aligned(s * 512 + i * PART, PART), PART), :] = t[m * PART : (m + 1) * PART]
            return 0

        lax.fori_loop(0, 16, turn_keys, 0)
    kv_sum = Scatter(
        net, n, to,
        lambda i, h: dkv.at[i, pl.ds(h * 512, 512)],
        (rdkv.at[0, pl.ds(0, 512)], rdkv.at[0, pl.ds(512, 512)]),
        lambda h: rdkv.at[1, pl.ds(h * 512, 512)],
        lambda h: rdkv.at[2, pl.ds(h * 512, 512)],
    )
    kv_sum.start()

    def unrope(i, _):
        tab = pl.ds(aligned((i % 32) * 16, 16), 16)
        x = od[i]
        od[i] = x * cosine[tab, :] - swap(x) * sine[tab, :]
        return 0

    lax.fori_loop(0, 64, unrope, 0)

    def place(i, _):
        dpre[pl.ds(aligned(i * 16, 16), 16), 384:512] = od[meta[64 + i]].astype(BF16)
        return 0

    lax.fori_loop(0, 64, place, 0)

    def branch_tile(start, cs):
        r = pl.ds(start, 256)
        return dot(hb[r, :], wm[0:256, cs]) + dot(dpre[r, 384:512], wmo[:, cs])

    branch = WideScatter(net, branch_tile, out_1, got_1, own, acc_1, r1_1, r2_1, y, z, c, n)
    branch.exchange()
    kv_sum.step()
    branch.start()
    u_sum.step()
    f_sum.finish()
    for h in range(2):
        grad_f[h * 144 : (h + 1) * 144, :] = f_sum.half(h)
    kv_sum.finish()

    def unrope_keys(i, _):
        tab = pl.ds(aligned((i % 32) * 16, 16), 16)
        r = pl.ds(aligned(i * 16, 16), 16)
        x = dkv[n, r, :].astype(F32) + (rdkv[1, r, :].astype(F32) + rdkv[2, r, :].astype(F32))
        dkvp[i] = x * cosine[tab, :] - swap(x) * sine[tab, :]
        return 0

    lax.fori_loop(0, 64, unrope_keys, 0)

    def place_keys(i, _):
        dpre[pl.ds(aligned(i * 16, 16), 16), 256:384] = dkvp[meta[64 + i]].astype(BF16)
        return 0

    lax.fori_loop(0, 64, place_keys, 0)

    def dln_tile(start, cs):
        r = pl.ds(start, 256)
        return dot(dpre[r, 0:448], w[0:448, cs])

    dln = WideScatter(net, dln_tile, out_2, got_2, own, acc_2, r1_2, r2_2, y, z, c, n)
    dln.exchange()
    branch.step()
    trans[...] = dpre[:, 256:512].T

    def weight_l(i, _):
        cs = pl.ds(aligned(i * COLS, COLS), COLS)
        sum_l[0:192, cs] = dot(trans[0:192, :], ln[:, cs]).astype(BF16)
        sum_l[192:256, cs] = dot(trans[192:256, :], g[:, cs]).astype(BF16)
        return 0

    lax.fori_loop(0, 4, weight_l, 0)
    dln.start()
    l_sum.start()
    brecv[n] = jnp.broadcast_to(jnp.sum(dpre[...].astype(F32), 0, keepdims=True), (8, COLS))
    late = []
    for j in (1, 3, 2):
        late.append(net.copy(brecv.at[n], brecv.at[n], to((n + j) % 4)))
    branch.second()
    u_sum.finish()
    for h in range(2):
        grad_u[h * 128 : (h + 1) * 128, :] = u_sum.half(h)
    dln.step()
    branch.second_step()
    l_sum.step()
    dln.second()
    branch.finish()
    for i in range(2):
        for h in range(2):
            bsend[i * 16 : (i + 1) * 16, h * 1024 : (h + 1) * 1024] = branch.result(i, h).astype(BF16)
    bfin[share(n), :] = bsend[:, my_cols]
    for j in (1, 3, 2):
        m = (n + j) % 4
        late.append(net.copy(bsend.at[:, w_cols(m)], bfin.at[share(n)], to(m)))
    dln.second_step()
    dln.finish()

    for i in range(2):
        for h in range(2):
            csend[i * 16 : (i + 1) * 16, h * 1024 : (h + 1) * 1024] = dln.result(i, h)
    grad = csend[...]
    ssend[...] = jnp.broadcast_to(jnp.sum(grad, 0, keepdims=True), (8, D))
    ssend[0:1, :] = jnp.sum(grad * xhat[...], 0, keepdims=True)
    for j in range(4):
        cs = slice(j * COLS, (j + 1) * COLS)
        csend[:, cs] = csend[:, cs] * gbs[j, 0:1, :]
    srecv[n] = ssend[:, my_cols]
    last = []
    for j in (1, 3, 2):
        m = (n + j) % 4
        last.append(net.copy(ssend.at[:, w_cols(m)], srecv.at[n], to(m)))
    grad = csend[...]
    first = jnp.sum(grad, 1, keepdims=True) / D
    second = jnp.sum(grad * xhat[...], 1, keepdims=True) / D
    x = xs[...].astype(F32)
    mean = jnp.sum(x, 1, keepdims=True) / D
    var = jnp.sum(x * x, 1, keepdims=True) / D - mean * mean
    csend[...] = lax.rsqrt(var + EPS) * (grad - first - xhat[...] * second)
    cfin[share(n), :] = csend[:, my_cols]
    final = []
    for j in (1, 3, 2):
        m = (n + j) % 4
        final.append(net.copy(csend.at[:, w_cols(m)], cfin.at[share(n)], to(m)))
    for x in last:
        x.wait_recv()
    yrecv[y] = (srecv[0] + srecv[1]) + (srecv[2] + srecv[3])
    last = []
    for j in (1, 3, 2):
        last.append(net.copy(yrecv.at[y], yrecv.at[y], (wide_of((y + j) % 4, z, c), n)))
    l_sum.finish()
    for h in range(2):
        grad_l[h * 128 : (h + 1) * 128, :] = l_sum.half(h)
    for x in late:
        x.wait_recv()
    valid = meta[128] + row < meta[129]
    base = bfin[...].astype(F32) + gb[2:3, :]
    res[...] = (tok[...].astype(F32) + jnp.where(valid, base, 0.0)).astype(BF16)
    for x in last:
        x.wait_recv()
    zrecv[z] = (yrecv[0] + yrecv[1]) + (yrecv[2] + yrecv[3])
    last = []
    for j in (1, 3, 2):
        last.append(net.copy(zrecv.at[z], zrecv.at[z], (wide_of(y, (z + j) % 4, c), n)))
    for x in final:
        x.wait_recv()
    ig[...] = cot[...].astype(F32) + cfin[...]
    for x in last:
        x.wait_recv()
    crecv[c] = (zrecv[0] + zrecv[1]) + (zrecv[2] + zrecv[3])
    x = net.copy(crecv.at[c], crecv.at[c], (wide_of(y, z, 1 - c), n))
    x.wait_recv()
    small[0:8, :] = crecv[0] + crecv[1]
    small[8:16, :] = (brecv[0] + brecv[1]) + (brecv[2] + brecv[3])
    net.drain()


def call_block(*args):
    vmem, anywhere = pl.BlockSpec(memory_space=pltpu.VMEM), pl.BlockSpec(memory_space=pl.ANY)
    shape = jax.ShapeDtypeStruct

    def buf(dtype, *size):
        return pltpu.VMEM(size, dtype)

    wide = [buf(BF16, 512, D), buf(BF16, 512, D), buf(BF16, 512, D), buf(BF16, 2, 192, D), buf(BF16, 96, D)]
    return pl.pallas_call(
        block_kernel,
        out_shape=(
            shape((BLOCK, COLS), BF16),
            shape((BLOCK, COLS), F32),
            shape((256, COLS), F32),
            shape((256, COLS), F32),
            shape((288, COLS), F32),
            shape((16, COLS), F32),
        ),
        in_specs=[pl.BlockSpec(memory_space=pltpu.SMEM)] + [vmem] * 10 + [anywhere] * 2,
        out_specs=(vmem,) * 6,
        scratch_shapes=[
            buf(BF16, ROWS, D),
            buf(BF16, ROWS, D),
            buf(BF16, 704, D),
            buf(BF16, 320, D),
            buf(BF16, 128, D),
            buf(BF16, PART, D),
            buf(F32, 4, 8, COLS),
            buf(F32, PART, D),
            buf(F32, 512, 128),
            buf(F32, 512, 128),
            buf(F32, 64, 16, 256),
            buf(F32, ROWS, UNITS),
            buf(BF16, ROWS, UNITS),
            buf(BF16, ROWS, 512),
            buf(BF16, 4, ROWS, 128),
            buf(BF16, 2 * MAXLEN, 128),
            buf(BF16, ROWS, 128),
            buf(BF16, ROWS, 128),
            buf(F32, 64, 16, 128),
            buf(F32, 2, 128, MAXLEN),
            buf(BF16, 4, ROWS, 128),
            buf(F32, 64, 16, 128),
            buf(BF16, 3, ROWS, 128),
            buf(BF16, 288, D),
            buf(BF16, 256, D),
            buf(BF16, 256, D),
            buf(BF16, 3, 288, COLS),
            buf(BF16, 3, 256, COLS),
            buf(BF16, 3, 256, COLS),
            *wide,
            *wide,
            buf(F32, 512, D),
            buf(BF16, 256, ROWS),
            buf(BF16, BLOCK, COLS),
            buf(BF16, PART, D),
            buf(BF16, BLOCK, COLS),
            buf(F32, PART, D),
            buf(F32, BLOCK, COLS),
            buf(F32, 8, D),
            buf(F32, 4, 8, COLS),
            buf(F32, 4, 8, COLS),
            buf(F32, 4, 8, COLS),
            buf(F32, 4, 8, COLS),
            buf(F32, 2, 8, COLS),
            buf(jnp.int32, 2, 8, MAXLEN),
            pltpu.SemaphoreType.DMA((200,)),
            pltpu.SemaphoreType.DMA((200,)),
            pltpu.SemaphoreType.DMA((2,)),
        ],
        compiler_params=pltpu.CompilerParams(collective_id=0, has_side_effects=True, vmem_limit_bytes=63 * 2**20),
    )(*args)


def split_kernel(res, ig, grad_l, grad_u, grad_f, small, res_o, ig_o, k_o, v_o, q_o, o_o, u_o, f_o, small_o):
    res_o[...] = res[...]
    ig_o[...] = ig[...]
    k_o[...] = grad_l[0:64, :]
    v_o[...] = grad_l[64:128, :]
    q_o[...] = grad_l[128:192, :]
    o_o[...] = grad_l[192:256, :]
    u_o[...] = grad_u[...].T
    f_o[...] = grad_f[0:256, :]
    small_o[0:16, :] = small[...]
    small_o[16:24, :] = grad_f[256:264, :]


def call_split(*args):
    vmem = pl.BlockSpec(memory_space=pltpu.VMEM)
    sizes = [(BLOCK, COLS), (64, COLS), (64, COLS), (64, COLS), (64, COLS), (COLS, UNITS), (UNITS, COLS), (24, COLS)]
    return pl.pallas_call(
        split_kernel,
        out_shape=(jax.ShapeDtypeStruct((BLOCK, COLS), BF16), *(jax.ShapeDtypeStruct(s, F32) for s in sizes)),
        in_specs=[vmem] * 6,
        out_specs=(vmem,) * 9,
        compiler_params=pltpu.CompilerParams(vmem_limit_bytes=32 * 2**20),
    )(*args)


def on_device(
    tokens, ln_gain, ln_bias, w_query, b_query, w_key, b_key, w_value, b_value, w_out, b_out,
    w_fc1, b_fc1, w_fc2, b_fc2, cotangent, lengths, dealing,
):
    wide = lax.axis_index("wide")
    per_seq = MAXLEN // BLOCK
    blocks = jnp.arange(NBLK, dtype=jnp.int32)
    slot_y, slot_z, slot_c = blocks // 8, (blocks // 2) % 4, blocks % 2
    chunk = jnp.stack([(slot_c * 4 + slot_z) * 4 + slot_y, 32 + (slot_c * 4 + slot_y) * 4 + slot_z], 1)
    hit = dealing[None, :] == blocks[:, None]
    there = jnp.sum(jnp.where(hit[:, :, None], chunk[None], 0), 1).reshape(-1)
    logical = jnp.stack([2 * dealing, 2 * dealing + 1], 1).reshape(-1)
    back = jnp.sum(jnp.where(chunk.reshape(-1)[None, :] == jnp.arange(64)[:, None], logical[None, :], 0), 1)
    mine = jnp.sum(jnp.where(blocks == wide, dealing, 0))
    limit = jnp.where(mine // per_seq == 0, lengths[0], lengths[1])
    meta = jnp.concatenate([there, back, jnp.stack([mine % per_seq * BLOCK, limit, lengths[0], lengths[1]])]).astype(jnp.int32)

    half = ROT // 2
    zero = jnp.zeros((5, COLS), F32)
    out_bias = b_out.astype(F32) + b_fc2.astype(F32)
    gb = jnp.concatenate([ln_gain[None], ln_bias[None], out_bias[None], zero], 0)
    bias = jnp.concatenate(
        [
            b_fc1, b_key, b_value, b_query, b_query[half:ROT], b_query[:half], b_key[half:ROT], b_key[:half],
        ]
    ).astype(F32)[None]
    cosine, sine = (
        np.ascontiguousarray(t.reshape(per_seq, 4, PART, 128).transpose(1, 0, 2, 3)).reshape(4, -1, 128)
        for t in rope_tables()
    )
    out = call_block(
        meta, tokens, cotangent, w_query.T, w_key.T, w_value.T, w_fc1, w_out, w_fc2, gb, bias,
        jnp.asarray(cosine), jnp.asarray(sine),
    )
    result, input_grad, key, value, query, proj, up, down, small = call_split(*out)
    sums = small[8]
    return (
        result,
        input_grad,
        small[0],
        small[1],
        query.T,
        sums[384:448],
        key.T,
        sums[256:320],
        value.T,
        sums[320:384],
        proj,
        small[16],
        up,
        sums[0:256],
        down,
        small[16],
    )


def solution(mesh):
    rows, col, units = P("wide", "narrow"), P("narrow"), P("wide")
    weight, out = P("narrow", "wide"), P("wide", "narrow")
    placed = (
        rows, col, col, weight, units, weight, units, weight, units, out, col, weight, units, out, col, rows, P(), P(),
    )
    given = (
        rows, rows, col, col, weight, units, weight, units, weight, units, out, col, weight, units, out, col,
    )
    return jax.shard_map(on_device, mesh=mesh, in_specs=placed, out_specs=given, check_vma=False)
```

```python
import jax
import jax.numpy as jnp
import numpy as np
from jax import lax
from jax.experimental import pallas as pl
from jax.experimental.pallas import tpu as pltpu
from jax.sharding import PartitionSpec as P

MESH = pl.DeviceIdType.MESH
D = 2048
HEAD_DIM = 64
ROT = 32
BLOCK = 128
MAXLEN = 2048
NBLK = 32
PART = 32
ROWS = NBLK * PART
COLS = 512
UNITS = 256
EPS = 1e-05
BF16 = jnp.bfloat16
F32 = jnp.float32


def rope_tables():
    half = ROT // 2
    inverse = (10000.0 ** (-(np.arange(half, dtype=np.float32) * np.float32(2.0) / np.float32(ROT)))).astype(np.float32)
    angles = (np.arange(MAXLEN, dtype=np.float32)[:, None] * inverse[None, :]).astype(np.float64)
    cosine = np.ones((MAXLEN, 128), np.float32)
    sine = np.zeros((MAXLEN, 128), np.float32)
    cosine[:, :half] = np.cos(angles)
    cosine[:, half:ROT] = np.cos(angles)
    sine[:, :half] = -np.sin(angles)
    sine[:, half:ROT] = np.sin(angles)
    return cosine, sine


class Net:
    def __init__(self, send, recv):
        self.send, self.recv, self.used, self.open = send, recv, 0, []

    def copy(self, src, dst, device):
        i = self.used
        self.used += 1
        c = pltpu.make_async_remote_copy(
            src_ref=src,
            dst_ref=dst,
            send_sem=self.send.at[i],
            recv_sem=self.recv.at[i],
            device_id=device,
            device_id_type=MESH,
        )
        c.start()
        self.open.append(c)
        return c

    def drain(self):
        for c in self.open:
            c.wait_send()


class Ring:
    def __init__(self, net, me, device, unit, half):
        self.net, self.unit, self.half = net, unit, half
        self.right, self.left = (me + 1) % 4, (me + 3) % 4
        self.to_right, self.to_left = device(self.right), device(self.left)
        self.me = me

    def start(self):
        own = self.unit(self.me)
        self.a = self.net.copy(own, own, self.to_right)
        self.b = self.net.copy(own, own, self.to_left)

    def forward(self):
        self.a.wait_recv()
        x = self.half(self.left, 0)
        self.c = self.net.copy(x, x, self.to_right)
        self.b.wait_recv()
        x = self.half(self.right, 1)
        self.d = self.net.copy(x, x, self.to_left)

    def finish(self):
        self.c.wait_recv()
        self.d.wait_recv()


def coords():
    w, n = lax.axis_index("wide"), lax.axis_index("narrow")
    return w // 8, (w // 2) % 4, w % 2, n


def wide_of(y, z, c):
    return (y * 4 + z) * 2 + c


def aligned(x, m):
    return pl.multiple_of(x, m)


def slot_a(c, z, y):
    return aligned(((c * 4 + z) * 4 + y) * 16, 16)


def slot_b(c, y, z):
    return aligned((32 + (c * 4 + y) * 4 + z) * 16, 16)


class Gather2:
    def __init__(self, net, one, two, first, second, block, half):
        self.net, self.block, self.half = net, block, half
        self.one, self.two = one, two
        self.first = [first((one + j) % 4) for j in range(4)]
        self.second = [second((two + j) % 4) for j in range(4)]
        self.p, self.q, self.r, self.s = {}, {}, {}, {}

    def at(self, j, k):
        return (self.one + j) % 4, (self.two + k) % 4

    def send(self, j):
        x = self.block(*self.at(j, 0))
        self.p[j] = self.net.copy(x, x, self.second[1])
        self.q[j] = self.net.copy(x, x, self.second[3])

    def start(self):
        x = self.block(*self.at(0, 0))
        self.a = self.net.copy(x, x, self.first[1])
        self.b = self.net.copy(x, x, self.first[3])
        self.send(0)

    def near_one(self):
        self.a.wait_recv()
        x = self.half(*self.at(3, 0), 0)
        self.c = self.net.copy(x, x, self.first[1])
        self.send(3)
        self.b.wait_recv()
        x = self.half(*self.at(1, 0), 1)
        self.d = self.net.copy(x, x, self.first[3])
        self.send(1)

    def far_one(self):
        self.c.wait_recv()
        self.d.wait_recv()
        self.send(2)

    def near_two(self, j):
        self.p[j].wait_recv()
        x = self.half(*self.at(j, 3), 0)
        self.r[j] = self.net.copy(x, x, self.second[1])
        self.q[j].wait_recv()
        x = self.half(*self.at(j, 1), 1)
        self.s[j] = self.net.copy(x, x, self.second[3])

    def far_two(self, j):
        self.r[j].wait_recv()
        self.s[j].wait_recv()


class WideGather:
    def __init__(self, net, buf, y, z, c, n):
        self.net, self.buf, self.c = net, buf, c

        def dev(y, z, c):
            return (wide_of(y, z, c), n)

        def block(start):
            return buf.at[pl.ds(start, 16)]

        def half(start, h):
            return buf.at[pl.ds(start, 16), pl.ds(h * 1024, 1024)]

        self.other = dev(y, z, 1 - c)
        self.slots = (slot_a, slot_b)
        self.parts = (
            Gather2(
                net, y, z, lambda i: dev(i, z, c), lambda i: dev(y, i, c),
                lambda i, k: block(slot_a(c, k, i)), lambda i, k, h: half(slot_a(c, k, i), h),
            ),
            Gather2(
                net, z, y, lambda i: dev(y, i, c), lambda i: dev(i, z, c),
                lambda i, k: block(slot_b(c, k, i)), lambda i, k, h: half(slot_b(c, k, i), h),
            ),
        )
        self.crossed = []

    def cross(self, k):
        for part, slot in zip(self.parts, self.slots):
            x = self.buf.at[pl.ds(slot(self.c, (part.two + k) % 4, 0), 64)]
            self.crossed.append(self.net.copy(x, x, self.other))

    def start(self):
        for x in self.parts:
            x.start()

    def near_one(self):
        for x in self.parts:
            x.near_one()

    def far_one(self):
        for x in self.parts:
            x.far_one()
        self.cross(0)

    def near_two(self, j):
        for x in self.parts:
            x.near_two(j)

    def cross_near(self):
        self.cross(3)
        self.cross(1)

    def far_two(self, j):
        for x in self.parts:
            x.far_two(j)
            b = x.block(*x.at(j, 2))
            self.crossed.append(self.net.copy(b, b, self.other))

    def finish(self):
        for x in self.crossed:
            x.wait_recv()


class Scatter:
    def __init__(self, net, me, device, part, rh, rl, rr):
        self.net, self.part, self.rh, self.rl, self.rr = net, part, rh, rl, rr
        self.me, self.right, self.left = me, (me + 1) % 4, (me + 3) % 4
        self.to_right, self.to_left = device(self.right), device(self.left)

    def start(self):
        self.start_far()
        self.start_right()
        self.start_left()

    def start_far(self):
        far = (self.me + 2) % 4
        self.s0 = self.net.copy(self.part(far, 0), self.rh[0], self.to_right)
        self.s1 = self.net.copy(self.part(far, 1), self.rh[1], self.to_left)

    def start_right(self):
        self.a0 = self.net.copy(self.part(self.right, 1), self.rl(1), self.to_right)

    def start_left(self):
        self.a1 = self.net.copy(self.part(self.left, 0), self.rr(0), self.to_left)

    def step(self):
        self.s0.wait_recv()
        p = self.part(self.right, 0)
        p[...] = (p[...].astype(F32) + self.rh[0][...].astype(F32)).astype(BF16)
        self.b0 = self.net.copy(p, self.rl(0), self.to_right)
        self.s1.wait_recv()
        p = self.part(self.left, 1)
        p[...] = (p[...].astype(F32) + self.rh[1][...].astype(F32)).astype(BF16)
        self.b1 = self.net.copy(p, self.rr(1), self.to_left)

    def finish(self):
        for x in (self.a0, self.a1, self.b0, self.b1):
            x.wait_recv()

    def half(self, h):
        return self.part(self.me, h)[...].astype(F32) + (self.rl(h)[...].astype(F32) + self.rr(h)[...].astype(F32))


class WideScatter:
    def __init__(self, net, tile, out, got, own, acc, r1, r2, y, z, c, n):
        self.net, self.tile, self.out, self.got, self.own, self.acc, self.c = net, tile, out, got, own, acc, c

        def dev(y, z, c):
            return (wide_of(y, z, c), n)

        self.other = dev(y, z, 1 - c)

        def cols(ref, start, h):
            return ref.at[pl.ds(aligned(start, 16), 16), pl.ds(h * 1024, 1024)]

        def ring(me, device, part, ref, base):
            return Scatter(
                net, me, device, part, (cols(ref, base, 0), cols(ref, base, 1)),
                lambda h: cols(ref, base + 16, h), lambda h: cols(ref, base + 32, h),
            )

        def first(base, one, two, device, k):
            return {
                j: ring(two, device, lambda i, h, j=j: cols(acc, base + i * 64 + (one + j) % 4 * 16, h), r1.at[k], j * 48)
                for j in (2, 1, 3, 0)
            }

        def second(base, one, two, device, k):
            return ring(one, device, lambda i, h: cols(acc, base + two * 64 + i * 16, h), r2, k * 48)

        def along_y(i):
            return dev(i, z, c)

        def along_z(i):
            return dev(y, i, c)

        self.one = (first(0, y, z, along_z, 0), first(256, z, y, along_y, 1))
        self.two = (second(0, y, z, along_y, 0), second(256, z, y, along_z, 1))

    def exchange(self):
        self.cross = []
        for p in range(2):
            mine = pl.ds(p * 256, 256)
            for i in range(4):
                cs = slice(i * COLS, (i + 1) * COLS)
                self.out[mine, cs] = self.tile(aligned(p * 512 + (1 - self.c) * 256, 256), cs).astype(BF16)
            self.cross.append(self.net.copy(self.out.at[mine], self.got.at[mine], self.other))
        for p in range(2):
            for i in range(4):
                cs = slice(i * COLS, (i + 1) * COLS)
                self.own[p * 256 : p * 256 + 256, cs] = self.tile(aligned(p * 512 + self.c * 256, 256), cs)

    def start(self):
        for p in range(2):
            self.cross[p].wait_recv()

            def add(i, p=p):
                r = pl.ds(aligned(p * 256 + i * 16, 16), 16)
                self.acc[r, :] = (self.own[r, :] + self.got[r, :].astype(F32)).astype(BF16)

            repeat(16, 4, add)
            for j in (2, 1, 3, 0):
                self.one[p][j].start()

    def step(self, j):
        for x in self.one:
            x[j].step()

    def hand_on(self, j):
        for x, t in zip(self.one, self.two):
            r = x[j]
            r.finish()
            for h in range(2):
                r.part(r.me, h)[...] = r.half(h).astype(BF16)
            if j == 2:
                t.start_far()
            if j == 1:
                t.start_right()
            if j == 3:
                t.start_left()

    def second_step(self):
        for r in self.two:
            r.step()

    def finish(self):
        for r in self.two:
            r.finish()

    def result(self, i, cs):
        return self.two[i].half(cs)


def wide_peers(y, z, c):
    for d in range(1, 32):
        yield wide_of((y + d // 8) % 4, (z + d // 2 % 4) % 4, (c + d % 2) % 2)


def greet(y, z, c, n):
    barrier = pltpu.get_barrier_semaphore()
    for w in wide_peers(y, z, c):
        pl.semaphore_signal(barrier, inc=1, device_id=(w, n), device_id_type=MESH)
    for j in (1, 2, 3):
        pl.semaphore_signal(barrier, inc=1, device_id=(wide_of(y, z, c), (n + j) % 4), device_id_type=MESH)
    pl.semaphore_wait(barrier, 34)


def repeat(count, step, body):
    def turn(i, _):
        for j in range(step):
            body(i * step + j)
        return 0

    lax.fori_loop(0, count // step, turn, 0)


def nt(a, b):
    return lax.dot_general(a, b, (((1,), (1,)), ((), ())), preferred_element_type=F32)


GELU_A = float(np.sqrt(2.0 / np.pi))
GELU_B = 0.044715


def dot(a, b):
    return jnp.dot(a, b, preferred_element_type=F32)


def lanes(shape):
    return lax.broadcasted_iota(jnp.int32, shape, len(shape) - 1)


def swap(x):
    return jnp.where(lanes(x.shape) < ROT // 2, pltpu.roll(x, 128 - ROT // 2, 1), pltpu.roll(x, ROT // 2, 1))


def block_kernel(
    dealing, lengths, tok, cot, wq, wk, wv, wu, wo, wd, v_gain, v_bias, b_q, b_k, b_v, b_o, b_u, b_d, cos_all, sin_all,
    res, ig, grad_l, grad_u, grad_f, small, norm,
    ln, g, w, wm, wmo, xs, gbs, xhat, cosine, sine, pre, slope, hb, dpre, kv, kk, xq, xd, od, dkvt, dkv, dkvp,
    rdkv, sum_f, sum_u, sum_l, r_f, r_u, r_l, out_1, got_1, acc_1, r1_1, r2_1, out_2, got_2, acc_2, r1_2, r2_2, own,
    trans, cmask, bsend, bfin, csend, cfin, ssend, srecv, brecv, wrecv, bias, index, there, kpos, send, recv, local,
):
    y, z, c, n = coords()
    net = Net(send, recv)
    my_cols = pl.ds(aligned(n * COLS, COLS), COLS)
    me = wide_of(y, z, c)
    own_a, own_b = slot_a(c, z, y), slot_b(c, y, z)

    def to(m):
        return (me, m)

    def w_cols(i):
        return pl.ds(aligned(i * COLS, COLS), COLS)

    def share(i):
        return pl.ds(aligned(i * PART, PART), PART)

    tables = [
        pltpu.make_async_copy(cos_all.at[n], cosine, local.at[0]),
        pltpu.make_async_copy(sin_all.at[n], sine, local.at[1]),
    ]
    for t in tables:
        t.start()
    w[256:320, my_cols] = wk[...]
    w[320:384, my_cols] = wv[...]
    w[384:448, my_cols] = wq[...]
    w[0:256, my_cols] = wu[...].T
    wm[0:256, my_cols] = wd[...]
    wm[256:320, my_cols] = wo[...]
    gbs[n, 0:1, :] = v_gain[...]
    gbs[n, 1:2, :] = v_bias[...]
    xs[:, my_cols] = tok[share(n), :]
    row = lax.broadcasted_iota(jnp.int32, (BLOCK, COLS), 0)
    block = dealing[me]
    valid = block % (MAXLEN // BLOCK) * BLOCK + row < jnp.where(block < MAXLEN // BLOCK, lengths[0], lengths[1])
    cmask[...] = jnp.where(valid, cot[...], jnp.zeros_like(cot))
    mine = cmask[share(n), :]
    g[pl.ds(own_a, 16), my_cols] = mine[0:16]
    g[pl.ds(own_b, 16), my_cols] = mine[16:32]
    greet(y, z, c, n)

    early, late = [], []
    for j in (1, 3, 2):
        m = (n + j) % 4
        early.append(net.copy(gbs.at[n], gbs.at[n], to(m)))
        early.append(net.copy(tok.at[share(m)], xs.at[:, my_cols], to(m)))
    for j in (1, 3, 2):
        m = (n + j) % 4
        late.append(net.copy(cmask.at[pl.ds(aligned(m * PART, 16), 16)], g.at[pl.ds(own_a, 16), my_cols], to(m)))
        late.append(net.copy(cmask.at[pl.ds(aligned(m * PART + 16, 16), 16)], g.at[pl.ds(own_b, 16), my_cols], to(m)))
    a_ring = Ring(net, n, to, lambda i: w.at[pl.ds(256, 192), w_cols(i)], lambda i, h: w.at[pl.ds(256 + h * 96, 96), w_cols(i)])
    u_ring = Ring(net, n, to, lambda i: w.at[pl.ds(0, 256), w_cols(i)], lambda i, h: w.at[pl.ds(h * 128, 128), w_cols(i)])
    d_ring = Ring(net, n, to, lambda i: wm.at[pl.ds(0, 256), w_cols(i)], lambda i, h: wm.at[pl.ds(h * 128, 128), w_cols(i)])
    o_ring = Ring(net, n, to, lambda i: wm.at[pl.ds(256, 64), w_cols(i)], lambda i, h: wm.at[pl.ds(256 + h * 32, 32), w_cols(i)])
    kv_ring = [
        Ring(
            net, n, to,
            lambda i, s=s: kv.at[i, pl.ds(s * 512, 512)],
            lambda i, h, s=s: kv.at[i, pl.ds(s * 512 + h * 256, 256)],
        )
        for s in range(2)
    ]
    a_ring.start()
    u_ring.start()
    o_ring.start()

    at = lanes((8, 128))
    part = lax.broadcasted_iota(jnp.int32, (8, 128), 0)
    found = jnp.zeros((8, 128), jnp.int32)
    for b in range(NBLK):
        sy, sz, sc = b // 8, b // 2 % 4, b % 2
        found = jnp.where((part < 2) & (at == dealing[b]), jnp.where(part == 0, (sc * 4 + sz) * 4 + sy, 32 + (sc * 4 + sy) * 4 + sz), found)
        found = jnp.where((part == 2) & (at == (sc * 4 + sz) * 4 + sy), 2 * dealing[b], found)
        found = jnp.where((part == 2) & (at == 32 + (sc * 4 + sy) * 4 + sz), 2 * dealing[b] + 1, found)
    index[...] = found
    to_scalars = pltpu.make_async_copy(index, there, local.at[2])
    to_scalars.start()
    half = ROT // 2
    bias[:, 0:256] = b_u[...].astype(F32)
    bias[:, 256:320] = b_k[...].astype(F32)
    bias[:, 320:384] = b_v[...].astype(F32)
    bias[:, 384:448] = b_q[...].astype(F32)
    bias[:, 448:464] = b_q[:, half:ROT].astype(F32)
    bias[:, 464:480] = b_q[:, 0:half].astype(F32)
    bias[:, 480:496] = b_k[:, half:ROT].astype(F32)
    bias[:, 496:512] = b_k[:, 0:half].astype(F32)
    for s in range(2):
        at = lanes((8, MAXLEN))
        kpos[s] = jnp.where(at < lengths[s], at, 1 << 20)
    wmo[0:64, :] = jnp.zeros((64, D), BF16)

    for x in early:
        x.wait_recv()
    x = xs[...].astype(F32)
    mean = jnp.sum(x, 1, keepdims=True) / D
    var = jnp.sum(x * x, 1, keepdims=True) / D - mean * mean
    inv = lax.rsqrt(var + EPS)
    xhat[...] = (x - mean) * inv
    for i in range(4):
        cs = slice(i * COLS, (i + 1) * COLS)
        low = (xhat[:, cs] * gbs[i, 0:1, :] + gbs[i, 1:2, :]).astype(BF16)
        ln[pl.ds(own_a, 16), cs] = low[0:16]
        ln[pl.ds(own_b, 16), cs] = low[16:32]

    lg = WideGather(net, ln, y, z, c, n)
    gg = WideGather(net, g, y, z, c, n)
    lg.start()
    for t in tables:
        t.wait()
    to_scalars.wait()
    lg.near_one()
    a_ring.forward()
    lg.near_two(0)
    lg.far_one()
    lg.near_two(3)
    lg.near_two(1)
    for x in late:
        x.wait_recv()
    u_ring.forward()
    o_ring.forward()
    lg.near_two(2)
    lg.cross_near()
    gg.start()
    for j in (0, 3, 1, 2):
        lg.far_two(j)
    d_ring.start()
    a_ring.finish()
    gg.near_one()

    w[448:640, :] = w[256:448, :]
    w[640:656, :] = w[400:416, :]
    w[656:672, :] = w[384:400, :]
    w[672:688, :] = w[272:288, :]
    w[688:704, :] = w[256:272, :]

    gg.near_two(0)
    gg.far_one()
    lg.finish()

    def project(i, _):
        r = pl.ds(aligned(i * 256, 256), 256)
        pre[pl.ds(i * 16, 16)] = (nt(ln[r, :], w[448:704, :]) + bias[:, 256:512]).reshape(16, 16, 256)
        return 0

    lax.fori_loop(0, 4, project, 0)

    def arrange(i):
        both = pre[there[i % 2, i // 2]]
        r = pl.ds(aligned(i * 16, 16), 16)
        tab = pl.ds(aligned((i % 32) * 16, 16), 16)
        a, b = both[:, 0:128], both[:, 128:256]
        cs, sn = cosine[tab, :], sine[tab, :]
        kv[n, r, :] = (a * cs + pltpu.roll(b, 32, 1) * sn).astype(BF16)
        q = (b * cs + pltpu.roll(b, 64, 1) * sn) * (HEAD_DIM**-0.5)
        xq[r, :] = jnp.where(lanes((16, 128)) < HEAD_DIM, q, 0.0).astype(BF16)

    repeat(32, 8, arrange)
    kv_ring[0].start()
    gg.near_two(3)
    gg.near_two(1)
    repeat(32, 8, lambda i: arrange(i + 32))
    kv_ring[1].start()
    gg.near_two(2)
    gg.cross_near()
    u_ring.finish()

    def units(i, _):
        r = pl.ds(aligned(i * 256, 256), 256)
        v = nt(ln[r, :], w[0:256, :]) + bias[:, 0:256]
        t = jnp.tanh(GELU_A * (v + GELU_B * (v * v * v)))
        hb[r, :] = (0.5 * v * (1.0 + t)).astype(BF16)
        slope[r, :] = 0.5 * (1.0 + t) + 0.5 * v * (1.0 - t * t) * (GELU_A * (1.0 + 3.0 * GELU_B * (v * v)))
        return 0

    lax.fori_loop(0, 4, units, 0)
    kv_ring[0].forward()
    for j in (0, 3, 1, 2):
        gg.far_two(j)
    d_ring.forward()
    o_ring.finish()
    wmo[64:128, :] = wm[256:320, :]
    gg.finish()

    def grad_o(i, _):
        r = pl.ds(aligned(i * 256, 256), 256)
        pre[pl.ds(i * 16, 16), :, 0:128] = nt(g[r, :], wmo[...]).reshape(16, 16, 128)
        return 0

    lax.fori_loop(0, 4, grad_o, 0)

    def arrange_do(i):
        xd[pl.ds(aligned(i * 16, 16), 16), :] = pre[there[i % 2, i // 2], :, 0:128].astype(BF16)

    repeat(64, 8, arrange_do)
    kv_ring[1].forward()

    def scatter_cols(buf, count, r):
        half = count // 2
        return Scatter(
            net, n, to,
            lambda i, h: buf.at[pl.ds(h * half, half), w_cols(i)],
            (r.at[0, pl.ds(0, half)], r.at[0, pl.ds(half, half)]),
            lambda h: r.at[1, pl.ds(h * half, half)],
            lambda h: r.at[2, pl.ds(h * half, half)],
        )

    f_sum = scatter_cols(sum_f, 288, r_f)
    u_sum = scatter_cols(sum_u, 256, r_u)
    l_sum = scatter_cols(sum_l, 256, r_l)

    def gather_keys(i):
        for m in range(4):
            kk[pl.ds(aligned(i * BLOCK + m * PART, PART), PART), :] = kv[m, share(i), :]

    def attend(s, t):
        keys = 512 * (t + 1)
        r = pl.ds(s * 512 + t * 128, 128)
        x = jnp.concatenate([xq[r, :], xd[r, :]], 0)
        near = kk[pl.ds(s * MAXLEN, keys), :]
        both = nt(x, near)
        i = lax.broadcasted_iota(jnp.int32, (128, 1), 0)
        qpos = (4 * t + i // PART) * BLOCK + n * PART + i % PART
        scores = jnp.where(kpos[s, 0:1, 0:keys] <= qpos, both[0:128], -1e30)
        e = jnp.exp(scores - jnp.max(scores, 1, keepdims=True))
        p = e * (1.0 / jnp.sum(e, 1, keepdims=True))
        dp = both[128:256]
        ds = p * (dp - jnp.sum(p * dp, 1, keepdims=True))
        yy = jnp.concatenate([ds.astype(BF16), p.astype(BF16)], 0)
        back = dot(yy, near)
        back = jnp.where(lanes((128, 128)) < HEAD_DIM, back[0:128] * (HEAD_DIM**-0.5), back[128:256])
        od[pl.ds(s * 32 + t * 8, 8)] = back.reshape(8, 16, 128)
        grads = dot(x.T, yy)
        if t == 3:
            dkvt[s, :, 0:keys] = grads
        else:
            dkvt[s, :, 0:keys] += grads

    def key_sum(s):
        return Scatter(
            net, n, to,
            lambda i, h: dkv.at[i, pl.ds(s * 512 + h * 256, 256)],
            (rdkv.at[0, pl.ds(s * 512, 256)], rdkv.at[0, pl.ds(s * 512 + 256, 256)]),
            lambda h: rdkv.at[1, pl.ds(s * 512 + h * 256, 256)],
            lambda h: rdkv.at[2, pl.ds(s * 512 + h * 256, 256)],
        )

    def weight_f(i, _):
        cs = pl.ds(aligned(i * COLS, COLS), COLS)
        sum_f[0:256, cs] = dot(trans[...], g[:, cs]).astype(BF16)
        sum_f[256:288, cs] = dot(jnp.ones((32, ROWS), BF16), g[:, cs]).astype(BF16)
        return 0

    kv_sum = [key_sum(0), key_sum(1)]
    for s in range(2):
        kv_ring[s].finish()
        repeat(16, 4, lambda i, s=s: gather_keys(i + 16 * s))
        for t in (3, 2, 1, 0):
            attend(s, t)

        def turn_keys(i, s=s):
            t = dkvt[s, :, pl.ds(aligned(i * BLOCK, BLOCK), BLOCK)].T.astype(BF16)
            for m in range(4):
                dkv[m, pl.ds(aligned(s * 512 + i * PART, PART), PART), :] = t[m * PART : (m + 1) * PART]

        repeat(16, 4, turn_keys)
        kv_sum[s].start()
        if s == 0:
            trans[...] = hb[...].T
            lax.fori_loop(0, 4, weight_f, 0)
            f_sum.start()
            d_ring.finish()

    def grad_units(i, _):
        r = pl.ds(aligned(i * 256, 256), 256)
        dpre[r, 0:256] = (nt(g[r, :], wm[0:256, :]) * slope[r, :]).astype(BF16)
        return 0

    lax.fori_loop(0, 4, grad_units, 0)
    kv_sum[0].step()

    def unrope(i):
        tab = pl.ds(aligned((i % 32) * 16, 16), 16)
        x = od[i]
        od[i] = x * cosine[tab, :] - swap(x) * sine[tab, :]

    repeat(64, 8, unrope)

    def place(i):
        dpre[pl.ds(aligned(i * 16, 16), 16), 384:512] = od[there[2, i]].astype(BF16)

    repeat(64, 8, place)
    kv_sum[1].step()

    def branch_tile(start, cs):
        r = pl.ds(start, 256)
        return dot(hb[r, :], wm[0:256, cs]) + dot(dpre[r, 384:512], wmo[:, cs])

    branch = WideScatter(net, branch_tile, out_1, got_1, own, acc_1, r1_1, r2_1, y, z, c, n)
    branch.exchange()
    branch.start()
    trans[...] = dpre[:, 0:256].T

    def weight_u(i, _):
        cs = pl.ds(aligned(i * COLS, COLS), COLS)
        sum_u[:, cs] = dot(trans[...], ln[:, cs]).astype(BF16)
        return 0

    lax.fori_loop(0, 4, weight_u, 0)
    u_sum.start()
    def unrope_keys(i):
        tab = pl.ds(aligned((i % 32) * 16, 16), 16)
        r = pl.ds(aligned(i * 16, 16), 16)
        x = dkv[n, r, :].astype(F32) + (rdkv[1, r, :].astype(F32) + rdkv[2, r, :].astype(F32))
        dkvp[i] = x * cosine[tab, :] - swap(x) * sine[tab, :]

    for s in range(2):
        kv_sum[s].finish()
        repeat(32, 8, lambda i, s=s: unrope_keys(i + 32 * s))

    def place_keys(i):
        dpre[pl.ds(aligned(i * 16, 16), 16), 256:384] = dkvp[there[2, i]].astype(BF16)

    repeat(64, 8, place_keys)

    def dln_tile(start, cs):
        r = pl.ds(start, 256)
        return dot(dpre[r, 0:448], w[0:448, cs])

    dln = WideScatter(net, dln_tile, out_2, got_2, own, acc_2, r1_2, r2_2, y, z, c, n)
    dln.exchange()
    for j in (2, 1, 3, 0):
        branch.step(j)
    dln.start()
    f_sum.step()
    u_sum.step()
    for j in (2, 1, 3, 0):
        branch.hand_on(j)
    trans[...] = dpre[:, 256:512].T

    def weight_l(i, _):
        cs = pl.ds(aligned(i * COLS, COLS), COLS)
        sum_l[0:192, cs] = dot(trans[0:192, :], ln[:, cs]).astype(BF16)
        sum_l[192:256, cs] = dot(trans[192:256, :], g[:, cs]).astype(BF16)
        return 0

    lax.fori_loop(0, 4, weight_l, 0)
    l_sum.start()
    for j in (2, 1, 3, 0):
        dln.step(j)
    branch.second_step()
    for j in (2, 1, 3, 0):
        dln.hand_on(j)
    brecv[n] = jnp.broadcast_to(jnp.sum(dpre[...].astype(F32), 0, keepdims=True), (8, COLS))
    late = []
    for j in (1, 3, 2):
        late.append(net.copy(brecv.at[n], brecv.at[n], to((n + j) % 4)))
    dln.second_step()
    branch.finish()
    for i in range(2):
        for h in range(2):
            bsend[i * 16 : (i + 1) * 16, h * 1024 : (h + 1) * 1024] = branch.result(i, h).astype(BF16)
    bfin[share(n), :] = bsend[:, my_cols]
    for j in (1, 3, 2):
        m = (n + j) % 4
        late.append(net.copy(bsend.at[:, w_cols(m)], bfin.at[share(n)], to(m)))
    l_sum.step()
    dln.finish()

    for i in range(2):
        for h in range(2):
            csend[i * 16 : (i + 1) * 16, h * 1024 : (h + 1) * 1024] = dln.result(i, h)
    grad = csend[...]
    sums = (jnp.sum(grad * xhat[...], 0, keepdims=True), jnp.sum(grad, 0, keepdims=True))
    for m in range(4):
        for k in range(2):
            for i in range(4):
                ssend[m, 4 * k + i : 4 * k + i + 1, :] = sums[k][:, m * COLS + i * 128 : m * COLS + i * 128 + 128]
    srecv[n] = ssend[n]
    last = []
    for j in (1, 3, 2):
        m = (n + j) % 4
        last.append(net.copy(ssend.at[m], srecv.at[n], to(m)))
    for j in range(4):
        cs = slice(j * COLS, (j + 1) * COLS)
        csend[:, cs] = csend[:, cs] * gbs[j, 0:1, :]
    grad = csend[...]
    first = jnp.sum(grad, 1, keepdims=True) / D
    second = jnp.sum(grad * xhat[...], 1, keepdims=True) / D
    x = xs[...].astype(F32)
    mean = jnp.sum(x, 1, keepdims=True) / D
    var = jnp.sum(x * x, 1, keepdims=True) / D - mean * mean
    csend[...] = lax.rsqrt(var + EPS) * (grad - first - xhat[...] * second)
    cfin[share(n), :] = csend[:, my_cols]
    final = []
    for j in (1, 3, 2):
        m = (n + j) % 4
        final.append(net.copy(csend.at[:, w_cols(m)], cfin.at[share(n)], to(m)))
    for x in last:
        x.wait_recv()
    wrecv[me] = (srecv[0] + srecv[1]) + (srecv[2] + srecv[3])
    last = [net.copy(wrecv.at[me], wrecv.at[me], (p, n)) for p in wide_peers(y, z, c)]
    f_sum.finish()
    for h in range(2):
        grad_f[h * 144 : (h + 1) * 144, :] = f_sum.half(h)
    u_sum.finish()
    for h in range(2):
        grad_u[h * 128 : (h + 1) * 128, :] = u_sum.half(h)
    l_sum.finish()
    for h in range(2):
        grad_l[h * 128 : (h + 1) * 128, :] = l_sum.half(h)
    for x in late:
        x.wait_recv()
    block = dealing[me]
    valid = block % (MAXLEN // BLOCK) * BLOCK + row < jnp.where(block < MAXLEN // BLOCK, lengths[0], lengths[1])
    base = bfin[...].astype(F32) + (b_o[...].astype(F32) + b_d[...].astype(F32))
    res[...] = (tok[...].astype(F32) + jnp.where(valid, base, 0.0)).astype(BF16)
    small[...] = (brecv[0] + brecv[1]) + (brecv[2] + brecv[3])
    for x in final:
        x.wait_recv()
    ig[...] = cot[...].astype(F32) + cfin[...]
    for x in last:
        x.wait_recv()
    norm[...] = jnp.sum(wrecv[...], 0)
    net.drain()


def call_block(*args):
    vmem, anywhere = pl.BlockSpec(memory_space=pltpu.VMEM), pl.BlockSpec(memory_space=pl.ANY)
    shape = jax.ShapeDtypeStruct

    def buf(dtype, *size):
        return pltpu.VMEM(size, dtype)

    wide = [buf(BF16, 512, D), buf(BF16, 512, D), buf(BF16, 512, D), buf(BF16, 2, 192, D), buf(BF16, 96, D)]
    return pl.pallas_call(
        block_kernel,
        out_shape=(
            shape((BLOCK, COLS), BF16),
            shape((BLOCK, COLS), F32),
            shape((256, COLS), F32),
            shape((256, COLS), F32),
            shape((288, COLS), F32),
            shape((8, COLS), F32),
            shape((8, 128), F32),
        ),
        in_specs=[pl.BlockSpec(memory_space=pltpu.SMEM)] * 2 + [vmem] * 16 + [anywhere] * 2,
        out_specs=(vmem,) * 7,
        scratch_shapes=[
            buf(BF16, ROWS, D),
            buf(BF16, ROWS, D),
            buf(BF16, 704, D),
            buf(BF16, 320, D),
            buf(BF16, 128, D),
            buf(BF16, PART, D),
            buf(F32, 4, 8, COLS),
            buf(F32, PART, D),
            buf(F32, 512, 128),
            buf(F32, 512, 128),
            buf(F32, 64, 16, 256),
            buf(F32, ROWS, UNITS),
            buf(BF16, ROWS, UNITS),
            buf(BF16, ROWS, 512),
            buf(BF16, 4, ROWS, 128),
            buf(BF16, 2 * MAXLEN, 128),
            buf(BF16, ROWS, 128),
            buf(BF16, ROWS, 128),
            buf(F32, 64, 16, 128),
            buf(F32, 2, 128, MAXLEN),
            buf(BF16, 4, ROWS, 128),
            buf(F32, 64, 16, 128),
            buf(BF16, 3, ROWS, 128),
            buf(BF16, 288, D),
            buf(BF16, 256, D),
            buf(BF16, 256, D),
            buf(BF16, 3, 288, COLS),
            buf(BF16, 3, 256, COLS),
            buf(BF16, 3, 256, COLS),
            *wide,
            *wide,
            buf(F32, 512, D),
            buf(BF16, 256, ROWS),
            buf(BF16, BLOCK, COLS),
            buf(BF16, PART, D),
            buf(BF16, BLOCK, COLS),
            buf(F32, PART, D),
            buf(F32, BLOCK, COLS),
            buf(F32, 4, 8, 128),
            buf(F32, 4, 8, 128),
            buf(F32, 4, 8, COLS),
            buf(F32, 32, 8, 128),
            buf(F32, 1, COLS),
            buf(jnp.int32, 8, 128),
            pltpu.SMEM((8, 128), jnp.int32),
            buf(jnp.int32, 2, 8, MAXLEN),
            pltpu.SemaphoreType.DMA((400,)),
            pltpu.SemaphoreType.DMA((400,)),
            pltpu.SemaphoreType.DMA((3,)),
        ],
        compiler_params=pltpu.CompilerParams(collective_id=0, has_side_effects=True, vmem_limit_bytes=63 * 2**20),
    )(*args)


def split_kernel(
    res, ig, grad_l, grad_u, grad_f, small, norm,
    res_o, ig_o, gain_o, bias_o, q_o, bq_o, k_o, bk_o, v_o, bv_o, o_o, bo_o, u_o, bu_o, f_o, bf_o,
):
    res_o[...] = res[...]
    ig_o[...] = ig[...]
    k_o[...] = grad_l[0:64, :]
    v_o[...] = grad_l[64:128, :]
    q_o[...] = grad_l[128:192, :]
    o_o[...] = grad_l[192:256, :]
    u_o[...] = grad_u[...].T
    f_o[...] = grad_f[0:256, :]
    for i in range(4):
        gain_o[:, i * 128 : i * 128 + 128] = norm[i : i + 1, :]
        bias_o[:, i * 128 : i * 128 + 128] = norm[4 + i : 5 + i, :]
    bu_o[...] = small[0:1, 0:256]
    bk_o[...] = small[0:1, 256:320]
    bv_o[...] = small[0:1, 320:384]
    bq_o[...] = small[0:1, 384:448]
    bo_o[...] = grad_f[256:257, :]
    bf_o[...] = grad_f[256:257, :]


def call_split(*args):
    vmem = pl.BlockSpec(memory_space=pltpu.VMEM)
    head, vector = (64, COLS), (1, COLS)
    sizes = [
        (BLOCK, COLS), vector, vector, head, (1, 64), head, (1, 64), head, (1, 64), head, vector,
        (COLS, UNITS), (1, UNITS), (UNITS, COLS), vector,
    ]
    return pl.pallas_call(
        split_kernel,
        out_shape=(jax.ShapeDtypeStruct((BLOCK, COLS), BF16), *(jax.ShapeDtypeStruct(s, F32) for s in sizes)),
        in_specs=[vmem] * 7,
        out_specs=(vmem,) * 16,
        compiler_params=pltpu.CompilerParams(vmem_limit_bytes=62 * 2**20),
    )(*args)


def on_device(
    tokens, ln_gain, ln_bias, w_query, b_query, w_key, b_key, w_value, b_value, w_out, b_out,
    w_fc1, b_fc1, w_fc2, b_fc2, cotangent, lengths, dealing,
):
    cosine, sine = (
        np.ascontiguousarray(t.reshape(MAXLEN // BLOCK, 4, PART, 128).transpose(1, 0, 2, 3)).reshape(4, -1, 128)
        for t in rope_tables()
    )
    out = call_block(
        dealing, lengths, tokens, cotangent, w_query.T, w_key.T, w_value.T, w_fc1, w_out, w_fc2,
        ln_gain[None], ln_bias[None], b_query[None], b_key[None], b_value[None], b_out[None], b_fc1[None], b_fc2[None],
        jnp.asarray(cosine), jnp.asarray(sine),
    )
    out = list(call_split(*out))
    for i in (4, 6, 8):
        out[i] = out[i].T
    for i in (2, 3, 5, 7, 9, 11, 13, 15):
        out[i] = out[i][0]
    return tuple(out)


def solution(mesh):
    rows, col, units = P("wide", "narrow"), P("narrow"), P("wide")
    weight, out = P("narrow", "wide"), P("wide", "narrow")
    placed = (
        rows, col, col, weight, units, weight, units, weight, units, out, col, weight, units, out, col, rows, P(), P(),
    )
    given = (
        rows, rows, col, col, weight, units, weight, units, weight, units, out, col, weight, units, out, col,
    )
    return jax.shard_map(on_device, mesh=mesh, in_specs=placed, out_specs=given, check_vma=False)
```

```python
import jax
import jax.numpy as jnp
import numpy as np
from jax import lax
from jax.experimental import pallas as pl
from jax.experimental.pallas import tpu as pltpu
from jax.sharding import PartitionSpec as P

MESH = pl.DeviceIdType.MESH
D = 2048
HEAD_DIM = 64
ROT = 32
BLOCK = 128
MAXLEN = 2048
NBLK = 32
PART = 32
ROWS = NBLK * PART
COLS = 512
UNITS = 256
EPS = 1e-05
SENDS, ARRIVALS = 16, 142
BF16 = jnp.bfloat16
F32 = jnp.float32


def rope_tables():
    half = ROT // 2
    inverse = (10000.0 ** (-(np.arange(half, dtype=np.float32) * np.float32(2.0) / np.float32(ROT)))).astype(np.float32)
    angles = (np.arange(MAXLEN, dtype=np.float32)[:, None] * inverse[None, :]).astype(np.float64)
    cosine = np.ones((MAXLEN, 128), np.float32)
    sine = np.zeros((MAXLEN, 128), np.float32)
    cosine[:, :half] = np.cos(angles)
    cosine[:, half:ROT] = np.cos(angles)
    sine[:, :half] = -np.sin(angles)
    sine[:, half:ROT] = np.sin(angles)
    return cosine, sine


class Net:
    def __init__(self, send, recv, anyone):
        self.send, self.recv, self.anyone = send, recv, anyone
        self.groups = self.slots = 0

    def group(self):
        self.groups += 1
        return self.groups - 1

    def slot(self):
        self.slots += 1
        return self.slots - 1

    def make(self, src, dst, device, group, slot):
        return pltpu.make_async_remote_copy(
            src_ref=src,
            dst_ref=dst,
            send_sem=self.send.at[group],
            recv_sem=self.recv.at[slot],
            device_id=device,
            device_id_type=MESH,
        )

    def copy(self, src, dst, device, group, slot):
        self.make(src, dst, device, group, slot).start()

    def arrived(self, ref, slot):
        self.make(ref, ref, self.anyone, 0, slot).wait_recv()

    def sent(self, ref, group):
        self.make(ref, ref, self.anyone, group, 0).wait_send()


class Ring:
    def __init__(self, net, group, me, device, unit, half):
        self.net, self.group, self.unit, self.half = net, group, unit, half
        self.me, self.right, self.left = me, (me + 1) % 4, (me + 3) % 4
        self.to_right, self.to_left = device(self.right), device(self.left)
        self.a, self.b, self.c = net.slot(), net.slot(), net.slot()

    def send(self, x, device, slot):
        self.net.copy(x, x, device, self.group, slot)

    def start(self):
        own = self.unit(self.me)
        self.send(own, self.to_right, self.a)
        self.send(own, self.to_left, self.b)

    def forward(self):
        self.net.arrived(self.unit(self.left), self.a)
        self.send(self.half(self.left, 0), self.to_right, self.c)
        self.net.arrived(self.unit(self.right), self.b)
        self.send(self.half(self.right, 1), self.to_left, self.c)

    def finish(self):
        self.net.arrived(self.unit((self.me + 2) % 4), self.c)


def coords():
    w, n = lax.axis_index("wide"), lax.axis_index("narrow")
    return w // 8, (w // 2) % 4, w % 2, n


def wide_of(y, z, c):
    return (y * 4 + z) * 2 + c


def aligned(x, m):
    return pl.multiple_of(x, m)


def slot_a(c, z, y):
    return aligned(((c * 4 + z) * 4 + y) * 16, 16)


def slot_b(c, y, z):
    return aligned((32 + (c * 4 + y) * 4 + z) * 16, 16)


class Gather2:
    def __init__(self, net, group, one, two, first, second, block, half):
        self.net, self.group, self.block, self.half = net, group, block, half
        self.one, self.two = one, two
        self.first = [first((one + j) % 4) for j in range(4)]
        self.second = [second((two + j) % 4) for j in range(4)]
        self.a, self.b, self.c = net.slot(), net.slot(), net.slot()
        self.p, self.q, self.r = ([net.slot() for _ in range(4)] for _ in range(3))

    def at(self, j, k):
        return (self.one + j) % 4, (self.two + k) % 4

    def move(self, x, device, slot):
        self.net.copy(x, x, device, self.group, slot)

    def send(self, j):
        x = self.block(*self.at(j, 0))
        self.move(x, self.second[1], self.p[j])
        self.move(x, self.second[3], self.q[j])

    def start(self):
        x = self.block(*self.at(0, 0))
        self.move(x, self.first[1], self.a)
        self.move(x, self.first[3], self.b)
        self.send(0)

    def near_one(self):
        self.net.arrived(self.block(*self.at(3, 0)), self.a)
        self.move(self.half(*self.at(3, 0), 0), self.first[1], self.c)
        self.net.arrived(self.block(*self.at(1, 0)), self.b)
        self.move(self.half(*self.at(1, 0), 1), self.first[3], self.c)

    def far_one(self):
        self.net.arrived(self.block(*self.at(2, 0)), self.c)
        self.send(2)

    def near_two(self, j):
        self.net.arrived(self.block(*self.at(j, 3)), self.p[j])
        self.move(self.half(*self.at(j, 3), 0), self.second[1], self.r[j])
        self.net.arrived(self.block(*self.at(j, 1)), self.q[j])
        self.move(self.half(*self.at(j, 1), 1), self.second[3], self.r[j])

    def far_two(self, j):
        self.net.arrived(self.block(*self.at(j, 2)), self.r[j])


class WideGather:
    def __init__(self, net, buf, y, z, c, n):
        self.net, self.buf, self.c = net, buf, c
        self.group, self.slot = net.group(), net.slot()

        def dev(y, z, c):
            return (wide_of(y, z, c), n)

        def block(start):
            return buf.at[pl.ds(start, 16)]

        def half(start, h):
            return buf.at[pl.ds(start, 16), pl.ds(h * 1024, 1024)]

        self.other = dev(y, z, 1 - c)
        self.slots = (slot_a, slot_b)
        self.parts = (
            Gather2(
                net, self.group, y, z, lambda i: dev(i, z, c), lambda i: dev(y, i, c),
                lambda i, k: block(slot_a(c, k, i)), lambda i, k, h: half(slot_a(c, k, i), h),
            ),
            Gather2(
                net, self.group, z, y, lambda i: dev(y, i, c), lambda i: dev(i, z, c),
                lambda i, k: block(slot_b(c, k, i)), lambda i, k, h: half(slot_b(c, k, i), h),
            ),
        )

    def cross(self, k):
        for part, slot in zip(self.parts, self.slots):
            x = self.buf.at[pl.ds(slot(self.c, (part.two + k) % 4, 0), 64)]
            self.net.copy(x, x, self.other, self.group, self.slot)

    def start(self):
        for x in self.parts:
            x.start()

    def near_one(self):
        for x in self.parts:
            x.near_one()
        for x in self.parts:
            x.send(3)
        for x in self.parts:
            x.send(1)

    def far_one(self):
        for x in self.parts:
            x.far_one()
        self.cross(0)

    def near_two(self, j):
        for x in self.parts:
            x.near_two(j)

    def cross_near(self):
        self.cross(3)
        self.cross(1)

    def far_two(self, j):
        for x in self.parts:
            x.far_two(j)
            b = x.block(*x.at(j, 2))
            self.net.copy(b, b, self.other, self.group, self.slot)

    def finish(self):
        self.net.arrived(self.buf.at[pl.ds(0, 512)], self.slot)

    def drain(self):
        self.net.sent(self.buf.at[pl.ds(0, 992)], self.group)


class Scatter:
    def __init__(self, net, group, me, device, part, passed, rh, got, rl, rr):
        self.net, self.group, self.part = net, group, part
        self.passed, self.rh, self.got, self.rl, self.rr = passed, rh, got, rl, rr
        self.me, self.right, self.left = me, (me + 1) % 4, (me + 3) % 4
        self.to_right, self.to_left = device(self.right), device(self.left)
        self.s, self.a = net.slot(), net.slot()

    def move(self, x, to, device, slot):
        self.net.copy(x, to, device, self.group, slot)

    def start(self):
        self.start_far()
        self.start_right()
        self.start_left()

    def start_far(self):
        far = (self.me + 2) % 4
        self.move(self.part(far, 0), self.rh[0], self.to_right, self.s)
        self.move(self.part(far, 1), self.rh[1], self.to_left, self.s)

    def start_right(self):
        self.move(self.part(self.right, 1), self.rl(1), self.to_right, self.a)

    def start_left(self):
        self.move(self.part(self.left, 0), self.rr(0), self.to_left, self.a)

    def step(self):
        self.net.arrived(self.passed, self.s)
        p = self.part(self.right, 0)
        p[...] = (p[...].astype(F32) + self.rh[0][...].astype(F32)).astype(BF16)
        self.move(p, self.rl(0), self.to_right, self.a)
        p = self.part(self.left, 1)
        p[...] = (p[...].astype(F32) + self.rh[1][...].astype(F32)).astype(BF16)
        self.move(p, self.rr(1), self.to_left, self.a)

    def finish(self):
        self.net.arrived(self.got, self.a)

    def half(self, h):
        return self.part(self.me, h)[...].astype(F32) + (self.rl(h)[...].astype(F32) + self.rr(h)[...].astype(F32))


class WideScatter:
    def __init__(self, net, tile, out, got, acc, r1, r2, y, z, c, n):
        self.net, self.tile, self.out, self.got, self.acc, self.c = net, tile, out, got, acc, c
        self.group, self.slots = net.group(), (net.slot(), net.slot())

        def dev(y, z, c):
            return (wide_of(y, z, c), n)

        self.other = dev(y, z, 1 - c)

        def cols(ref, start, h):
            return ref.at[pl.ds(aligned(start, 16), 16), pl.ds(h * 1024, 1024)]

        def ring(me, device, part, ref, base):
            return Scatter(
                net, self.group, me, device, part,
                ref.at[pl.ds(base, 16)], (cols(ref, base, 0), cols(ref, base, 1)),
                ref.at[pl.ds(base + 16, 32)], lambda h: cols(ref, base + 16, h), lambda h: cols(ref, base + 32, h),
            )

        def first(base, one, two, device, k):
            return {
                j: ring(two, device, lambda i, h, j=j: cols(acc, base + i * 64 + (one + j) % 4 * 16, h), r1.at[k], j * 48)
                for j in (2, 1, 3, 0)
            }

        def second(base, one, two, device, k):
            return ring(one, device, lambda i, h: cols(acc, base + two * 64 + i * 16, h), r2, k * 48)

        def along_y(i):
            return dev(i, z, c)

        def along_z(i):
            return dev(y, i, c)

        self.one = (first(0, y, z, along_z, 0), first(256, z, y, along_y, 1))
        self.two = (second(0, y, z, along_y, 0), second(256, z, y, along_z, 1))

    def exchange(self):
        for p in range(2):
            mine = pl.ds(p * 256, 256)
            for i in range(4):
                cs = slice(i * COLS, (i + 1) * COLS)
                self.out[mine, cs] = self.tile(aligned(p * 512 + (1 - self.c) * 256, 256), cs).astype(BF16)
            self.net.copy(self.out.at[mine], self.got.at[mine], self.other, self.group, self.slots[p])

    def start(self):
        for p in range(2):
            mine = pl.ds(p * 256, 256)
            self.net.arrived(self.got.at[mine], self.slots[p])
            for i in range(4):
                cs = slice(i * COLS, (i + 1) * COLS)
                term = self.tile(aligned(p * 512 + self.c * 256, 256), cs)
                self.acc[mine, cs] = (term + self.got[mine, cs].astype(F32)).astype(BF16)
            for j in (2, 1, 3, 0):
                self.one[p][j].start()

    def step(self, j):
        for x in self.one:
            x[j].step()

    def hand_on(self, j):
        for x, t in zip(self.one, self.two):
            r = x[j]
            r.finish()
            for h in range(2):
                r.part(r.me, h)[...] = r.half(h).astype(BF16)
            if j == 2:
                t.start_far()
            if j == 1:
                t.start_right()
            if j == 3:
                t.start_left()

    def second_step(self):
        for r in self.two:
            r.step()

    def finish(self):
        for r in self.two:
            r.finish()

    def result(self, i, cs):
        return self.two[i].half(cs)

    def drain(self, ref):
        self.net.sent(ref.at[pl.ds(0, 992)], self.group)


def wide_peers(y, z, c):
    for d in range(1, 32):
        yield wide_of((y + d // 8) % 4, (z + d // 2 % 4) % 4, (c + d % 2) % 2)


def greet(y, z, c, n):
    peers = [(wide_of((y + d) % 4, z, c), n) for d in (1, 3)]
    peers += [(wide_of(y, (z + d) % 4, c), n) for d in (1, 3)]
    peers += [(wide_of(y, z, 1 - c), n)]
    peers += [(wide_of(y, z, c), (n + d) % 4) for d in (1, 3, 2)]
    barrier = pltpu.get_barrier_semaphore()
    for p in peers:
        pl.semaphore_signal(barrier, inc=1, device_id=p, device_id_type=MESH)
    pl.semaphore_wait(barrier, len(peers))


def repeat(count, step, body):
    def turn(i, _):
        for j in range(step):
            body(i * step + j)
        return 0

    lax.fori_loop(0, count // step, turn, 0)


def nt(a, b):
    return lax.dot_general(a, b, (((1,), (1,)), ((), ())), preferred_element_type=F32)


GELU_A = float(np.sqrt(2.0 / np.pi))
GELU_B = 0.044715


def dot(a, b):
    return jnp.dot(a, b, preferred_element_type=F32)


def lanes(shape):
    return lax.broadcasted_iota(jnp.int32, shape, len(shape) - 1)


def swap(x):
    return jnp.where(lanes(x.shape) < ROT // 2, pltpu.roll(x, 128 - ROT // 2, 1), pltpu.roll(x, ROT // 2, 1))


def block_kernel(
    dealing, lengths, tok, cot, wq, wk, wv, wu, wo, wd, v_gain, v_bias, b_q, b_k, b_v, b_o, b_u, b_d, cos_all, sin_all,
    res, ig, grad_l, grad_u, grad_f, small, norm,
    ln, g, w, wm, wmo, xs, gbs, xhat, cosine, sine, pre, slope, hb, dpre, kv, kk, xq, xd, od, dkvt, dkv, dkvp,
    rdkv, sum_f, sum_u, sum_l, r_f, r_u, r_l, out_1, got_1, acc_1, r1_1, r2_1, out_2, got_2, acc_2, r1_2, r2_2,
    trans, hidden, cmask, bsend, bfin, csend, cfin, ssend, srecv, brecv, wrecv, bias, index, there, kpos, send, recv, local,
):
    y, z, c, n = coords()
    net = Net(send, recv, (wide_of(y, z, 1 - c), n))
    my_cols = pl.ds(aligned(n * COLS, COLS), COLS)
    me = wide_of(y, z, c)
    own_a, own_b = slot_a(c, z, y), slot_b(c, y, z)

    def to(m):
        return (me, m)

    def w_cols(i):
        return pl.ds(aligned(i * COLS, COLS), COLS)

    def share(i):
        return pl.ds(aligned(i * PART, PART), PART)

    tables = [
        pltpu.make_async_copy(cos_all.at[n], cosine, local.at[0]),
        pltpu.make_async_copy(sin_all.at[n], sine, local.at[1]),
    ]
    for t in tables:
        t.start()
    w[256:320, my_cols] = wk[...]
    w[320:384, my_cols] = wv[...]
    w[384:448, my_cols] = wq[...]
    w[0:256, my_cols] = wu[...].T
    wm[0:256, my_cols] = wd[...]
    wm[256:320, my_cols] = wo[...]
    for i in range(4):
        gbs[n, i : i + 1, :] = v_gain[:, i * 128 : i * 128 + 128]
        gbs[n, 4 + i : 5 + i, :] = v_bias[:, i * 128 : i * 128 + 128]
    xs[:, my_cols] = tok[share(n), :]
    row = lax.broadcasted_iota(jnp.int32, (BLOCK, COLS), 0)
    block = dealing[me]
    valid = block % (MAXLEN // BLOCK) * BLOCK + row < jnp.where(block < MAXLEN // BLOCK, lengths[0], lengths[1])
    cmask[...] = jnp.where(valid, cot[...], jnp.zeros_like(cot))
    mine = cmask[share(n), :]
    g[pl.ds(own_a, 16), my_cols] = mine[0:16]
    g[pl.ds(own_b, 16), my_cols] = mine[16:32]
    greet(y, z, c, n)

    rings, turns = net.group(), net.group()
    tokens_in, gains_in, cot_in = net.slot(), net.slot(), net.slot()
    gains_out = net.group()
    for j in (1, 3, 2):
        m = (n + j) % 4
        net.copy(tok.at[share(m)], xs.at[:, my_cols], to(m), turns, tokens_in)
        net.copy(gbs.at[n], gbs.at[n], to(m), gains_out, gains_in)

    def x_ring(ref, start, count):
        half = count // 2
        return Ring(
            net, rings, n, to,
            lambda i: ref.at[pl.ds(start, count), w_cols(i)],
            lambda i, h: ref.at[pl.ds(start + h * half, half), w_cols(i)],
        )

    a_ring = x_ring(w, 256, 192)
    u_ring = x_ring(w, 0, 256)
    d_ring = x_ring(wm, 0, 256)
    o_ring = x_ring(wm, 256, 64)
    kv_ring = [
        Ring(
            net, rings, n, to,
            lambda i, s=s: kv.at[i, pl.ds(s * 512, 512)],
            lambda i, h, s=s: kv.at[i, pl.ds(s * 512 + h * 256, 256)],
        )
        for s in range(2)
    ]
    a_ring.start()
    for j in (1, 3, 2):
        m = (n + j) % 4
        for p, start in enumerate((own_a, own_b)):
            x = cmask.at[pl.ds(aligned(m * PART + p * 16, 16), 16)]
            net.copy(x, g.at[pl.ds(start, 16), my_cols], to(m), turns, cot_in)
    u_ring.start()
    o_ring.start()

    at = lanes((8, 128))
    part = lax.broadcasted_iota(jnp.int32, (8, 128), 0)
    found = jnp.zeros((8, 128), jnp.int32)
    for b in range(NBLK):
        sy, sz, sc = b // 8, b // 2 % 4, b % 2
        found = jnp.where((part < 2) & (at == dealing[b]), jnp.where(part == 0, (sc * 4 + sz) * 4 + sy, 32 + (sc * 4 + sy) * 4 + sz), found)
        found = jnp.where((part == 2) & (at == (sc * 4 + sz) * 4 + sy), 2 * dealing[b], found)
        found = jnp.where((part == 2) & (at == 32 + (sc * 4 + sy) * 4 + sz), 2 * dealing[b] + 1, found)
    index[...] = found
    to_scalars = pltpu.make_async_copy(index, there, local.at[2])
    to_scalars.start()
    half = ROT // 2
    bias[:, 0:128] = b_u[0:1, :].astype(F32)
    bias[:, 128:256] = b_u[1:2, :].astype(F32)
    bias[:, 256:320] = b_k[...].astype(F32)
    bias[:, 320:384] = b_v[...].astype(F32)
    bias[:, 384:448] = b_q[...].astype(F32)
    bias[:, 448:464] = b_q[:, half:ROT].astype(F32)
    bias[:, 464:480] = b_q[:, 0:half].astype(F32)
    bias[:, 480:496] = b_k[:, half:ROT].astype(F32)
    bias[:, 496:512] = b_k[:, 0:half].astype(F32)
    for s in range(2):
        at = lanes((8, MAXLEN))
        kpos[s] = jnp.where(at < lengths[s], at, 1 << 20)
    wmo[0:64, :] = jnp.zeros((64, D), BF16)

    net.arrived(dpre.at[pl.ds(0, 96)], tokens_in)
    x = xs[...].astype(F32)
    mean = jnp.sum(x, 1, keepdims=True) / D
    var = jnp.sum(x * x, 1, keepdims=True) / D - mean * mean
    inv = lax.rsqrt(var + EPS)
    xhat[...] = (x - mean) * inv
    net.arrived(srecv.at[pl.ds(0, 3)], gains_in)
    for i in range(16):
        cs = slice(i * 128, (i + 1) * 128)
        low = (xhat[:, cs] * gbs[i // 4, i % 4 : i % 4 + 1, :] + gbs[i // 4, i % 4 + 4 : i % 4 + 5, :]).astype(BF16)
        ln[pl.ds(own_a, 16), cs] = low[0:16]
        ln[pl.ds(own_b, 16), cs] = low[16:32]

    lg = WideGather(net, ln, y, z, c, n)
    gg = WideGather(net, g, y, z, c, n)
    lg.start()
    for t in tables:
        t.wait()
    to_scalars.wait()
    lg.near_one()
    a_ring.forward()
    lg.near_two(0)
    net.arrived(dpre.at[pl.ds(0, 96)], cot_in)
    lg.far_one()
    gg.start()
    lg.near_two(3)
    u_ring.forward()
    lg.near_two(1)
    o_ring.forward()
    lg.near_two(2)
    lg.cross_near()
    gg.near_one()
    for j in (0, 3, 1, 2):
        lg.far_two(j)
    d_ring.start()
    a_ring.finish()
    gg.near_two(0)
    gg.far_one()

    w[448:640, :] = w[256:448, :]
    w[640:656, :] = w[400:416, :]
    w[656:672, :] = w[384:400, :]
    w[672:688, :] = w[272:288, :]
    w[688:704, :] = w[256:272, :]

    lg.finish()

    def project(i, _):
        r = pl.ds(aligned(i * 512, 512), 512)
        pre[pl.ds(i * 32, 32)] = (nt(ln[r, :], w[448:704, :]) + bias[:, 256:512]).reshape(32, 16, 256)
        return 0

    lax.fori_loop(0, 2, project, 0)

    def arrange(i):
        both = pre[there[i % 2, i // 2]]
        r = pl.ds(aligned(i * 16, 16), 16)
        tab = pl.ds(aligned((i % 32) * 16, 16), 16)
        a, b = both[:, 0:128], both[:, 128:256]
        cs, sn = cosine[tab, :], sine[tab, :]
        kv[n, r, :] = (a * cs + pltpu.roll(b, 32, 1) * sn).astype(BF16)
        q = (b * cs + pltpu.roll(b, 64, 1) * sn) * (HEAD_DIM**-0.5)
        xq[r, :] = jnp.where(lanes((16, 128)) < HEAD_DIM, q, 0.0).astype(BF16)

    repeat(32, 8, arrange)
    kv_ring[0].start()
    repeat(32, 8, lambda i: arrange(i + 32))
    kv_ring[1].start()
    gg.near_two(3)
    gg.near_two(1)
    gg.near_two(2)
    gg.cross_near()
    u_ring.finish()

    def units(i, _):
        r = pl.ds(aligned(i * 512, 512), 512)
        v = nt(ln[r, :], w[0:256, :]) + bias[:, 0:256]
        t = jnp.tanh(GELU_A * (v + GELU_B * (v * v * v)))
        hb[r, :] = (0.5 * v * (1.0 + t)).astype(BF16)
        slope[r, :] = 0.5 * (1.0 + t) + 0.5 * v * (1.0 - t * t) * (GELU_A * (1.0 + 3.0 * GELU_B * (v * v)))
        return 0

    lax.fori_loop(0, 2, units, 0)
    hidden[0:256, :] = hb[...].T
    hidden[256:288, :] = jnp.ones((32, ROWS), BF16)
    kv_ring[0].forward()
    for j in (0, 3, 1, 2):
        gg.far_two(j)
    o_ring.finish()
    wmo[64:128, :] = wm[256:320, :]
    gg.finish()

    def grad_o(i, _):
        r = pl.ds(aligned(i * 512, 512), 512)
        pre[pl.ds(i * 32, 32), :, 0:128] = nt(g[r, :], wmo[...]).reshape(32, 16, 128)
        return 0

    lax.fori_loop(0, 2, grad_o, 0)

    def arrange_do(i):
        xd[pl.ds(aligned(i * 16, 16), 16), :] = pre[there[i % 2, i // 2], :, 0:128].astype(BF16)

    repeat(64, 8, arrange_do)
    kv_ring[1].forward()

    def scatter_cols(buf, count, r):
        half = count // 2
        return Scatter(
            net, net.group(), n, to,
            lambda i, h: buf.at[pl.ds(h * half, half), w_cols(i)],
            r.at[0], (r.at[0, pl.ds(0, half)], r.at[0, pl.ds(half, half)]),
            r.at[pl.ds(1, 2)], lambda h: r.at[1, pl.ds(h * half, half)], lambda h: r.at[2, pl.ds(h * half, half)],
        )

    f_sum = scatter_cols(sum_f, 288, r_f)
    u_sum = scatter_cols(sum_u, 256, r_u)
    l_sum = scatter_cols(sum_l, 256, r_l)

    def gather_keys(i):
        for m in range(4):
            kk[pl.ds(aligned(i * BLOCK + m * PART, PART), PART), :] = kv[m, share(i), :]

    def attend(s, t):
        keys = 512 * (t + 1)
        r = pl.ds(s * 512 + t * 128, 128)
        x = jnp.concatenate([xq[r, :], xd[r, :]], 0)
        near = kk[pl.ds(s * MAXLEN, keys), :]
        both = nt(x, near)
        i = lax.broadcasted_iota(jnp.int32, (128, 1), 0)
        qpos = (4 * t + i // PART) * BLOCK + n * PART + i % PART
        scores = jnp.where(kpos[s, 0:1, 0:keys] <= qpos, both[0:128], -1e30)
        e = jnp.exp(scores - jnp.max(scores, 1, keepdims=True))
        p = e * (1.0 / jnp.sum(e, 1, keepdims=True))
        dp = both[128:256]
        ds = p * (dp - jnp.sum(p * dp, 1, keepdims=True))
        yy = jnp.concatenate([ds.astype(BF16), p.astype(BF16)], 0)
        back = dot(yy, near)
        back = jnp.where(lanes((128, 128)) < HEAD_DIM, back[0:128] * (HEAD_DIM**-0.5), back[128:256])
        od[pl.ds(s * 32 + t * 8, 8)] = back.reshape(8, 16, 128)
        grads = dot(x.T, yy)
        if t == 3:
            dkvt[s, :, 0:keys] = grads
        else:
            dkvt[s, :, 0:keys] += grads

    keys_out = net.group()

    def key_sum(s):
        def rows(start, count):
            return pl.ds(s * 512 + start, count)

        return Scatter(
            net, keys_out, n, to,
            lambda i, h: dkv.at[i, rows(h * 256, 256)],
            rdkv.at[0, rows(0, 512)], (rdkv.at[0, rows(0, 256)], rdkv.at[0, rows(256, 256)]),
            rdkv.at[pl.ds(1, 2), rows(0, 512)],
            lambda h: rdkv.at[1, rows(h * 256, 256)],
            lambda h: rdkv.at[2, rows(h * 256, 256)],
        )

    def weight_f(i, _):
        cs = pl.ds(aligned(i * COLS, COLS), COLS)
        sum_f[:, cs] = dot(hidden[...], g[:, cs]).astype(BF16)
        return 0

    kv_sum = [key_sum(0), key_sum(1)]
    for s in range(2):
        kv_ring[s].finish()
        repeat(16, 4, lambda i, s=s: gather_keys(i + 16 * s))
        for t in (3, 2, 1, 0):
            attend(s, t)
            if (s, t) == (1, 2):
                kv_sum[0].step()
            if (s, t) == (0, 2):
                d_ring.forward()

        def turn_keys(i, s=s):
            t = dkvt[s, :, pl.ds(aligned(i * BLOCK, BLOCK), BLOCK)].T.astype(BF16)
            for m in range(4):
                dkv[m, pl.ds(aligned(s * 512 + i * PART, PART), PART), :] = t[m * PART : (m + 1) * PART]

        repeat(16, 4, turn_keys)
        kv_sum[s].start()
    d_ring.finish()

    def grad_units(i, _):
        r = pl.ds(aligned(i * 512, 512), 512)
        dpre[r, 0:256] = (nt(g[r, :], wm[0:256, :]) * slope[r, :]).astype(BF16)
        return 0

    def unrope(i):
        tab = pl.ds(aligned((i % 32) * 16, 16), 16)
        x = od[i]
        od[i] = x * cosine[tab, :] - swap(x) * sine[tab, :]

    repeat(64, 8, unrope)

    def place(i):
        dpre[pl.ds(aligned(i * 16, 16), 16), 384:512] = od[there[2, i]].astype(BF16)

    repeat(64, 8, place)

    def dln_tile(start, cs):
        r = pl.ds(start, 256)
        return dot(dpre[r, 0:448], w[0:448, cs])

    def branch_tile(start, cs):
        r = pl.ds(start, 256)
        return dot(hb[r, :], wm[0:256, cs]) + dot(dpre[r, 384:512], wmo[:, cs])

    branch = WideScatter(net, branch_tile, out_1, got_1, acc_1, r1_1, r2_1, y, z, c, n)
    dln = WideScatter(net, dln_tile, out_2, got_2, acc_2, r1_2, r2_2, y, z, c, n)
    branch.exchange()
    kv_sum[1].step()
    lax.fori_loop(0, 2, grad_units, 0)

    def unrope_keys(i):
        tab = pl.ds(aligned((i % 32) * 16, 16), 16)
        r = pl.ds(aligned(i * 16, 16), 16)
        x = dkv[n, r, :].astype(F32) + (rdkv[1, r, :].astype(F32) + rdkv[2, r, :].astype(F32))
        dkvp[i] = x * cosine[tab, :] - swap(x) * sine[tab, :]

    kv_sum[0].finish()
    repeat(32, 8, unrope_keys)
    branch.start()
    kv_sum[1].finish()
    repeat(32, 8, lambda i: unrope_keys(i + 32))

    def place_keys(i):
        dpre[pl.ds(aligned(i * 16, 16), 16), 256:384] = dkvp[there[2, i]].astype(BF16)

    repeat(64, 8, place_keys)
    dln.exchange()
    lax.fori_loop(0, 4, weight_f, 0)
    f_sum.start()
    branch.step(2)
    branch.step(1)
    dln.start()
    branch.step(3)
    branch.step(0)
    trans[...] = dpre[:, 0:256].T

    def weight_u(i, _):
        cs = pl.ds(aligned(i * COLS, COLS), COLS)
        sum_u[:, cs] = dot(trans[...], ln[:, cs]).astype(BF16)
        return 0

    lax.fori_loop(0, 4, weight_u, 0)
    u_sum.start()
    dln.step(2)
    dln.step(1)
    branch.hand_on(2)
    branch.hand_on(1)
    dln.step(3)
    dln.step(0)
    f_sum.step()
    trans[...] = dpre[:, 256:512].T

    def weight_l(i, _):
        cs = pl.ds(aligned(i * COLS, COLS), COLS)
        sum_l[0:192, cs] = dot(trans[0:192, :], ln[:, cs]).astype(BF16)
        sum_l[192:256, cs] = dot(trans[192:256, :], g[:, cs]).astype(BF16)
        return 0

    lax.fori_loop(0, 4, weight_l, 0)
    l_sum.start()
    dln.hand_on(2)
    dln.hand_on(1)
    dln.hand_on(3)
    dln.second_step()
    dln.hand_on(0)
    branch.hand_on(3)
    branch.second_step()
    branch.hand_on(0)
    u_sum.step()
    sums = jnp.sum(dpre[...].astype(F32), 0, keepdims=True)
    for i in range(4):
        brecv[n, i : i + 1, :] = sums[:, i * 128 : i * 128 + 128]
    small_out, small_in, branch_out, branch_in = net.group(), net.slot(), net.group(), net.slot()
    for j in (1, 3, 2):
        net.copy(brecv.at[n], brecv.at[n], to((n + j) % 4), small_out, small_in)
    dln.finish()

    for i in range(2):
        for h in range(2):
            csend[i * 16 : (i + 1) * 16, h * 1024 : (h + 1) * 1024] = dln.result(i, h)
    grad = csend[...]
    sums = (jnp.sum(grad * xhat[...], 0, keepdims=True), jnp.sum(grad, 0, keepdims=True))
    for m in range(4):
        for k in range(2):
            for i in range(4):
                ssend[m, 4 * k + i : 4 * k + i + 1, :] = sums[k][:, m * COLS + i * 128 : m * COLS + i * 128 + 128]
    srecv[n] = ssend[n]
    norm_out, norm_in, final_out, final_in, all_out, all_in = net.group(), net.slot(), net.group(), net.slot(), net.group(), net.slot()
    for j in (1, 3, 2):
        m = (n + j) % 4
        net.copy(ssend.at[m], srecv.at[n], to(m), norm_out, norm_in)
    for i in range(16):
        cs = slice(i * 128, (i + 1) * 128)
        csend[:, cs] = csend[:, cs] * gbs[i // 4, i % 4 : i % 4 + 1, :]
    grad = csend[...]
    first = jnp.sum(grad, 1, keepdims=True) / D
    second = jnp.sum(grad * xhat[...], 1, keepdims=True) / D
    x = xs[...].astype(F32)
    mean = jnp.sum(x, 1, keepdims=True) / D
    var = jnp.sum(x * x, 1, keepdims=True) / D - mean * mean
    csend[...] = lax.rsqrt(var + EPS) * (grad - first - xhat[...] * second)
    cfin[share(n), :] = csend[:, my_cols]
    for j in (1, 3, 2):
        m = (n + j) % 4
        net.copy(csend.at[:, w_cols(m)], cfin.at[share(n)], to(m), final_out, final_in)
    net.arrived(srecv.at[pl.ds(0, 3)], norm_in)
    wrecv[me] = (srecv[0] + srecv[1]) + (srecv[2] + srecv[3])
    for p in wide_peers(y, z, c):
        net.copy(wrecv.at[me], wrecv.at[me], (p, n), all_out, all_in)
    l_sum.step()
    branch.finish()
    for i in range(2):
        for h in range(2):
            bsend[i * 16 : (i + 1) * 16, h * 1024 : (h + 1) * 1024] = branch.result(i, h).astype(BF16)
    bfin[share(n), :] = bsend[:, my_cols]
    for j in (1, 3, 2):
        m = (n + j) % 4
        net.copy(bsend.at[:, w_cols(m)], bfin.at[share(n)], to(m), branch_out, branch_in)
    f_sum.finish()
    for h in range(2):
        grad_f[h * 144 : (h + 1) * 144, :] = f_sum.half(h)
    u_sum.finish()
    for h in range(2):
        grad_u[h * 128 : (h + 1) * 128, :] = u_sum.half(h)
    l_sum.finish()
    for h in range(2):
        grad_l[h * 128 : (h + 1) * 128, :] = l_sum.half(h)
    net.arrived(dpre.at[pl.ds(0, 96)], branch_in)
    net.arrived(srecv.at[pl.ds(0, 3)], small_in)
    block = dealing[me]
    valid = block % (MAXLEN // BLOCK) * BLOCK + row < jnp.where(block < MAXLEN // BLOCK, lengths[0], lengths[1])
    valid = valid[:, 0:128]
    for i in range(4):
        cs = slice(i * 128, i * 128 + 128)
        base = bfin[:, cs].astype(F32) + (b_o[i : i + 1, :].astype(F32) + b_d[i : i + 1, :].astype(F32))
        res[:, cs] = (tok[:, cs].astype(F32) + jnp.where(valid, base, 0.0)).astype(BF16)
    small[...] = (brecv[0] + brecv[1]) + (brecv[2] + brecv[3])
    net.arrived(cfin.at[pl.ds(0, 96)], final_in)
    ig[...] = cot[...].astype(F32) + cfin[...]
    net.arrived(wrecv.at[pl.ds(0, 31)], all_in)
    norm[...] = jnp.sum(wrecv[...], 0)

    lg.drain()
    gg.drain()
    branch.drain(ln)
    dln.drain(ln)
    net.sent(ln.at[pl.ds(0, 768)], rings)
    net.sent(ln.at[pl.ds(0, 192)], keys_out)
    net.sent(dpre.at[pl.ds(0, 864)], f_sum.group)
    net.sent(dpre.at[pl.ds(0, 768)], u_sum.group)
    net.sent(dpre.at[pl.ds(0, 768)], l_sum.group)
    net.sent(dpre.at[pl.ds(0, 192)], turns)
    net.sent(srecv.at[pl.ds(0, 3)], gains_out)
    net.sent(srecv.at[pl.ds(0, 3)], small_out)
    net.sent(dpre.at[pl.ds(0, 96)], branch_out)
    net.sent(srecv.at[pl.ds(0, 3)], norm_out)
    net.sent(cfin.at[pl.ds(0, 96)], final_out)
    net.sent(wrecv.at[pl.ds(0, 31)], all_out)
    assert (net.groups, net.slots) == (SENDS, ARRIVALS), (net.groups, net.slots)


def call_block(*args):
    vmem, anywhere = pl.BlockSpec(memory_space=pltpu.VMEM), pl.BlockSpec(memory_space=pl.ANY)
    shape = jax.ShapeDtypeStruct

    def buf(dtype, *size):
        return pltpu.VMEM(size, dtype)

    wide = [buf(BF16, 512, D), buf(BF16, 512, D), buf(BF16, 512, D), buf(BF16, 2, 192, D), buf(BF16, 96, D)]
    return pl.pallas_call(
        block_kernel,
        out_shape=(
            shape((BLOCK, COLS), BF16),
            shape((BLOCK, COLS), F32),
            shape((256, COLS), F32),
            shape((256, COLS), F32),
            shape((288, COLS), F32),
            shape((8, 128), F32),
            shape((8, 128), F32),
        ),
        in_specs=[pl.BlockSpec(memory_space=pltpu.SMEM)] * 2 + [vmem] * 16 + [anywhere] * 2,
        out_specs=(vmem,) * 7,
        scratch_shapes=[
            buf(BF16, ROWS, D),
            buf(BF16, ROWS, D),
            buf(BF16, 704, D),
            buf(BF16, 320, D),
            buf(BF16, 128, D),
            buf(BF16, PART, D),
            buf(F32, 4, 8, 128),
            buf(F32, PART, D),
            buf(F32, 512, 128),
            buf(F32, 512, 128),
            buf(F32, 64, 16, 256),
            buf(F32, ROWS, UNITS),
            buf(BF16, ROWS, UNITS),
            buf(BF16, ROWS, 512),
            buf(BF16, 4, ROWS, 128),
            buf(BF16, 2 * MAXLEN, 128),
            buf(BF16, ROWS, 128),
            buf(BF16, ROWS, 128),
            buf(F32, 64, 16, 128),
            buf(F32, 2, 128, MAXLEN),
            buf(BF16, 4, ROWS, 128),
            buf(F32, 64, 16, 128),
            buf(BF16, 3, ROWS, 128),
            buf(BF16, 288, D),
            buf(BF16, 256, D),
            buf(BF16, 256, D),
            buf(BF16, 3, 288, COLS),
            buf(BF16, 3, 256, COLS),
            buf(BF16, 3, 256, COLS),
            *wide,
            *wide,
            buf(BF16, 256, ROWS),
            buf(BF16, 288, ROWS),
            buf(BF16, BLOCK, COLS),
            buf(BF16, PART, D),
            buf(BF16, BLOCK, COLS),
            buf(F32, PART, D),
            buf(F32, BLOCK, COLS),
            buf(F32, 4, 8, 128),
            buf(F32, 4, 8, 128),
            buf(F32, 4, 8, 128),
            buf(F32, 32, 8, 128),
            buf(F32, 1, COLS),
            buf(jnp.int32, 8, 128),
            pltpu.SMEM((8, 128), jnp.int32),
            buf(jnp.int32, 2, 8, MAXLEN),
            pltpu.SemaphoreType.DMA((SENDS,)),
            pltpu.SemaphoreType.DMA((ARRIVALS,)),
            pltpu.SemaphoreType.DMA((3,)),
        ],
        compiler_params=pltpu.CompilerParams(collective_id=0, has_side_effects=True, vmem_limit_bytes=63 * 2**20),
    )(*args)


def split_kernel(
    res, ig, grad_l, grad_u, grad_f, small, norm,
    res_o, ig_o, gain_o, bias_o, q_o, bq_o, k_o, bk_o, v_o, bv_o, o_o, bo_o, u_o, bu_o, f_o, bf_o,
):
    res_o[...] = res[...]
    ig_o[...] = ig[...]
    k_o[...] = grad_l[0:64, :]
    v_o[...] = grad_l[64:128, :]
    q_o[...] = grad_l[128:192, :]
    o_o[...] = grad_l[192:256, :]
    u_o[...] = grad_u[...].T
    f_o[...] = grad_f[0:256, :]
    for i in range(4):
        gain_o[:, i * 128 : i * 128 + 128] = norm[i : i + 1, :]
        bias_o[:, i * 128 : i * 128 + 128] = norm[4 + i : 5 + i, :]
    bu_o[:, 0:128] = small[0:1, :]
    bu_o[:, 128:256] = small[1:2, :]
    bk_o[...] = small[2:3, 0:64]
    bv_o[...] = small[2:3, 64:128]
    bq_o[...] = small[3:4, 0:64]
    bo_o[...] = grad_f[256:257, :]
    bf_o[...] = grad_f[256:257, :]


def call_split(*args):
    vmem = pl.BlockSpec(memory_space=pltpu.VMEM)
    head, vector = (64, COLS), (1, COLS)
    sizes = [
        (BLOCK, COLS), vector, vector, head, (1, 64), head, (1, 64), head, (1, 64), head, vector,
        (COLS, UNITS), (1, UNITS), (UNITS, COLS), vector,
    ]
    return pl.pallas_call(
        split_kernel,
        out_shape=(jax.ShapeDtypeStruct((BLOCK, COLS), BF16), *(jax.ShapeDtypeStruct(s, F32) for s in sizes)),
        in_specs=[vmem] * 7,
        out_specs=(vmem,) * 16,
        compiler_params=pltpu.CompilerParams(vmem_limit_bytes=62 * 2**20),
    )(*args)


def on_device(
    tokens, ln_gain, ln_bias, w_query, b_query, w_key, b_key, w_value, b_value, w_out, b_out,
    w_fc1, b_fc1, w_fc2, b_fc2, cotangent, lengths, dealing,
):
    cosine, sine = (
        np.ascontiguousarray(t.reshape(MAXLEN // BLOCK, 4, PART, 128).transpose(1, 0, 2, 3)).reshape(4, -1, 128)
        for t in rope_tables()
    )
    out = call_block(
        dealing, lengths, tokens, cotangent, w_query.T, w_key.T, w_value.T, w_fc1, w_out, w_fc2,
        ln_gain[None], ln_bias[None], b_query[None], b_key[None], b_value[None], b_out.reshape(-1, 128),
        b_fc1.reshape(-1, 128), b_fc2.reshape(-1, 128),
        jnp.asarray(cosine), jnp.asarray(sine),
    )
    out = list(call_split(*out))
    for i in (4, 6, 8):
        out[i] = out[i].T
    for i in (2, 3, 5, 7, 9, 11, 13, 15):
        out[i] = out[i][0]
    return tuple(out)


def solution(mesh):
    rows, col, units = P("wide", "narrow"), P("narrow"), P("wide")
    weight, out = P("narrow", "wide"), P("wide", "narrow")
    placed = (
        rows, col, col, weight, units, weight, units, weight, units, out, col, weight, units, out, col, rows, P(), P(),
    )
    given = (
        rows, rows, col, col, weight, units, weight, units, weight, units, out, col, weight, units, out, col,
    )
    return jax.shard_map(on_device, mesh=mesh, in_specs=placed, out_specs=given, check_vma=False)
```

```python
import jax
import jax.numpy as jnp
import numpy as np
from jax import lax
from jax.experimental import pallas as pl
from jax.experimental.pallas import tpu as pltpu
from jax.sharding import PartitionSpec as P

MESH = pl.DeviceIdType.MESH
D = 2048
HEAD_DIM = 64
ROT = 32
BLOCK = 128
MAXLEN = 2048
NBLK = 32
PART = 32
ROWS = NBLK * PART
COLS = 512
UNITS = 256
EPS = 1e-05
SENDS, ARRIVALS = 17, 143
BF16 = jnp.bfloat16
F32 = jnp.float32


def rope_tables():
    half = ROT // 2
    inverse = (10000.0 ** (-(np.arange(half, dtype=np.float32) * np.float32(2.0) / np.float32(ROT)))).astype(np.float32)
    angles = (np.arange(MAXLEN, dtype=np.float32)[:, None] * inverse[None, :]).astype(np.float64)
    cosine = np.ones((MAXLEN, 128), np.float32)
    sine = np.zeros((MAXLEN, 128), np.float32)
    cosine[:, :half] = np.cos(angles)
    cosine[:, half:ROT] = np.cos(angles)
    sine[:, :half] = -np.sin(angles)
    sine[:, half:ROT] = np.sin(angles)
    return cosine, sine


class Net:
    def __init__(self, send, recv, anyone):
        self.send, self.recv, self.anyone = send, recv, anyone
        self.groups = self.slots = 0

    def group(self):
        self.groups += 1
        return self.groups - 1

    def slot(self):
        self.slots += 1
        return self.slots - 1

    def make(self, src, dst, device, group, slot):
        return pltpu.make_async_remote_copy(
            src_ref=src,
            dst_ref=dst,
            send_sem=self.send.at[group],
            recv_sem=self.recv.at[slot],
            device_id=device,
            device_id_type=MESH,
        )

    def copy(self, src, dst, device, group, slot):
        self.make(src, dst, device, group, slot).start()

    def arrived(self, ref, slot):
        self.make(ref, ref, self.anyone, 0, slot).wait_recv()

    def sent(self, ref, group):
        self.make(ref, ref, self.anyone, group, 0).wait_send()


class Ring:
    def __init__(self, net, group, me, device, unit, half):
        self.net, self.group, self.unit, self.half = net, group, unit, half
        self.me, self.right, self.left = me, (me + 1) % 4, (me + 3) % 4
        self.to_right, self.to_left = device(self.right), device(self.left)
        self.a, self.b, self.c = net.slot(), net.slot(), net.slot()

    def send(self, x, device, slot):
        self.net.copy(x, x, device, self.group, slot)

    def start(self):
        own = self.unit(self.me)
        self.send(own, self.to_right, self.a)
        self.send(own, self.to_left, self.b)

    def forward(self):
        self.net.arrived(self.unit(self.left), self.a)
        self.send(self.half(self.left, 0), self.to_right, self.c)
        self.net.arrived(self.unit(self.right), self.b)
        self.send(self.half(self.right, 1), self.to_left, self.c)

    def finish(self):
        self.net.arrived(self.unit((self.me + 2) % 4), self.c)


def coords():
    w, n = lax.axis_index("wide"), lax.axis_index("narrow")
    return w // 8, (w // 2) % 4, w % 2, n


def wide_of(y, z, c):
    return (y * 4 + z) * 2 + c


def aligned(x, m):
    return pl.multiple_of(x, m)


def slot_a(c, z, y):
    return aligned(((c * 4 + z) * 4 + y) * 16, 16)


def slot_b(c, y, z):
    return aligned((32 + (c * 4 + y) * 4 + z) * 16, 16)


class Gather2:
    def __init__(self, net, group, one, two, first, second, block, half):
        self.net, self.group, self.block, self.half = net, group, block, half
        self.one, self.two = one, two
        self.first = [first((one + j) % 4) for j in range(4)]
        self.second = [second((two + j) % 4) for j in range(4)]
        self.a, self.b, self.c = net.slot(), net.slot(), net.slot()
        self.p, self.q, self.r = ([net.slot() for _ in range(4)] for _ in range(3))

    def at(self, j, k):
        return (self.one + j) % 4, (self.two + k) % 4

    def move(self, x, device, slot):
        self.net.copy(x, x, device, self.group, slot)

    def send(self, j):
        x = self.block(*self.at(j, 0))
        self.move(x, self.second[1], self.p[j])
        self.move(x, self.second[3], self.q[j])

    def start(self):
        x = self.block(*self.at(0, 0))
        self.move(x, self.first[1], self.a)
        self.move(x, self.first[3], self.b)
        self.move(x, self.first[2], self.c)
        self.send(0)

    def near_one(self):
        self.net.arrived(self.block(*self.at(3, 0)), self.a)
        self.send(3)
        self.net.arrived(self.block(*self.at(1, 0)), self.b)
        self.send(1)

    def far_one(self):
        self.net.arrived(self.block(*self.at(2, 0)), self.c)
        self.send(2)

    def near_two(self, j):
        self.net.arrived(self.block(*self.at(j, 3)), self.p[j])
        self.move(self.half(*self.at(j, 3), 0), self.second[1], self.r[j])
        self.net.arrived(self.block(*self.at(j, 1)), self.q[j])
        self.move(self.half(*self.at(j, 1), 1), self.second[3], self.r[j])

    def far_two(self, j):
        self.net.arrived(self.block(*self.at(j, 2)), self.r[j])


class WideGather:
    def __init__(self, net, buf, y, z, c, n):
        self.net, self.buf, self.c = net, buf, c
        self.group, self.slot = net.group(), net.slot()

        def dev(y, z, c):
            return (wide_of(y, z, c), n)

        def block(start):
            return buf.at[pl.ds(start, 16)]

        def half(start, h):
            return buf.at[pl.ds(start, 16), pl.ds(h * 1024, 1024)]

        self.other = dev(y, z, 1 - c)
        self.slots = (slot_a, slot_b)
        self.parts = (
            Gather2(
                net, self.group, y, z, lambda i: dev(i, z, c), lambda i: dev(y, i, c),
                lambda i, k: block(slot_a(c, k, i)), lambda i, k, h: half(slot_a(c, k, i), h),
            ),
            Gather2(
                net, self.group, z, y, lambda i: dev(y, i, c), lambda i: dev(i, z, c),
                lambda i, k: block(slot_b(c, k, i)), lambda i, k, h: half(slot_b(c, k, i), h),
            ),
        )

    def cross(self, k):
        for part, slot in zip(self.parts, self.slots):
            x = self.buf.at[pl.ds(slot(self.c, (part.two + k) % 4, 0), 64)]
            self.net.copy(x, x, self.other, self.group, self.slot)

    def start(self):
        for x in self.parts:
            x.start()

    def near_one(self):
        for x in self.parts:
            x.near_one()

    def far_one(self):
        for x in self.parts:
            x.far_one()
        self.cross(0)

    def near_two(self, j):
        for x in self.parts:
            x.near_two(j)

    def cross_near(self):
        self.cross(3)
        self.cross(1)

    def far_two(self, j):
        for x in self.parts:
            x.far_two(j)
            b = x.block(*x.at(j, 2))
            self.net.copy(b, b, self.other, self.group, self.slot)

    def finish(self):
        self.net.arrived(self.buf.at[pl.ds(0, 512)], self.slot)

    def drain(self):
        self.net.sent(self.buf.at[pl.ds(0, 992)], self.group)


class Scatter:
    def __init__(self, net, group, me, device, part, passed, rh, got, rl, rr):
        self.net, self.group, self.part = net, group, part
        self.passed, self.rh, self.got, self.rl, self.rr = passed, rh, got, rl, rr
        self.me, self.right, self.left = me, (me + 1) % 4, (me + 3) % 4
        self.to_right, self.to_left = device(self.right), device(self.left)
        self.s, self.a = net.slot(), net.slot()

    def move(self, x, to, device, slot):
        self.net.copy(x, to, device, self.group, slot)

    def start(self):
        self.start_far()
        self.start_right()
        self.start_left()

    def start_far(self):
        far = (self.me + 2) % 4
        self.move(self.part(far, 0), self.rh[0], self.to_right, self.s)
        self.move(self.part(far, 1), self.rh[1], self.to_left, self.s)

    def start_right(self):
        self.move(self.part(self.right, 1), self.rl(1), self.to_right, self.a)

    def start_left(self):
        self.move(self.part(self.left, 0), self.rr(0), self.to_left, self.a)

    def step(self):
        self.net.arrived(self.passed, self.s)
        p = self.part(self.right, 0)
        p[...] = (p[...].astype(F32) + self.rh[0][...].astype(F32)).astype(BF16)
        self.move(p, self.rl(0), self.to_right, self.a)
        p = self.part(self.left, 1)
        p[...] = (p[...].astype(F32) + self.rh[1][...].astype(F32)).astype(BF16)
        self.move(p, self.rr(1), self.to_left, self.a)

    def finish(self):
        self.net.arrived(self.got, self.a)

    def half(self, h):
        return self.part(self.me, h)[...].astype(F32) + (self.rl(h)[...].astype(F32) + self.rr(h)[...].astype(F32))


class Direct:
    def __init__(self, net, group, me, device, part, got, base):
        self.net, self.group, self.me, self.part = net, group, me, part
        self.device, self.got, self.base, self.slot = device, got, base, net.slot()

    def send(self, j):
        i = (self.me + j) % 4
        x = self.part(i)
        self.net.copy(x, self.got.at[pl.ds(self.base + 16 * (j - 1), 16)], self.device(i), self.group, self.slot)

    def finish(self):
        self.net.arrived(self.got.at[pl.ds(self.base, 48)], self.slot)

    def result(self, cs):
        total = self.part(self.me)[:, cs].astype(F32)
        for j in range(3):
            total += self.got[self.base + 16 * j : self.base + 16 * j + 16, cs].astype(F32)
        return total


class WideScatter:
    def __init__(self, net, tile, out, got, acc, r1, r2, y, z, c, n):
        self.net, self.tile, self.out, self.got, self.acc, self.c = net, tile, out, got, acc, c
        self.group, self.slots = net.group(), (net.slot(), net.slot())

        def dev(y, z, c):
            return (wide_of(y, z, c), n)

        self.other = dev(y, z, 1 - c)

        def cols(ref, start, h):
            return ref.at[pl.ds(aligned(start, 16), 16), pl.ds(h * 1024, 1024)]

        def ring(me, device, part, ref, base):
            return Scatter(
                net, self.group, me, device, part,
                ref.at[pl.ds(base, 16)], (cols(ref, base, 0), cols(ref, base, 1)),
                ref.at[pl.ds(base + 16, 32)], lambda h: cols(ref, base + 16, h), lambda h: cols(ref, base + 32, h),
            )

        def first(base, one, two, device, k):
            return {
                j: ring(two, device, lambda i, h, j=j: cols(acc, base + i * 64 + (one + j) % 4 * 16, h), r1.at[k], j * 48)
                for j in (2, 1, 3, 0)
            }

        def second(base, one, two, device, k):
            return Direct(
                net, self.group, one, device,
                lambda i: acc.at[pl.ds(aligned(base + two * 64 + i * 16, 16), 16)], r2, k * 48,
            )

        def along_y(i):
            return dev(i, z, c)

        def along_z(i):
            return dev(y, i, c)

        self.one = (first(0, y, z, along_z, 0), first(256, z, y, along_y, 1))
        self.two = (second(0, y, z, along_y, 0), second(256, z, y, along_z, 1))

    def exchange(self):
        for p in range(2):
            mine = pl.ds(p * 256, 256)
            for i in range(4):
                cs = slice(i * COLS, (i + 1) * COLS)
                self.out[mine, cs] = self.tile(aligned(p * 512 + (1 - self.c) * 256, 256), cs).astype(BF16)
            self.net.copy(self.out.at[mine], self.got.at[mine], self.other, self.group, self.slots[p])

    def start(self):
        for p in range(2):
            mine = pl.ds(p * 256, 256)
            self.net.arrived(self.got.at[mine], self.slots[p])
            for i in range(4):
                cs = slice(i * COLS, (i + 1) * COLS)
                term = self.tile(aligned(p * 512 + self.c * 256, 256), cs)
                self.acc[mine, cs] = (term + self.got[mine, cs].astype(F32)).astype(BF16)
            for j in (2, 1, 3, 0):
                self.one[p][j].start_far()
            for j in (2, 1, 3, 0):
                self.one[p][j].start_right()
                self.one[p][j].start_left()

    def step(self, j):
        for x in self.one:
            x[j].step()

    def hand_on(self, j, also=None):
        for p, (x, t) in enumerate(zip(self.one, self.two)):
            r = x[j]
            r.finish()
            for h in range(2):
                v = r.half(h)
                r.part(r.me, h)[...] = v.astype(BF16)
                if also is not None:
                    also(p, (t.me + j) % 4, slice(h * 1024, (h + 1) * 1024), v)
            if j:
                t.send(j)

    def finish(self):
        for r in self.two:
            r.finish()

    def result(self, i, cs):
        return self.two[i].result(cs)

    def drain(self, ref):
        self.net.sent(ref.at[pl.ds(0, 992)], self.group)


def other_chips(y, z, c):
    for d in range(1, 16):
        yield wide_of((y + d // 4) % 4, (z + d % 4) % 4, c)


def greet(y, z, c, n):
    peers = [(wide_of((y + d) % 4, z, c), n) for d in (1, 3, 2)]
    peers += [(wide_of(y, (z + d) % 4, c), n) for d in (1, 3, 2)]
    peers += [(wide_of(y, z, 1 - c), n)]
    peers += [(wide_of(y, z, c), (n + d) % 4) for d in (1, 3, 2)]
    barrier = pltpu.get_barrier_semaphore()
    for p in peers:
        pl.semaphore_signal(barrier, inc=1, device_id=p, device_id_type=MESH)
    return lambda: pl.semaphore_wait(barrier, len(peers))


def repeat(count, step, body):
    def turn(i, _):
        for j in range(step):
            body(i * step + j)
        return 0

    lax.fori_loop(0, count // step, turn, 0)


def nt(a, b):
    return lax.dot_general(a, b, (((1,), (1,)), ((), ())), preferred_element_type=F32)


GELU_A = float(np.sqrt(2.0 / np.pi))
GELU_B = 0.044715


def dot(a, b):
    return jnp.dot(a, b, preferred_element_type=F32)


def lanes(shape):
    return lax.broadcasted_iota(jnp.int32, shape, len(shape) - 1)


def swap(x):
    return jnp.where(lanes(x.shape) < ROT // 2, pltpu.roll(x, 128 - ROT // 2, 1), pltpu.roll(x, ROT // 2, 1))


def block_kernel(
    dealing, lengths, i_tok, i_cot, i_wq, i_wk, i_wv, i_wu, i_wo, i_wd,
    i_gain, i_bias, i_bq, i_bk, i_bv, i_bo, i_bu, i_bd, cos_all, sin_all,
    o_res, o_ig, o_gain, o_bias, o_q, o_bq, o_k, o_bk, o_v, o_bv, o_o, o_bo, o_u, o_bu, o_f,
    tok, cot, wu, v_gain, v_bias, b_q, b_k, b_v, b_o, b_u, b_d,
    res, ig, grad_l, grad_u, grad_f, v_512, v_64, v_256,
    ln, g, w, wm, wmo, xs, gbs, xhat, cosine, sine, cosine_held, sine_held, slope, hb, dpre, kv, kk, xq, xd, od, dkvt, dkv, dkvp,
    rdkv, sum_f, sum_u, sum_l, r_f, r_u, r_l, out_1, got_1, acc_1, r1_1, r2_1, out_2, got_2, acc_2, r1_2, r2_2,
    trans, hidden, cmask, bsend, bfin, csend, clow, cfin, ssend, srecv, brecv, wrecv, nsum, hats, column, bias, index, there, kpos, send, recv, local, inward,
):
    y, z, c, n = coords()
    net = Net(send, recv, (wide_of(y, z, 1 - c), n))
    my_cols = pl.ds(aligned(n * COLS, COLS), COLS)
    me = wide_of(y, z, c)
    own_a, own_b = slot_a(c, z, y), slot_b(c, y, z)

    def to(m):
        return (me, m)

    def w_cols(i):
        return pl.ds(aligned(i * COLS, COLS), COLS)

    def share(i):
        return pl.ds(aligned(i * PART, PART), PART)

    loads = []

    def load(x, to):
        loads.append(pltpu.make_async_copy(x, to, inward.at[len(loads)]))
        loads[-1].start()

    load(i_tok, tok)
    load(i_wk, w.at[pl.ds(256, 64), my_cols])
    load(i_wv, w.at[pl.ds(320, 64), my_cols])
    load(i_wq, w.at[pl.ds(384, 64), my_cols])
    load(i_cot, cot)
    load(i_wu, wu)
    load(i_wo, wm.at[pl.ds(256, 64), my_cols])
    load(i_gain, v_gain)
    load(i_bias, v_bias)
    early = len(loads)
    load(i_wd, wm.at[pl.ds(0, 256), my_cols])
    for x, at in ((i_bq, b_q), (i_bk, b_k), (i_bv, b_v), (i_bo, b_o), (i_bu, b_u), (i_bd, b_d)):
        load(x, at)
    load(cos_all.at[n], cosine)
    load(sin_all.at[n], sine)
    all_greeted = greet(y, z, c, n)
    for x in loads[:early]:
        x.wait()
    w[0:256, my_cols] = wu[...].T
    for i in range(4):
        gbs[n, i : i + 1, :] = v_gain[:, i * 128 : i * 128 + 128]
        gbs[n, 4 + i : 5 + i, :] = v_bias[:, i * 128 : i * 128 + 128]
    xs[:, my_cols] = tok[share(n), :]
    row = lax.broadcasted_iota(jnp.int32, (BLOCK, COLS), 0)
    block = dealing[me]
    valid = block % (MAXLEN // BLOCK) * BLOCK + row < jnp.where(block < MAXLEN // BLOCK, lengths[0], lengths[1])
    cmask[...] = jnp.where(valid, cot[...], jnp.zeros_like(cot))
    mine = cmask[share(n), :]
    g[pl.ds(own_a, 16), my_cols] = mine[0:16]
    g[pl.ds(own_b, 16), my_cols] = mine[16:32]
    all_greeted()

    rings, turns = net.group(), net.group()
    tokens_in, gains_in, cot_in = net.slot(), net.slot(), net.slot()
    gains_out = net.group()
    for j in (1, 3, 2):
        m = (n + j) % 4
        net.copy(tok.at[share(m)], xs.at[:, my_cols], to(m), turns, tokens_in)
        net.copy(gbs.at[n], gbs.at[n], to(m), gains_out, gains_in)

    def x_ring(ref, start, count):
        half = count // 2
        return Ring(
            net, rings, n, to,
            lambda i: ref.at[pl.ds(start, count), w_cols(i)],
            lambda i, h: ref.at[pl.ds(start + h * half, half), w_cols(i)],
        )

    a_ring = x_ring(w, 256, 192)
    u_ring = x_ring(w, 0, 256)
    d_ring = x_ring(wm, 0, 256)
    o_ring = x_ring(wm, 256, 64)
    kv_ring = [
        Ring(
            net, rings, n, to,
            lambda i, s=s: kv.at[i, pl.ds(s * 32, 32)],
            lambda i, h, s=s: kv.at[i, pl.ds(s * 32 + h * 16, 16)],
        )
        for s in range(2)
    ]
    a_ring.start()
    for j in (1, 3, 2):
        m = (n + j) % 4
        for p, start in enumerate((own_a, own_b)):
            x = cmask.at[pl.ds(aligned(m * PART + p * 16, 16), 16)]
            net.copy(x, g.at[pl.ds(start, 16), my_cols], to(m), turns, cot_in)
    u_ring.start()
    o_ring.start()

    for x in loads[early:]:
        x.wait()
    at = lanes((8, 128))
    part = lax.broadcasted_iota(jnp.int32, (8, 128), 0)
    found = jnp.zeros((8, 128), jnp.int32)
    for b in range(NBLK):
        sy, sz, sc = b // 8, b // 2 % 4, b % 2
        found = jnp.where((part < 2) & (at == dealing[b]), jnp.where(part == 0, (sc * 4 + sz) * 4 + sy, 32 + (sc * 4 + sy) * 4 + sz), found)
        found = jnp.where((part == 2) & (at == (sc * 4 + sz) * 4 + sy), 2 * dealing[b], found)
        found = jnp.where((part == 2) & (at == 32 + (sc * 4 + sy) * 4 + sz), 2 * dealing[b] + 1, found)
        found = jnp.where((part == 3) & (at == (sc * 4 + sz) * 4 + sy), 2 * dealing[b] % 32, found)
        found = jnp.where((part == 3) & (at == 32 + (sc * 4 + sy) * 4 + sz), 2 * dealing[b] % 32 + 1, found)
    index[...] = found
    to_scalars = pltpu.make_async_copy(index, there, local.at[0])
    to_scalars.start()
    half = ROT // 2
    bias[:, 0:128] = b_u[0:1, :].astype(F32)
    bias[:, 128:256] = b_u[1:2, :].astype(F32)
    bias[:, 256:320] = b_k[...].astype(F32)
    bias[:, 320:384] = b_v[...].astype(F32)
    bias[:, 384:448] = b_q[...].astype(F32)
    bias[:, 448:464] = b_q[:, half:ROT].astype(F32)
    bias[:, 464:480] = b_q[:, 0:half].astype(F32)
    bias[:, 480:496] = b_k[:, half:ROT].astype(F32)
    bias[:, 496:512] = b_k[:, 0:half].astype(F32)
    for s in range(2):
        at = lanes((8, MAXLEN))
        kpos[s] = jnp.where(at < lengths[s], at, 1 << 20)
    wmo[0:64, :] = jnp.zeros((64, D), BF16)

    net.arrived(dpre.at[pl.ds(0, 96)], tokens_in)
    x = xs[...].astype(F32)
    mean = jnp.sum(x, 1, keepdims=True) / D
    var = jnp.sum(x * x, 1, keepdims=True) / D - mean * mean
    inv = lax.rsqrt(var + EPS)
    xhat[...] = (x - mean) * inv
    net.arrived(srecv.at[pl.ds(0, 3)], gains_in)
    for i in range(16):
        cs = slice(i * 128, (i + 1) * 128)
        low = (xhat[:, cs] * gbs[i // 4, i % 4 : i % 4 + 1, :] + gbs[i // 4, i % 4 + 4 : i % 4 + 5, :]).astype(BF16)
        ln[pl.ds(own_a, 16), cs] = low[0:16]
        ln[pl.ds(own_b, 16), cs] = low[16:32]

    lg = WideGather(net, ln, y, z, c, n)
    gg = WideGather(net, g, y, z, c, n)
    lg.start()
    to_scalars.wait()

    def hold(i):
        cosine_held[i] = cosine[there[3, i]]
        sine_held[i] = sine[there[3, i]]

    repeat(64, 8, hold)
    lg.near_one()
    a_ring.forward()
    d_ring.start()
    net.arrived(dpre.at[pl.ds(0, 96)], cot_in)
    lg.near_two(0)
    lg.far_one()
    gg.start()
    lg.near_two(3)
    lg.near_two(1)
    lg.near_two(2)
    lg.cross_near()
    gg.near_one()
    u_ring.forward()
    o_ring.forward()
    for j in (0, 3, 1, 2):
        lg.far_two(j)
    a_ring.finish()
    gg.near_two(0)
    gg.far_one()

    w[448:640, :] = w[256:448, :]
    w[640:656, :] = w[400:416, :]
    w[656:672, :] = w[384:400, :]
    w[672:688, :] = w[272:288, :]
    w[688:704, :] = w[256:272, :]

    lg.finish()
    x = (nt(ln[...], w[448:704, :]) + bias[:, 256:512]).reshape(64, 16, 256)
    a, b = x[:, :, 0:128], x[:, :, 128:256]
    kv[n] = (a * cosine_held[...] + pltpu.roll(b, 32, 2) * sine_held[...]).astype(BF16)
    kv_ring[0].start()
    kv_ring[1].start()
    x = (b * cosine_held[...] + pltpu.roll(b, 64, 2) * sine_held[...]) * (HEAD_DIM**-0.5)
    xq[...] = jnp.where(lanes((64, 16, 128)) < HEAD_DIM, x, 0.0).astype(BF16)
    gg.near_two(3)
    gg.near_two(1)
    gg.near_two(2)
    gg.cross_near()
    u_ring.finish()

    def units(i, _):
        r = pl.ds(aligned(i * 512, 512), 512)
        v = nt(ln[r, :], w[0:256, :]) + bias[:, 0:256]
        t = jnp.tanh(GELU_A * (v + GELU_B * (v * v * v)))
        hb[r, :] = (0.5 * v * (1.0 + t)).astype(BF16)
        slope[r, :] = 0.5 * (1.0 + t) + 0.5 * v * (1.0 - t * t) * (GELU_A * (1.0 + 3.0 * GELU_B * (v * v)))
        return 0

    lax.fori_loop(0, 2, units, 0)
    hidden[0:256, :] = hb[...].T
    hidden[256:288, :] = jnp.ones((32, ROWS), BF16)
    def scatter_cols(buf, count, r):
        half = count // 2
        return Scatter(
            net, net.group(), n, to,
            lambda i, h: buf.at[pl.ds(h * half, half), w_cols(i)],
            r.at[0], (r.at[0, pl.ds(0, half)], r.at[0, pl.ds(half, half)]),
            r.at[pl.ds(1, 2)], lambda h: r.at[1, pl.ds(h * half, half)], lambda h: r.at[2, pl.ds(h * half, half)],
        )

    f_sum = scatter_cols(sum_f, 288, r_f)
    u_sum = scatter_cols(sum_u, 256, r_u)
    l_sum = scatter_cols(sum_l, 256, r_l)

    def weight_f(i, _):
        cs = pl.ds(aligned(i * 1024, 1024), 1024)
        sum_f[:, cs] = dot(hidden[...], g[:, cs]).astype(BF16)
        return 0

    kv_ring[0].forward()
    d_ring.forward()
    o_ring.finish()
    wmo[64:128, :] = wm[256:320, :]
    for j in (0, 3, 1, 2):
        gg.far_two(j)
    kv_ring[1].forward()

    gg.finish()
    hats_out, hats_in = net.group(), net.slot()
    hats[y] = xhat[0:16, :]
    hats[4 + z] = xhat[16:32, :]
    for d in (1, 3, 2):
        net.copy(xhat.at[pl.ds(0, 16)], hats.at[y], (wide_of((y + d) % 4, z, c), n), hats_out, hats_in)
        net.copy(xhat.at[pl.ds(16, 16)], hats.at[4 + z], (wide_of(y, (z + d) % 4, c), n), hats_out, hats_in)
    lax.fori_loop(0, 2, weight_f, 0)
    f_sum.start()

    def grad_o(i, _):
        r = pl.ds(aligned(i * 512, 512), 512)
        xd[pl.ds(i * 32, 32)] = nt(g[r, :], wmo[...]).astype(BF16).reshape(32, 16, 128)
        return 0

    lax.fori_loop(0, 2, grad_o, 0)

    def gather_keys(i):
        for m in range(4):
            for p in range(2):
                kk[pl.ds(aligned(i * BLOCK + m * PART + p * 16, 16), 16), :] = kv[m, there[p, i]]

    def attend(s, t):
        keys = 512 * (t + 1)
        held = [there[k % 2, s * 16 + t * 4 + k // 2] for k in range(8)]
        x = jnp.concatenate([xq[i] for i in held] + [xd[i] for i in held], 0)
        near = kk[pl.ds(s * MAXLEN, keys), :]
        both = nt(x, near)
        i = lax.broadcasted_iota(jnp.int32, (128, 1), 0)
        qpos = (4 * t + i // PART) * BLOCK + n * PART + i % PART
        scores = jnp.where(kpos[s, 0:1, 0:keys] <= qpos, both[0:128], -1e30)
        e = jnp.exp(scores - jnp.max(scores, 1, keepdims=True))
        p = e * (1.0 / jnp.sum(e, 1, keepdims=True))
        dp = both[128:256]
        ds = p * (dp - jnp.sum(p * dp, 1, keepdims=True))
        yy = jnp.concatenate([ds.astype(BF16), p.astype(BF16)], 0)
        back = dot(yy, near)
        back = jnp.where(lanes((128, 128)) < HEAD_DIM, back[0:128] * (HEAD_DIM**-0.5), back[128:256])
        od[pl.ds(s * 32 + t * 8, 8)] = back.reshape(8, 16, 128)
        grads = dot(x.T, yy)
        if t == 3:
            dkvt[s, :, 0:keys] = grads
        else:
            dkvt[s, :, 0:keys] += grads

    keys_out = net.group()

    def key_sum(s, part):
        def rows(start, count):
            return pl.ds(s * 512 + part * 256 + start, count)

        return Scatter(
            net, keys_out, n, to,
            lambda i, h: dkv.at[i, rows(h * 128, 128)],
            rdkv.at[0, rows(0, 256)], (rdkv.at[0, rows(0, 128)], rdkv.at[0, rows(128, 128)]),
            rdkv.at[pl.ds(1, 2), rows(0, 256)],
            lambda h: rdkv.at[1, rows(h * 128, 128)],
            lambda h: rdkv.at[2, rows(h * 128, 128)],
        )

    def turn_keys(s, h):
        for i in range(8 * h, 8 * h + 8):
            t = dkvt[s, :, i * BLOCK : (i + 1) * BLOCK].T.astype(BF16)
            for m in range(4):
                dkv[m, s * 512 + i * PART : s * 512 + (i + 1) * PART, :] = t[m * PART : (m + 1) * PART]

    kv_sum = [key_sum(0, 1), key_sum(0, 0), key_sum(1, 1), key_sum(1, 0)]
    kv_ring[0].finish()
    kv_ring[1].finish()
    repeat(32, 4, gather_keys)
    attend(0, 3)
    attend(0, 2)
    turn_keys(0, 1)
    kv_sum[0].start()
    attend(0, 1)
    attend(0, 0)
    turn_keys(0, 0)
    kv_sum[1].start()
    attend(1, 3)
    attend(1, 2)
    turn_keys(1, 1)
    kv_sum[2].start()
    attend(1, 1)
    attend(1, 0)
    turn_keys(1, 0)
    kv_sum[3].start()
    kv_sum[0].step()
    kv_sum[1].step()

    def unrope(s):
        x = od[pl.ds(s * 32, 32)].reshape(512, 128)
        od[pl.ds(s * 32, 32)] = (x * cosine[...].reshape(512, 128) - swap(x) * sine[...].reshape(512, 128)).reshape(32, 16, 128)

    unrope(0)
    unrope(1)

    def place(i):
        dpre[pl.ds(aligned(i * 16, 16), 16), 384:512] = od[there[2, i]].astype(BF16)

    repeat(64, 8, place)

    def dln_tile(start, cs):
        r = pl.ds(start, 256)
        return dot(dpre[r, 0:448], w[0:448, cs])

    def branch_tile(start, cs):
        r = pl.ds(start, 256)
        return dot(hb[r, :], wm[0:256, cs]) + dot(dpre[r, 384:512], wmo[:, cs])

    branch = WideScatter(net, branch_tile, out_1, got_1, acc_1, r1_1, r2_1, y, z, c, n)
    dln = WideScatter(net, dln_tile, out_2, got_2, acc_2, r1_2, r2_2, y, z, c, n)
    d_ring.finish()
    branch.exchange()
    kv_sum[2].step()

    def grad_units(i, _):
        r = pl.ds(aligned(i * 512, 512), 512)
        dpre[r, 0:256] = (nt(g[r, :], wm[0:256, :]) * slope[r, :]).astype(BF16)
        return 0

    lax.fori_loop(0, 2, grad_units, 0)

    kv_sum[3].step()
    trans[...] = dpre[:, 0:256].T

    def weight_u(i, _):
        cs = pl.ds(aligned(i * 1024, 1024), 1024)
        sum_u[:, cs] = dot(trans[...], ln[:, cs]).astype(BF16)
        return 0

    lax.fori_loop(0, 2, weight_u, 0)
    u_sum.start()
    def unrope_keys(s):
        r = pl.ds(s * 512, 512)
        x = dkv[n, r, :].astype(F32) + (rdkv[1, r, :].astype(F32) + rdkv[2, r, :].astype(F32))
        dkvp[pl.ds(s * 32, 32)] = (x * cosine[...].reshape(512, 128) - swap(x) * sine[...].reshape(512, 128)).reshape(32, 16, 128)

    kv_sum[0].finish()
    kv_sum[1].finish()
    unrope_keys(0)
    branch.start()
    kv_sum[2].finish()
    kv_sum[3].finish()
    unrope_keys(1)

    def place_keys(i):
        dpre[pl.ds(aligned(i * 16, 16), 16), 256:384] = dkvp[there[2, i]].astype(BF16)

    repeat(64, 8, place_keys)
    dln.exchange()
    trans[...] = dpre[:, 256:512].T

    def weight_l(i, _):
        cs = pl.ds(aligned(i * 1024, 1024), 1024)
        sum_l[0:192, cs] = dot(trans[0:192, :], ln[:, cs]).astype(BF16)
        sum_l[192:256, cs] = dot(trans[192:256, :], g[:, cs]).astype(BF16)
        return 0

    lax.fori_loop(0, 2, weight_l, 0)
    l_sum.start()
    branch.step(2)
    branch.step(1)
    dln.start()
    branch.step(3)
    branch.step(0)
    f_sum.step()
    for j in (2, 1, 3, 0):
        dln.step(j)
    for j in (2, 1, 3, 0):
        branch.hand_on(j)
    u_sum.step()

    def norm_sums(p, i, cs, v):
        column[0:1, cs] += jnp.sum(v * hats[4 * p + i, :, cs], 0, keepdims=True)
        column[1:2, cs] += jnp.sum(v, 0, keepdims=True)

    column[...] = jnp.zeros((8, D), F32)
    net.arrived(hats.at[pl.ds(0, 6)], hats_in)
    for j in (2, 1, 3, 0):
        dln.hand_on(j, norm_sums)
    norm_out, norm_in, final_out, final_in, all_out, all_in = net.group(), net.slot(), net.group(), net.slot(), net.group(), net.slot()
    for m in range(4):
        for k in range(2):
            for i in range(4):
                ssend[m, 4 * k + i : 4 * k + i + 1, :] = column[k : k + 1, m * COLS + i * 128 : m * COLS + i * 128 + 128]
    chip = y * 4 + z
    wrecv[chip] = ssend[...]
    for p in other_chips(y, z, c):
        net.copy(ssend, wrecv.at[chip], (p, n), norm_out, norm_in)
    sums = jnp.sum(dpre[...].astype(F32), 0, keepdims=True)
    for i in range(4):
        brecv[n, i : i + 1, :] = sums[:, i * 128 : i * 128 + 128]
    small_out, small_in, branch_out, branch_in = net.group(), net.slot(), net.group(), net.slot()
    for j in (1, 3, 2):
        net.copy(brecv.at[n], brecv.at[n], to((n + j) % 4), small_out, small_in)
    l_sum.step()
    branch.finish()
    for i in range(2):
        for h in range(2):
            cs = slice(h * 1024, (h + 1) * 1024)
            bsend[i * 16 : (i + 1) * 16, cs] = branch.result(i, cs).astype(BF16)
    bfin[share(n), :] = bsend[:, my_cols]
    for j in (1, 3, 2):
        m = (n + j) % 4
        net.copy(bsend.at[:, w_cols(m)], bfin.at[share(n)], to(m), branch_out, branch_in)
    dln.finish()

    for i in range(2):
        for h in range(2):
            cs = slice(h * 1024, (h + 1) * 1024)
            csend[i * 16 : (i + 1) * 16, cs] = dln.result(i, cs)
    for i in range(16):
        cs = slice(i * 128, (i + 1) * 128)
        csend[:, cs] = csend[:, cs] * gbs[i // 4, i % 4 : i % 4 + 1, :]
    grad = csend[...]
    first = jnp.sum(grad, 1, keepdims=True) / D
    second = jnp.sum(grad * xhat[...], 1, keepdims=True) / D
    x = xs[...].astype(F32)
    mean = jnp.sum(x, 1, keepdims=True) / D
    var = jnp.sum(x * x, 1, keepdims=True) / D - mean * mean
    clow[...] = (lax.rsqrt(var + EPS) * (grad - first - xhat[...] * second)).astype(BF16)
    cfin[share(n), :] = clow[:, my_cols]
    for j in (1, 3, 2):
        m = (n + j) % 4
        net.copy(clow.at[:, w_cols(m)], cfin.at[share(n)], to(m), final_out, final_in)
    net.arrived(wrecv.at[pl.ds(0, 15)], norm_in)
    nsum[...] = jnp.sum(wrecv[...], 0)
    srecv[n * 2 + c] = nsum[n]
    for j in (1, 3, 2, 0):
        m = (n + j) % 4
        for d in (0, 1) if j else (1,):
            net.copy(nsum.at[m], srecv.at[n * 2 + c], (wide_of(y, z, (c + d) % 2), m), all_out, all_in)
    outs = []

    def give(x, to):
        outs.append(pltpu.make_async_copy(x, to, local.at[1 + len(outs)]))
        outs[-1].start()

    f_sum.finish()
    for h in range(2):
        grad_f[h * 144 : (h + 1) * 144, :] = f_sum.half(h)
    v_512[2] = grad_f[256:257, :]
    give(grad_f.at[pl.ds(0, 256)], o_f)
    give(v_512.at[2], o_bo)
    u_sum.finish()
    for h in range(2):
        grad_u[:, h * 128 : (h + 1) * 128] = u_sum.half(h).T
    give(grad_u, o_u)
    l_sum.finish()
    for h in range(2):
        grad_l[h * 128 : (h + 1) * 128, :] = l_sum.half(h)
    for i, x in enumerate((o_k, o_v, o_q, o_o)):
        give(grad_l.at[pl.ds(64 * i, 64)], x)
    net.arrived(dpre.at[pl.ds(0, 96)], branch_in)
    block = dealing[me]
    valid = block % (MAXLEN // BLOCK) * BLOCK + row < jnp.where(block < MAXLEN // BLOCK, lengths[0], lengths[1])
    valid = valid[:, 0:128]
    for i in range(4):
        cs = slice(i * 128, i * 128 + 128)
        base = bfin[:, cs].astype(F32) + (b_o[i : i + 1, :].astype(F32) + b_d[i : i + 1, :].astype(F32))
        res[:, cs] = (tok[:, cs].astype(F32) + jnp.where(valid, base, 0.0)).astype(BF16)
    give(res, o_res)
    net.arrived(srecv.at[pl.ds(0, 3)], small_in)
    sums = (brecv[0] + brecv[1]) + (brecv[2] + brecv[3])
    v_256[:, 0:128] = sums[0:1]
    v_256[:, 128:256] = sums[1:2]
    v_64[0] = sums[2:3, 0:64]
    v_64[1] = sums[2:3, 64:128]
    v_64[2] = sums[3:4, 0:64]
    give(v_256, o_bu)
    for i, x in enumerate((o_bk, o_bv, o_bq)):
        give(v_64.at[i], x)
    net.arrived(cfin.at[pl.ds(0, 96)], final_in)
    ig[...] = cot[...].astype(F32) + cfin[...].astype(F32)
    give(ig, o_ig)
    net.arrived(srecv.at[pl.ds(0, 7)], all_in)
    sums = jnp.sum(srecv[...], 0)
    for i in range(4):
        v_512[0, :, i * 128 : i * 128 + 128] = sums[i : i + 1]
        v_512[1, :, i * 128 : i * 128 + 128] = sums[4 + i : 5 + i]
    give(v_512.at[0], o_gain)
    give(v_512.at[1], o_bias)

    lg.drain()
    gg.drain()
    branch.drain(ln)
    dln.drain(ln)
    net.sent(ln.at[pl.ds(0, 768)], rings)
    net.sent(ln.at[pl.ds(0, 192)], keys_out)
    net.sent(dpre.at[pl.ds(0, 864)], f_sum.group)
    net.sent(dpre.at[pl.ds(0, 768)], u_sum.group)
    net.sent(dpre.at[pl.ds(0, 768)], l_sum.group)
    net.sent(dpre.at[pl.ds(0, 192)], turns)
    net.sent(srecv.at[pl.ds(0, 3)], gains_out)
    net.sent(srecv.at[pl.ds(0, 3)], small_out)
    net.sent(dpre.at[pl.ds(0, 96)], branch_out)
    net.sent(wrecv.at[pl.ds(0, 15)], norm_out)
    net.sent(cfin.at[pl.ds(0, 96)], final_out)
    net.sent(srecv.at[pl.ds(0, 7)], all_out)
    net.sent(hats.at[pl.ds(0, 6)], hats_out)
    for x in outs:
        x.wait()
    assert (net.groups, net.slots) == (SENDS, ARRIVALS), (net.groups, net.slots)


RESULTS = (
    (BLOCK, COLS), (1, COLS), (1, COLS), (64, COLS), (1, 64), (64, COLS), (1, 64), (64, COLS), (1, 64), (64, COLS), (1, COLS),
    (COLS, UNITS), (1, UNITS), (UNITS, COLS),
)


def call_block(*args):
    anywhere = pl.BlockSpec(memory_space=pl.ANY)
    shape = jax.ShapeDtypeStruct

    def buf(dtype, *size):
        return pltpu.VMEM(size, dtype)

    wide = [buf(BF16, 512, D), buf(BF16, 512, D), buf(BF16, 512, D), buf(BF16, 2, 192, D), buf(BF16, 96, D)]
    return pl.pallas_call(
        block_kernel,
        out_shape=(shape((BLOCK, COLS), BF16), *(shape(x, F32) for x in RESULTS)),
        in_specs=[pl.BlockSpec(memory_space=pltpu.SMEM)] * 2 + [anywhere] * 18,
        out_specs=(anywhere,) * 15,
        scratch_shapes=[
            buf(BF16, BLOCK, COLS),
            buf(BF16, BLOCK, COLS),
            buf(BF16, COLS, UNITS),
            buf(F32, 1, COLS),
            buf(F32, 1, COLS),
            buf(BF16, 1, 64),
            buf(BF16, 1, 64),
            buf(BF16, 1, 64),
            buf(BF16, 4, 128),
            buf(BF16, 2, 128),
            buf(BF16, 4, 128),
            buf(BF16, BLOCK, COLS),
            buf(F32, BLOCK, COLS),
            buf(F32, 256, COLS),
            buf(F32, COLS, UNITS),
            buf(F32, 288, COLS),
            buf(F32, 3, 1, COLS),
            buf(F32, 3, 1, 64),
            buf(F32, 1, UNITS),
            buf(BF16, ROWS, D),
            buf(BF16, ROWS, D),
            buf(BF16, 704, D),
            buf(BF16, 320, D),
            buf(BF16, 128, D),
            buf(BF16, PART, D),
            buf(F32, 4, 8, 128),
            buf(F32, PART, D),
            buf(F32, 32, 16, 128),
            buf(F32, 32, 16, 128),
            buf(F32, 64, 16, 128),
            buf(F32, 64, 16, 128),
            buf(F32, ROWS, UNITS),
            buf(BF16, ROWS, UNITS),
            buf(BF16, ROWS, 512),
            buf(BF16, 4, 64, 16, 128),
            buf(BF16, 2 * MAXLEN, 128),
            buf(BF16, 64, 16, 128),
            buf(BF16, 64, 16, 128),
            buf(F32, 64, 16, 128),
            buf(F32, 2, 128, MAXLEN),
            buf(BF16, 4, ROWS, 128),
            buf(F32, 64, 16, 128),
            buf(BF16, 3, ROWS, 128),
            buf(BF16, 288, D),
            buf(BF16, 256, D),
            buf(BF16, 256, D),
            buf(BF16, 3, 288, COLS),
            buf(BF16, 3, 256, COLS),
            buf(BF16, 3, 256, COLS),
            *wide,
            *wide,
            buf(BF16, 256, ROWS),
            buf(BF16, 288, ROWS),
            buf(BF16, BLOCK, COLS),
            buf(BF16, PART, D),
            buf(BF16, BLOCK, COLS),
            buf(F32, PART, D),
            buf(BF16, PART, D),
            buf(BF16, BLOCK, COLS),
            buf(F32, 4, 8, 128),
            buf(F32, 8, 8, 128),
            buf(F32, 4, 8, 128),
            buf(F32, 16, 4, 8, 128),
            buf(F32, 4, 8, 128),
            buf(F32, 8, 16, D),
            buf(F32, 8, D),
            buf(F32, 1, COLS),
            buf(jnp.int32, 8, 128),
            pltpu.SMEM((8, 128), jnp.int32),
            buf(jnp.int32, 2, 8, MAXLEN),
            pltpu.SemaphoreType.DMA((SENDS,)),
            pltpu.SemaphoreType.DMA((ARRIVALS,)),
            pltpu.SemaphoreType.DMA((18,)),
            pltpu.SemaphoreType.DMA((18,)),
        ],
        compiler_params=pltpu.CompilerParams(collective_id=0, has_side_effects=True, vmem_limit_bytes=63 * 2**20),
    )(*args)


def relay_kernel(*refs):
    given, taken, held, here, there = refs[:15], refs[15:31], refs[31:46], refs[46], refs[47]
    order = sorted(range(15), key=lambda i: -given[i].size)
    come = [pltpu.make_async_copy(given[i], held[i], here.at[i]) for i in range(15)]
    go = [pltpu.make_async_copy(held[i], taken[i], there.at[i]) for i in range(15)]
    go.append(pltpu.make_async_copy(held[11], taken[15], there.at[15]))
    for i in order:
        come[i].start()
    for i in order:
        come[i].wait()
        go[i].start()
        if i == 11:
            go[15].start()
    for x in go:
        x.wait()


def relay(arrays):
    anywhere = pl.BlockSpec(memory_space=pl.ANY)
    return pl.pallas_call(
        relay_kernel,
        out_shape=tuple(jax.ShapeDtypeStruct(x.shape, x.dtype) for x in (*arrays, arrays[11])),
        in_specs=[anywhere] * 15,
        out_specs=(anywhere,) * 16,
        scratch_shapes=[pltpu.VMEM(x.shape, x.dtype) for x in arrays]
        + [pltpu.SemaphoreType.DMA((15,)), pltpu.SemaphoreType.DMA((16,))],
        compiler_params=pltpu.CompilerParams(vmem_limit_bytes=62 * 2**20),
    )(*arrays)


def on_device(
    tokens, ln_gain, ln_bias, w_query, b_query, w_key, b_key, w_value, b_value, w_out, b_out,
    w_fc1, b_fc1, w_fc2, b_fc2, cotangent, lengths, dealing,
):
    cosine, sine = (
        np.ascontiguousarray(t.reshape(MAXLEN // BLOCK, 4, PART, 128).transpose(1, 0, 2, 3)).reshape(4, -1, 16, 128)
        for t in rope_tables()
    )
    out = call_block(
        dealing, lengths, tokens, cotangent, w_query.T, w_key.T, w_value.T, w_fc1, w_out, w_fc2,
        ln_gain[None], ln_bias[None], b_query[None], b_key[None], b_value[None], b_out.reshape(-1, 128),
        b_fc1.reshape(-1, 128), b_fc2.reshape(-1, 128),
        jnp.asarray(cosine), jnp.asarray(sine),
    )
    out = list(relay(out))
    for i in (4, 6, 8):
        out[i] = out[i].T
    for i in (2, 3, 5, 7, 9, 11, 13, 15):
        out[i] = out[i][0]
    return tuple(out)


def solution(mesh):
    rows, col, units = P("wide", "narrow"), P("narrow"), P("wide")
    weight, out = P("narrow", "wide"), P("wide", "narrow")
    placed = (
        rows, col, col, weight, units, weight, units, weight, units, out, col, weight, units, out, col, rows, P(), P(),
    )
    given = (
        rows, rows, col, col, weight, units, weight, units, weight, units, out, col, weight, units, out, col,
    )
    return jax.shard_map(on_device, mesh=mesh, in_specs=placed, out_specs=given, check_vma=False)
```

```python
import jax
import jax.numpy as jnp
import numpy as np
from jax import lax
from jax.experimental import pallas as pl
from jax.experimental.pallas import tpu as pltpu
from jax.sharding import PartitionSpec as P

MESH = pl.DeviceIdType.MESH
D = 2048
HEAD_DIM = 64
ROT = 32
BLOCK = 128
MAXLEN = 2048
NBLK = 32
PART = 32
ROWS = NBLK * PART
COLS = 512
UNITS = 256
EPS = 1e-05
SENDS, ARRIVALS = 17, 143
BF16 = jnp.bfloat16
F32 = jnp.float32


def rope_tables():
    half = ROT // 2
    inverse = (10000.0 ** (-(np.arange(half, dtype=np.float32) * np.float32(2.0) / np.float32(ROT)))).astype(np.float32)
    angles = (np.arange(MAXLEN, dtype=np.float32)[:, None] * inverse[None, :]).astype(np.float64)
    cosine = np.ones((MAXLEN, 128), np.float32)
    sine = np.zeros((MAXLEN, 128), np.float32)
    cosine[:, :half] = np.cos(angles)
    cosine[:, half:ROT] = np.cos(angles)
    sine[:, :half] = -np.sin(angles)
    sine[:, half:ROT] = np.sin(angles)
    return cosine, sine


class Net:
    def __init__(self, send, recv, anyone):
        self.send, self.recv, self.anyone = send, recv, anyone
        self.groups = self.slots = 0

    def group(self):
        self.groups += 1
        return self.groups - 1

    def slot(self):
        self.slots += 1
        return self.slots - 1

    def make(self, src, dst, device, group, slot):
        return pltpu.make_async_remote_copy(
            src_ref=src,
            dst_ref=dst,
            send_sem=self.send.at[group],
            recv_sem=self.recv.at[slot],
            device_id=device,
            device_id_type=MESH,
        )

    def copy(self, src, dst, device, group, slot):
        self.make(src, dst, device, group, slot).start()

    def arrived(self, ref, slot):
        self.make(ref, ref, self.anyone, 0, slot).wait_recv()

    def sent(self, ref, group):
        self.make(ref, ref, self.anyone, group, 0).wait_send()


class Ring:
    def __init__(self, net, group, me, device, unit, half):
        self.net, self.group, self.unit, self.half = net, group, unit, half
        self.me, self.right, self.left = me, (me + 1) % 4, (me + 3) % 4
        self.to_right, self.to_left = device(self.right), device(self.left)
        self.a, self.b, self.c = net.slot(), net.slot(), net.slot()

    def send(self, x, device, slot):
        self.net.copy(x, x, device, self.group, slot)

    def start(self):
        own = self.unit(self.me)
        self.send(own, self.to_right, self.a)
        self.send(own, self.to_left, self.b)

    def forward(self):
        self.net.arrived(self.unit(self.left), self.a)
        self.send(self.half(self.left, 0), self.to_right, self.c)
        self.net.arrived(self.unit(self.right), self.b)
        self.send(self.half(self.right, 1), self.to_left, self.c)

    def finish(self):
        self.net.arrived(self.unit((self.me + 2) % 4), self.c)


def coords():
    w, n = lax.axis_index("wide"), lax.axis_index("narrow")
    return w // 8, (w // 2) % 4, w % 2, n


def wide_of(y, z, c):
    return (y * 4 + z) * 2 + c


def aligned(x, m):
    return pl.multiple_of(x, m)


def slot_a(c, z, y):
    return aligned(((c * 4 + z) * 4 + y) * 16, 16)


def slot_b(c, y, z):
    return aligned((32 + (c * 4 + y) * 4 + z) * 16, 16)


class Gather2:
    def __init__(self, net, group, one, two, first, second, block, half):
        self.net, self.group, self.block, self.half = net, group, block, half
        self.one, self.two = one, two
        self.first = [first((one + j) % 4) for j in range(4)]
        self.second = [second((two + j) % 4) for j in range(4)]
        self.a, self.b, self.c = net.slot(), net.slot(), net.slot()
        self.p, self.q, self.r = ([net.slot() for _ in range(4)] for _ in range(3))

    def at(self, j, k):
        return (self.one + j) % 4, (self.two + k) % 4

    def move(self, x, device, slot):
        self.net.copy(x, x, device, self.group, slot)

    def send(self, j):
        x = self.block(*self.at(j, 0))
        self.move(x, self.second[1], self.p[j])
        self.move(x, self.second[3], self.q[j])

    def start(self):
        x = self.block(*self.at(0, 0))
        self.move(x, self.first[1], self.a)
        self.move(x, self.first[3], self.b)
        self.move(x, self.first[2], self.c)
        self.send(0)

    def near_one(self):
        self.net.arrived(self.block(*self.at(3, 0)), self.a)
        self.send(3)
        self.net.arrived(self.block(*self.at(1, 0)), self.b)
        self.send(1)

    def far_one(self):
        self.net.arrived(self.block(*self.at(2, 0)), self.c)
        self.send(2)

    def near_two(self, j):
        self.net.arrived(self.block(*self.at(j, 3)), self.p[j])
        self.move(self.half(*self.at(j, 3), 0), self.second[1], self.r[j])
        self.net.arrived(self.block(*self.at(j, 1)), self.q[j])
        self.move(self.half(*self.at(j, 1), 1), self.second[3], self.r[j])

    def far_two(self, j):
        self.net.arrived(self.block(*self.at(j, 2)), self.r[j])


class WideGather:
    def __init__(self, net, buf, y, z, c, n):
        self.net, self.buf, self.c = net, buf, c
        self.group, self.slot = net.group(), net.slot()

        def dev(y, z, c):
            return (wide_of(y, z, c), n)

        def block(start):
            return buf.at[pl.ds(start, 16)]

        def half(start, h):
            return buf.at[pl.ds(start, 16), pl.ds(h * 1024, 1024)]

        self.other = dev(y, z, 1 - c)
        self.slots = (slot_a, slot_b)
        self.parts = (
            Gather2(
                net, self.group, y, z, lambda i: dev(i, z, c), lambda i: dev(y, i, c),
                lambda i, k: block(slot_a(c, k, i)), lambda i, k, h: half(slot_a(c, k, i), h),
            ),
            Gather2(
                net, self.group, z, y, lambda i: dev(y, i, c), lambda i: dev(i, z, c),
                lambda i, k: block(slot_b(c, k, i)), lambda i, k, h: half(slot_b(c, k, i), h),
            ),
        )

    def cross(self, k):
        for part, slot in zip(self.parts, self.slots):
            x = self.buf.at[pl.ds(slot(self.c, (part.two + k) % 4, 0), 64)]
            self.net.copy(x, x, self.other, self.group, self.slot)

    def start(self):
        for x in self.parts:
            x.start()

    def near_one(self):
        for x in self.parts:
            x.near_one()

    def far_one(self):
        for x in self.parts:
            x.far_one()
        self.cross(0)

    def near_two(self, j):
        for x in self.parts:
            x.near_two(j)

    def cross_near(self):
        self.cross(3)
        self.cross(1)

    def far_two(self, j):
        for x in self.parts:
            x.far_two(j)
            b = x.block(*x.at(j, 2))
            self.net.copy(b, b, self.other, self.group, self.slot)

    def finish(self):
        self.net.arrived(self.buf.at[pl.ds(0, 512)], self.slot)

    def drain(self):
        self.net.sent(self.buf.at[pl.ds(0, 992)], self.group)


class Scatter:
    def __init__(self, net, group, me, device, part, passed, rh, got, rl, rr):
        self.net, self.group, self.part = net, group, part
        self.passed, self.rh, self.got, self.rl, self.rr = passed, rh, got, rl, rr
        self.me, self.right, self.left = me, (me + 1) % 4, (me + 3) % 4
        self.to_right, self.to_left = device(self.right), device(self.left)
        self.s, self.a = net.slot(), net.slot()

    def move(self, x, to, device, slot):
        self.net.copy(x, to, device, self.group, slot)

    def start(self):
        self.start_far()
        self.start_right()
        self.start_left()

    def start_far(self):
        far = (self.me + 2) % 4
        self.move(self.part(far, 0), self.rh[0], self.to_right, self.s)
        self.move(self.part(far, 1), self.rh[1], self.to_left, self.s)

    def start_right(self):
        self.move(self.part(self.right, 1), self.rl(1), self.to_right, self.a)

    def start_left(self):
        self.move(self.part(self.left, 0), self.rr(0), self.to_left, self.a)

    def step(self):
        self.net.arrived(self.passed, self.s)
        p = self.part(self.right, 0)
        p[...] = (p[...].astype(F32) + self.rh[0][...].astype(F32)).astype(BF16)
        self.move(p, self.rl(0), self.to_right, self.a)
        p = self.part(self.left, 1)
        p[...] = (p[...].astype(F32) + self.rh[1][...].astype(F32)).astype(BF16)
        self.move(p, self.rr(1), self.to_left, self.a)

    def finish(self):
        self.net.arrived(self.got, self.a)

    def half(self, h):
        return self.part(self.me, h)[...].astype(F32) + (self.rl(h)[...].astype(F32) + self.rr(h)[...].astype(F32))


class Direct:
    def __init__(self, net, group, me, device, part, got, base):
        self.net, self.group, self.me, self.part = net, group, me, part
        self.device, self.got, self.base, self.slot = device, got, base, net.slot()

    def send(self, j):
        i = (self.me + j) % 4
        x = self.part(i)
        self.net.copy(x, self.got.at[pl.ds(self.base + 16 * (j - 1), 16)], self.device(i), self.group, self.slot)

    def finish(self):
        self.net.arrived(self.got.at[pl.ds(self.base, 48)], self.slot)

    def result(self, cs):
        total = self.part(self.me)[:, cs].astype(F32)
        for j in range(3):
            total += self.got[self.base + 16 * j : self.base + 16 * j + 16, cs].astype(F32)
        return total


class WideScatter:
    def __init__(self, net, tile, out, got, acc, r1, r2, y, z, c, n):
        self.net, self.tile, self.out, self.got, self.acc, self.c = net, tile, out, got, acc, c
        self.group, self.slots = net.group(), (net.slot(), net.slot())

        def dev(y, z, c):
            return (wide_of(y, z, c), n)

        self.other = dev(y, z, 1 - c)

        def cols(ref, start, h):
            return ref.at[pl.ds(aligned(start, 16), 16), pl.ds(h * 1024, 1024)]

        def ring(me, device, part, ref, base):
            return Scatter(
                net, self.group, me, device, part,
                ref.at[pl.ds(base, 16)], (cols(ref, base, 0), cols(ref, base, 1)),
                ref.at[pl.ds(base + 16, 32)], lambda h: cols(ref, base + 16, h), lambda h: cols(ref, base + 32, h),
            )

        def first(base, one, two, device, k):
            return {
                j: ring(two, device, lambda i, h, j=j: cols(acc, base + i * 64 + (one + j) % 4 * 16, h), r1.at[k], j * 48)
                for j in (2, 1, 3, 0)
            }

        def second(base, one, two, device, k):
            return Direct(
                net, self.group, one, device,
                lambda i: acc.at[pl.ds(aligned(base + two * 64 + i * 16, 16), 16)], r2, k * 48,
            )

        def along_y(i):
            return dev(i, z, c)

        def along_z(i):
            return dev(y, i, c)

        self.one = (first(0, y, z, along_z, 0), first(256, z, y, along_y, 1))
        self.two = (second(0, y, z, along_y, 0), second(256, z, y, along_z, 1))

    def exchange(self):
        for p in range(2):
            mine = pl.ds(p * 256, 256)
            for i in range(4):
                cs = slice(i * COLS, (i + 1) * COLS)
                self.out[mine, cs] = self.tile(aligned(p * 512 + (1 - self.c) * 256, 256), cs).astype(BF16)
            self.net.copy(self.out.at[mine], self.got.at[mine], self.other, self.group, self.slots[p])

    def start(self):
        for p in range(2):
            mine = pl.ds(p * 256, 256)
            self.net.arrived(self.got.at[mine], self.slots[p])
            for i in range(4):
                cs = slice(i * COLS, (i + 1) * COLS)
                term = self.tile(aligned(p * 512 + self.c * 256, 256), cs)
                self.acc[mine, cs] = (term + self.got[mine, cs].astype(F32)).astype(BF16)
            for j in (2, 1, 3, 0):
                self.one[p][j].start_far()
            for j in (2, 1, 3, 0):
                self.one[p][j].start_right()
                self.one[p][j].start_left()

    def step(self, j):
        for x in self.one:
            x[j].step()

    def hand_on(self, j, also=None):
        for p, (x, t) in enumerate(zip(self.one, self.two)):
            r = x[j]
            r.finish()
            for h in range(2):
                v = r.half(h)
                r.part(r.me, h)[...] = v.astype(BF16)
                if also is not None:
                    also(p, (t.me + j) % 4, slice(h * 1024, (h + 1) * 1024), v)
            if j:
                t.send(j)

    def finish(self):
        for r in self.two:
            r.finish()

    def result(self, i, cs):
        return self.two[i].result(cs)

    def drain(self, ref):
        self.net.sent(ref.at[pl.ds(0, 992)], self.group)


def other_chips(y, z, c):
    for d in range(1, 16):
        yield wide_of((y + d // 4) % 4, (z + d % 4) % 4, c)


def greet(y, z, c, n):
    peers = [(wide_of((y + d) % 4, z, c), n) for d in (1, 3, 2)]
    peers += [(wide_of(y, (z + d) % 4, c), n) for d in (1, 3, 2)]
    peers += [(wide_of(y, z, 1 - c), n)]
    peers += [(wide_of(y, z, c), (n + d) % 4) for d in (1, 3, 2)]
    barrier = pltpu.get_barrier_semaphore()
    for p in peers:
        pl.semaphore_signal(barrier, inc=1, device_id=p, device_id_type=MESH)
    return lambda: pl.semaphore_wait(barrier, len(peers))


def repeat(count, step, body):
    def turn(i, _):
        for j in range(step):
            body(i * step + j)
        return 0

    lax.fori_loop(0, count // step, turn, 0)


def nt(a, b):
    return lax.dot_general(a, b, (((1,), (1,)), ((), ())), preferred_element_type=F32)


GELU_A = float(np.sqrt(2.0 / np.pi))
GELU_B = 0.044715


def dot(a, b):
    return jnp.dot(a, b, preferred_element_type=F32)


def lanes(shape):
    return lax.broadcasted_iota(jnp.int32, shape, len(shape) - 1)


def swap(x):
    return jnp.where(lanes(x.shape) < ROT // 2, pltpu.roll(x, 128 - ROT // 2, 1), pltpu.roll(x, ROT // 2, 1))


def block_kernel(
    dealing, lengths, i_tok, i_cot, i_wq, i_wk, i_wv, i_wu, i_wo, i_wd,
    i_gain, i_bias, i_bq, i_bk, i_bv, i_bo, i_bu, i_bd, cos_all, sin_all,
    o_res, o_ig, o_gain, o_bias, o_q, o_bq, o_k, o_bk, o_v, o_bv, o_o, o_bo, o_u, o_bu, o_f,
    tok, cot, wu, v_gain, v_bias, b_q, b_k, b_v, b_o, b_u, b_d,
    res, ig, grad_l, grad_u, grad_f, v_512, v_64, v_256,
    ln, g, w, wm, wmo, xs, gbs, xhat, cosine, sine, cosine_held, sine_held, slope, hb, dpre, kv, kk, xq, xd, od, dkvt, dkv, dkvp,
    rdkv, sum_f, sum_u, sum_l, r_f, r_u, r_l, out_1, got_1, acc_1, r1_1, r2_1, out_2, got_2, acc_2, r1_2, r2_2,
    trans, hidden, cmask, bsend, bfin, csend, clow, cfin, ssend, srecv, brecv, wrecv, nsum, hats, column, bias, index, there, kpos, send, recv, local, inward,
):
    y, z, c, n = coords()
    net = Net(send, recv, (wide_of(y, z, 1 - c), n))
    my_cols = pl.ds(aligned(n * COLS, COLS), COLS)
    me = wide_of(y, z, c)
    own_a, own_b = slot_a(c, z, y), slot_b(c, y, z)

    def to(m):
        return (me, m)

    def w_cols(i):
        return pl.ds(aligned(i * COLS, COLS), COLS)

    def share(i):
        return pl.ds(aligned(i * PART, PART), PART)

    loads = []

    def load(x, to):
        loads.append(pltpu.make_async_copy(x, to, inward.at[len(loads)]))
        loads[-1].start()

    load(i_tok, tok)
    load(i_wk, w.at[pl.ds(256, 64), my_cols])
    load(i_wv, w.at[pl.ds(320, 64), my_cols])
    load(i_wq, w.at[pl.ds(384, 64), my_cols])
    load(i_cot, cot)
    load(i_wu, wu)
    load(i_wo, wm.at[pl.ds(256, 64), my_cols])
    load(i_gain, v_gain)
    load(i_bias, v_bias)
    early = len(loads)
    load(i_wd, wm.at[pl.ds(0, 256), my_cols])
    for x, at in ((i_bq, b_q), (i_bk, b_k), (i_bv, b_v), (i_bo, b_o), (i_bu, b_u), (i_bd, b_d)):
        load(x, at)
    load(cos_all.at[n], cosine)
    load(sin_all.at[n], sine)
    all_greeted = greet(y, z, c, n)
    for x in loads[:early]:
        x.wait()
    w[0:256, my_cols] = wu[...].T
    for i in range(4):
        gbs[n, i : i + 1, :] = v_gain[:, i * 128 : i * 128 + 128]
        gbs[n, 4 + i : 5 + i, :] = v_bias[:, i * 128 : i * 128 + 128]
    xs[:, my_cols] = tok[share(n), :]
    row = lax.broadcasted_iota(jnp.int32, (BLOCK, COLS), 0)
    block = dealing[me]
    valid = block % (MAXLEN // BLOCK) * BLOCK + row < jnp.where(block < MAXLEN // BLOCK, lengths[0], lengths[1])
    cmask[...] = jnp.where(valid, cot[...], jnp.zeros_like(cot))
    mine = cmask[share(n), :]
    g[pl.ds(own_a, 16), my_cols] = mine[0:16]
    g[pl.ds(own_b, 16), my_cols] = mine[16:32]
    all_greeted()

    rings, turns = net.group(), net.group()
    tokens_in, gains_in, cot_in = net.slot(), net.slot(), net.slot()
    gains_out = net.group()
    for j in (1, 3, 2):
        m = (n + j) % 4
        net.copy(tok.at[share(m)], xs.at[:, my_cols], to(m), turns, tokens_in)
        net.copy(gbs.at[n], gbs.at[n], to(m), gains_out, gains_in)

    def x_ring(ref, start, count):
        half = count // 2
        return Ring(
            net, rings, n, to,
            lambda i: ref.at[pl.ds(start, count), w_cols(i)],
            lambda i, h: ref.at[pl.ds(start + h * half, half), w_cols(i)],
        )

    a_ring = x_ring(w, 256, 192)
    u_ring = x_ring(w, 0, 256)
    d_ring = x_ring(wm, 0, 256)
    o_ring = x_ring(wm, 256, 64)
    kv_ring = [
        Ring(
            net, rings, n, to,
            lambda i, s=s: kv.at[i, pl.ds(s * 32, 32)],
            lambda i, h, s=s: kv.at[i, pl.ds(s * 32 + h * 16, 16)],
        )
        for s in range(2)
    ]
    a_ring.start()
    for j in (1, 3, 2):
        m = (n + j) % 4
        for p, start in enumerate((own_a, own_b)):
            x = cmask.at[pl.ds(aligned(m * PART + p * 16, 16), 16)]
            net.copy(x, g.at[pl.ds(start, 16), my_cols], to(m), turns, cot_in)
    u_ring.start()
    o_ring.start()

    for x in loads[early:]:
        x.wait()
    at = lanes((8, 128))
    part = lax.broadcasted_iota(jnp.int32, (8, 128), 0)
    found = jnp.zeros((8, 128), jnp.int32)
    for b in range(NBLK):
        sy, sz, sc = b // 8, b // 2 % 4, b % 2
        found = jnp.where((part < 2) & (at == dealing[b]), jnp.where(part == 0, (sc * 4 + sz) * 4 + sy, 32 + (sc * 4 + sy) * 4 + sz), found)
        found = jnp.where((part == 2) & (at == (sc * 4 + sz) * 4 + sy), 2 * dealing[b], found)
        found = jnp.where((part == 2) & (at == 32 + (sc * 4 + sy) * 4 + sz), 2 * dealing[b] + 1, found)
        found = jnp.where((part == 3) & (at == (sc * 4 + sz) * 4 + sy), 2 * dealing[b] % 32, found)
        found = jnp.where((part == 3) & (at == 32 + (sc * 4 + sy) * 4 + sz), 2 * dealing[b] % 32 + 1, found)
    index[...] = found
    to_scalars = pltpu.make_async_copy(index, there, local.at[0])
    to_scalars.start()
    half = ROT // 2
    bias[:, 0:128] = b_u[0:1, :].astype(F32)
    bias[:, 128:256] = b_u[1:2, :].astype(F32)
    bias[:, 256:320] = b_k[...].astype(F32)
    bias[:, 320:384] = b_v[...].astype(F32)
    bias[:, 384:448] = b_q[...].astype(F32)
    bias[:, 448:464] = b_q[:, half:ROT].astype(F32)
    bias[:, 464:480] = b_q[:, 0:half].astype(F32)
    bias[:, 480:496] = b_k[:, half:ROT].astype(F32)
    bias[:, 496:512] = b_k[:, 0:half].astype(F32)
    for s in range(2):
        at = lanes((8, MAXLEN))
        kpos[s] = jnp.where(at < lengths[s], at, 1 << 20)
    wmo[0:64, :] = jnp.zeros((64, D), BF16)

    net.arrived(dpre.at[pl.ds(0, 96)], tokens_in)
    x = xs[...].astype(F32)
    mean = jnp.sum(x, 1, keepdims=True) / D
    var = jnp.sum(x * x, 1, keepdims=True) / D - mean * mean
    inv = lax.rsqrt(var + EPS)
    xhat[...] = (x - mean) * inv
    net.arrived(srecv.at[pl.ds(0, 3)], gains_in)
    for i in range(16):
        cs = slice(i * 128, (i + 1) * 128)
        low = (xhat[:, cs] * gbs[i // 4, i % 4 : i % 4 + 1, :] + gbs[i // 4, i % 4 + 4 : i % 4 + 5, :]).astype(BF16)
        ln[pl.ds(own_a, 16), cs] = low[0:16]
        ln[pl.ds(own_b, 16), cs] = low[16:32]

    lg = WideGather(net, ln, y, z, c, n)
    gg = WideGather(net, g, y, z, c, n)
    lg.start()
    to_scalars.wait()

    def hold(i):
        cosine_held[i] = cosine[there[3, i]]
        sine_held[i] = sine[there[3, i]]

    repeat(64, 8, hold)
    lg.near_one()
    a_ring.forward()
    d_ring.start()
    net.arrived(dpre.at[pl.ds(0, 96)], cot_in)
    lg.near_two(0)
    lg.far_one()
    gg.start()
    lg.near_two(3)
    lg.near_two(1)
    lg.near_two(2)
    lg.cross_near()
    gg.near_one()
    u_ring.forward()
    o_ring.forward()
    for j in (0, 3, 1, 2):
        lg.far_two(j)
    a_ring.finish()
    gg.near_two(0)
    gg.far_one()

    w[448:640, :] = w[256:448, :]
    w[640:656, :] = w[400:416, :]
    w[656:672, :] = w[384:400, :]
    w[672:688, :] = w[272:288, :]
    w[688:704, :] = w[256:272, :]

    lg.finish()
    x = (nt(ln[...], w[448:704, :]) + bias[:, 256:512]).reshape(64, 16, 256)
    a, b = x[:, :, 0:128], x[:, :, 128:256]
    kv[n] = (a * cosine_held[...] + pltpu.roll(b, 32, 2) * sine_held[...]).astype(BF16)
    kv_ring[0].start()
    kv_ring[1].start()
    x = (b * cosine_held[...] + pltpu.roll(b, 64, 2) * sine_held[...]) * (HEAD_DIM**-0.5)
    xq[...] = jnp.where(lanes((64, 16, 128)) < HEAD_DIM, x, 0.0).astype(BF16)
    gg.near_two(3)
    gg.near_two(1)
    gg.near_two(2)
    gg.cross_near()
    u_ring.finish()

    def units(i, _):
        r = pl.ds(aligned(i * 512, 512), 512)
        v = nt(ln[r, :], w[0:256, :]) + bias[:, 0:256]
        t = jnp.tanh(GELU_A * (v + GELU_B * (v * v * v)))
        hb[r, :] = (0.5 * v * (1.0 + t)).astype(BF16)
        slope[r, :] = 0.5 * (1.0 + t) + 0.5 * v * (1.0 - t * t) * (GELU_A * (1.0 + 3.0 * GELU_B * (v * v)))
        return 0

    lax.fori_loop(0, 2, units, 0)
    hidden[0:256, :] = hb[...].T
    hidden[256:288, :] = jnp.ones((32, ROWS), BF16)
    def scatter_cols(buf, count, r):
        half = count // 2
        return Scatter(
            net, net.group(), n, to,
            lambda i, h: buf.at[pl.ds(h * half, half), w_cols(i)],
            r.at[0], (r.at[0, pl.ds(0, half)], r.at[0, pl.ds(half, half)]),
            r.at[pl.ds(1, 2)], lambda h: r.at[1, pl.ds(h * half, half)], lambda h: r.at[2, pl.ds(h * half, half)],
        )

    f_sum = scatter_cols(sum_f, 288, r_f)
    u_sum = scatter_cols(sum_u, 256, r_u)
    l_sum = scatter_cols(sum_l, 256, r_l)

    def weight_f(i, _):
        cs = pl.ds(aligned(i * 1024, 1024), 1024)
        sum_f[:, cs] = dot(hidden[...], g[:, cs]).astype(BF16)
        return 0

    kv_ring[0].forward()
    o_ring.finish()
    wmo[64:128, :] = wm[256:320, :]
    for j in (0, 3, 1, 2):
        gg.far_two(j)
    kv_ring[1].forward()
    d_ring.forward()

    gg.finish()
    hats_out, hats_in = net.group(), net.slot()
    hats[y] = xhat[0:16, :]
    hats[4 + z] = xhat[16:32, :]
    for d in (1, 3, 2):
        net.copy(xhat.at[pl.ds(0, 16)], hats.at[y], (wide_of((y + d) % 4, z, c), n), hats_out, hats_in)
        net.copy(xhat.at[pl.ds(16, 16)], hats.at[4 + z], (wide_of(y, (z + d) % 4, c), n), hats_out, hats_in)
    lax.fori_loop(0, 2, weight_f, 0)

    def grad_o(i, _):
        r = pl.ds(aligned(i * 512, 512), 512)
        xd[pl.ds(i * 32, 32)] = nt(g[r, :], wmo[...]).astype(BF16).reshape(32, 16, 128)
        return 0

    lax.fori_loop(0, 2, grad_o, 0)

    def gather_keys(i):
        for m in range(4):
            for p in range(2):
                kk[pl.ds(aligned(i * BLOCK + m * PART + p * 16, 16), 16), :] = kv[m, there[p, i]]

    def attend(s, t):
        keys = 512 * (t + 1)
        held = [there[k % 2, s * 16 + t * 4 + k // 2] for k in range(8)]
        x = jnp.concatenate([xq[i] for i in held] + [xd[i] for i in held], 0)
        near = kk[pl.ds(s * MAXLEN, keys), :]
        both = nt(x, near)
        i = lax.broadcasted_iota(jnp.int32, (128, 1), 0)
        qpos = (4 * t + i // PART) * BLOCK + n * PART + i % PART
        scores = jnp.where(kpos[s, 0:1, 0:keys] <= qpos, both[0:128], -1e30)
        e = jnp.exp(scores - jnp.max(scores, 1, keepdims=True))
        p = e * (1.0 / jnp.sum(e, 1, keepdims=True))
        dp = both[128:256]
        ds = p * (dp - jnp.sum(p * dp, 1, keepdims=True))
        yy = jnp.concatenate([ds.astype(BF16), p.astype(BF16)], 0)
        back = dot(yy, near)
        back = jnp.where(lanes((128, 128)) < HEAD_DIM, back[0:128] * (HEAD_DIM**-0.5), back[128:256])
        od[pl.ds(s * 32 + t * 8, 8)] = back.reshape(8, 16, 128)
        grads = dot(x.T, yy)
        if t == 3:
            dkvt[s, :, 0:keys] = grads
        else:
            dkvt[s, :, 0:keys] += grads

    keys_out = net.group()

    def key_sum(s, part):
        def rows(start, count):
            return pl.ds(s * 512 + part * 256 + start, count)

        return Scatter(
            net, keys_out, n, to,
            lambda i, h: dkv.at[i, rows(h * 128, 128)],
            rdkv.at[0, rows(0, 256)], (rdkv.at[0, rows(0, 128)], rdkv.at[0, rows(128, 128)]),
            rdkv.at[pl.ds(1, 2), rows(0, 256)],
            lambda h: rdkv.at[1, rows(h * 128, 128)],
            lambda h: rdkv.at[2, rows(h * 128, 128)],
        )

    def turn_keys(s, h):
        for i in range(8 * h, 8 * h + 8):
            t = dkvt[s, :, i * BLOCK : (i + 1) * BLOCK].T.astype(BF16)
            for m in range(4):
                dkv[m, s * 512 + i * PART : s * 512 + (i + 1) * PART, :] = t[m * PART : (m + 1) * PART]

    kv_sum = [key_sum(0, 1), key_sum(0, 0), key_sum(1, 1), key_sum(1, 0)]
    kv_ring[0].finish()
    kv_ring[1].finish()
    f_sum.start()
    repeat(32, 4, gather_keys)
    attend(0, 3)
    attend(0, 2)
    turn_keys(0, 1)
    kv_sum[0].start()
    attend(0, 1)
    attend(0, 0)
    turn_keys(0, 0)
    kv_sum[1].start()
    attend(1, 3)
    attend(1, 2)
    turn_keys(1, 1)
    kv_sum[2].start()
    attend(1, 1)
    attend(1, 0)
    turn_keys(1, 0)
    kv_sum[3].start()

    def unrope(s):
        x = od[pl.ds(s * 32, 32)].reshape(512, 128)
        od[pl.ds(s * 32, 32)] = (x * cosine[...].reshape(512, 128) - swap(x) * sine[...].reshape(512, 128)).reshape(32, 16, 128)

    unrope(0)
    unrope(1)

    def place(i):
        dpre[pl.ds(aligned(i * 16, 16), 16), 384:512] = od[there[2, i]].astype(BF16)

    repeat(64, 8, place)

    def dln_tile(start, cs):
        r = pl.ds(start, 256)
        return dot(dpre[r, 0:448], w[0:448, cs])

    def branch_tile(start, cs):
        r = pl.ds(start, 256)
        return dot(hb[r, :], wm[0:256, cs]) + dot(dpre[r, 384:512], wmo[:, cs])

    branch = WideScatter(net, branch_tile, out_1, got_1, acc_1, r1_1, r2_1, y, z, c, n)
    dln = WideScatter(net, dln_tile, out_2, got_2, acc_2, r1_2, r2_2, y, z, c, n)
    d_ring.finish()
    branch.exchange()
    kv_sum[0].step()
    kv_sum[1].step()

    def grad_units(i, _):
        r = pl.ds(aligned(i * 512, 512), 512)
        dpre[r, 0:256] = (nt(g[r, :], wm[0:256, :]) * slope[r, :]).astype(BF16)
        return 0

    lax.fori_loop(0, 2, grad_units, 0)

    kv_sum[2].step()
    kv_sum[3].step()
    branch.start()
    trans[...] = dpre[:, 0:256].T

    def weight_u(i, _):
        cs = pl.ds(aligned(i * 1024, 1024), 1024)
        sum_u[:, cs] = dot(trans[...], ln[:, cs]).astype(BF16)
        return 0

    lax.fori_loop(0, 2, weight_u, 0)
    u_sum.start()
    def unrope_keys(s):
        r = pl.ds(s * 512, 512)
        x = dkv[n, r, :].astype(F32) + (rdkv[1, r, :].astype(F32) + rdkv[2, r, :].astype(F32))
        dkvp[pl.ds(s * 32, 32)] = (x * cosine[...].reshape(512, 128) - swap(x) * sine[...].reshape(512, 128)).reshape(32, 16, 128)

    kv_sum[0].finish()
    kv_sum[1].finish()
    unrope_keys(0)
    kv_sum[2].finish()
    kv_sum[3].finish()
    unrope_keys(1)

    def place_keys(i):
        dpre[pl.ds(aligned(i * 16, 16), 16), 256:384] = dkvp[there[2, i]].astype(BF16)

    repeat(64, 8, place_keys)
    dln.exchange()
    for j in (2, 1, 3, 0):
        branch.step(j)
    trans[...] = dpre[:, 256:512].T

    def weight_l(i, _):
        cs = pl.ds(aligned(i * 1024, 1024), 1024)
        sum_l[0:192, cs] = dot(trans[0:192, :], ln[:, cs]).astype(BF16)
        sum_l[192:256, cs] = dot(trans[192:256, :], g[:, cs]).astype(BF16)
        return 0

    lax.fori_loop(0, 2, weight_l, 0)
    l_sum.start()
    dln.start()
    f_sum.step()
    for j in (2, 1, 3, 0):
        dln.step(j)
    for j in (2, 1, 3, 0):
        branch.hand_on(j)
    u_sum.step()

    def norm_sums(p, i, cs, v):
        column[0:1, cs] += jnp.sum(v * hats[4 * p + i, :, cs], 0, keepdims=True)
        column[1:2, cs] += jnp.sum(v, 0, keepdims=True)

    column[...] = jnp.zeros((8, D), F32)
    net.arrived(hats.at[pl.ds(0, 6)], hats_in)
    for j in (2, 1, 3, 0):
        dln.hand_on(j, norm_sums)
    norm_out, norm_in, final_out, final_in, all_out, all_in = net.group(), net.slot(), net.group(), net.slot(), net.group(), net.slot()
    for m in range(4):
        for k in range(2):
            for i in range(4):
                ssend[m, 4 * k + i : 4 * k + i + 1, :] = column[k : k + 1, m * COLS + i * 128 : m * COLS + i * 128 + 128]
    chip = y * 4 + z
    wrecv[chip] = ssend[...]
    for p in other_chips(y, z, c):
        net.copy(ssend, wrecv.at[chip], (p, n), norm_out, norm_in)
    sums = jnp.sum(dpre[...].astype(F32), 0, keepdims=True)
    for i in range(4):
        brecv[n, i : i + 1, :] = sums[:, i * 128 : i * 128 + 128]
    small_out, small_in, branch_out, branch_in = net.group(), net.slot(), net.group(), net.slot()
    for j in (1, 3, 2):
        net.copy(brecv.at[n], brecv.at[n], to((n + j) % 4), small_out, small_in)
    l_sum.step()
    branch.finish()
    for i in range(2):
        for h in range(2):
            cs = slice(h * 1024, (h + 1) * 1024)
            bsend[i * 16 : (i + 1) * 16, cs] = branch.result(i, cs).astype(BF16)
    bfin[share(n), :] = bsend[:, my_cols]
    for j in (1, 3, 2):
        m = (n + j) % 4
        net.copy(bsend.at[:, w_cols(m)], bfin.at[share(n)], to(m), branch_out, branch_in)
    dln.finish()

    for i in range(2):
        for h in range(2):
            cs = slice(h * 1024, (h + 1) * 1024)
            csend[i * 16 : (i + 1) * 16, cs] = dln.result(i, cs)
    for i in range(16):
        cs = slice(i * 128, (i + 1) * 128)
        csend[:, cs] = csend[:, cs] * gbs[i // 4, i % 4 : i % 4 + 1, :]
    grad = csend[...]
    first = jnp.sum(grad, 1, keepdims=True) / D
    second = jnp.sum(grad * xhat[...], 1, keepdims=True) / D
    x = xs[...].astype(F32)
    mean = jnp.sum(x, 1, keepdims=True) / D
    var = jnp.sum(x * x, 1, keepdims=True) / D - mean * mean
    clow[...] = (lax.rsqrt(var + EPS) * (grad - first - xhat[...] * second)).astype(BF16)
    cfin[share(n), :] = clow[:, my_cols]
    for j in (1, 3, 2):
        m = (n + j) % 4
        net.copy(clow.at[:, w_cols(m)], cfin.at[share(n)], to(m), final_out, final_in)
    net.arrived(wrecv.at[pl.ds(0, 15)], norm_in)
    nsum[...] = jnp.sum(wrecv[...], 0)
    srecv[n * 2 + c] = nsum[n]
    for j in (1, 3, 2, 0):
        m = (n + j) % 4
        for d in (0, 1) if j else (1,):
            net.copy(nsum.at[m], srecv.at[n * 2 + c], (wide_of(y, z, (c + d) % 2), m), all_out, all_in)
    outs = []

    def give(x, to):
        outs.append(pltpu.make_async_copy(x, to, local.at[1 + len(outs)]))
        outs[-1].start()

    f_sum.finish()
    for h in range(2):
        grad_f[h * 144 : (h + 1) * 144, :] = f_sum.half(h)
    v_512[2] = grad_f[256:257, :]
    give(grad_f.at[pl.ds(0, 256)], o_f)
    give(v_512.at[2], o_bo)
    u_sum.finish()
    for h in range(2):
        grad_u[:, h * 128 : (h + 1) * 128] = u_sum.half(h).T
    give(grad_u, o_u)
    l_sum.finish()
    for h in range(2):
        grad_l[h * 128 : (h + 1) * 128, :] = l_sum.half(h)
    for i, x in enumerate((o_k, o_v, o_q, o_o)):
        give(grad_l.at[pl.ds(64 * i, 64)], x)
    net.arrived(dpre.at[pl.ds(0, 96)], branch_in)
    block = dealing[me]
    valid = block % (MAXLEN // BLOCK) * BLOCK + row < jnp.where(block < MAXLEN // BLOCK, lengths[0], lengths[1])
    valid = valid[:, 0:128]
    for i in range(4):
        cs = slice(i * 128, i * 128 + 128)
        base = bfin[:, cs].astype(F32) + (b_o[i : i + 1, :].astype(F32) + b_d[i : i + 1, :].astype(F32))
        res[:, cs] = (tok[:, cs].astype(F32) + jnp.where(valid, base, 0.0)).astype(BF16)
    give(res, o_res)
    net.arrived(srecv.at[pl.ds(0, 3)], small_in)
    sums = (brecv[0] + brecv[1]) + (brecv[2] + brecv[3])
    v_256[:, 0:128] = sums[0:1]
    v_256[:, 128:256] = sums[1:2]
    v_64[0] = sums[2:3, 0:64]
    v_64[1] = sums[2:3, 64:128]
    v_64[2] = sums[3:4, 0:64]
    give(v_256, o_bu)
    for i, x in enumerate((o_bk, o_bv, o_bq)):
        give(v_64.at[i], x)
    net.arrived(cfin.at[pl.ds(0, 96)], final_in)
    ig[...] = cot[...].astype(F32) + cfin[...].astype(F32)
    give(ig, o_ig)
    net.arrived(srecv.at[pl.ds(0, 7)], all_in)
    sums = jnp.sum(srecv[...], 0)
    for i in range(4):
        v_512[0, :, i * 128 : i * 128 + 128] = sums[i : i + 1]
        v_512[1, :, i * 128 : i * 128 + 128] = sums[4 + i : 5 + i]
    give(v_512.at[0], o_gain)
    give(v_512.at[1], o_bias)

    lg.drain()
    gg.drain()
    branch.drain(ln)
    dln.drain(ln)
    net.sent(ln.at[pl.ds(0, 768)], rings)
    net.sent(ln.at[pl.ds(0, 192)], keys_out)
    net.sent(dpre.at[pl.ds(0, 864)], f_sum.group)
    net.sent(dpre.at[pl.ds(0, 768)], u_sum.group)
    net.sent(dpre.at[pl.ds(0, 768)], l_sum.group)
    net.sent(dpre.at[pl.ds(0, 192)], turns)
    net.sent(srecv.at[pl.ds(0, 3)], gains_out)
    net.sent(srecv.at[pl.ds(0, 3)], small_out)
    net.sent(dpre.at[pl.ds(0, 96)], branch_out)
    net.sent(wrecv.at[pl.ds(0, 15)], norm_out)
    net.sent(cfin.at[pl.ds(0, 96)], final_out)
    net.sent(srecv.at[pl.ds(0, 7)], all_out)
    net.sent(hats.at[pl.ds(0, 6)], hats_out)
    for x in outs:
        x.wait()
    assert (net.groups, net.slots) == (SENDS, ARRIVALS), (net.groups, net.slots)


RESULTS = (
    (BLOCK, COLS), (1, COLS), (1, COLS), (64, COLS), (1, 64), (64, COLS), (1, 64), (64, COLS), (1, 64), (64, COLS), (1, COLS),
    (COLS, UNITS), (1, UNITS), (UNITS, COLS),
)


def call_block(*args):
    anywhere = pl.BlockSpec(memory_space=pl.ANY)
    shape = jax.ShapeDtypeStruct

    def buf(dtype, *size):
        return pltpu.VMEM(size, dtype)

    wide = [buf(BF16, 512, D), buf(BF16, 512, D), buf(BF16, 512, D), buf(BF16, 2, 192, D), buf(BF16, 96, D)]
    return pl.pallas_call(
        block_kernel,
        out_shape=(shape((BLOCK, COLS), BF16), *(shape(x, F32) for x in RESULTS)),
        in_specs=[pl.BlockSpec(memory_space=pltpu.SMEM)] * 2 + [anywhere] * 18,
        out_specs=(anywhere,) * 15,
        scratch_shapes=[
            buf(BF16, BLOCK, COLS),
            buf(BF16, BLOCK, COLS),
            buf(BF16, COLS, UNITS),
            buf(F32, 1, COLS),
            buf(F32, 1, COLS),
            buf(BF16, 1, 64),
            buf(BF16, 1, 64),
            buf(BF16, 1, 64),
            buf(BF16, 4, 128),
            buf(BF16, 2, 128),
            buf(BF16, 4, 128),
            buf(BF16, BLOCK, COLS),
            buf(F32, BLOCK, COLS),
            buf(F32, 256, COLS),
            buf(F32, COLS, UNITS),
            buf(F32, 288, COLS),
            buf(F32, 3, 1, COLS),
            buf(F32, 3, 1, 64),
            buf(F32, 1, UNITS),
            buf(BF16, ROWS, D),
            buf(BF16, ROWS, D),
            buf(BF16, 704, D),
            buf(BF16, 320, D),
            buf(BF16, 128, D),
            buf(BF16, PART, D),
            buf(F32, 4, 8, 128),
            buf(F32, PART, D),
            buf(F32, 32, 16, 128),
            buf(F32, 32, 16, 128),
            buf(F32, 64, 16, 128),
            buf(F32, 64, 16, 128),
            buf(F32, ROWS, UNITS),
            buf(BF16, ROWS, UNITS),
            buf(BF16, ROWS, 512),
            buf(BF16, 4, 64, 16, 128),
            buf(BF16, 2 * MAXLEN, 128),
            buf(BF16, 64, 16, 128),
            buf(BF16, 64, 16, 128),
            buf(F32, 64, 16, 128),
            buf(F32, 2, 128, MAXLEN),
            buf(BF16, 4, ROWS, 128),
            buf(F32, 64, 16, 128),
            buf(BF16, 3, ROWS, 128),
            buf(BF16, 288, D),
            buf(BF16, 256, D),
            buf(BF16, 256, D),
            buf(BF16, 3, 288, COLS),
            buf(BF16, 3, 256, COLS),
            buf(BF16, 3, 256, COLS),
            *wide,
            *wide,
            buf(BF16, 256, ROWS),
            buf(BF16, 288, ROWS),
            buf(BF16, BLOCK, COLS),
            buf(BF16, PART, D),
            buf(BF16, BLOCK, COLS),
            buf(F32, PART, D),
            buf(BF16, PART, D),
            buf(BF16, BLOCK, COLS),
            buf(F32, 4, 8, 128),
            buf(F32, 8, 8, 128),
            buf(F32, 4, 8, 128),
            buf(F32, 16, 4, 8, 128),
            buf(F32, 4, 8, 128),
            buf(F32, 8, 16, D),
            buf(F32, 8, D),
            buf(F32, 1, COLS),
            buf(jnp.int32, 8, 128),
            pltpu.SMEM((8, 128), jnp.int32),
            buf(jnp.int32, 2, 8, MAXLEN),
            pltpu.SemaphoreType.DMA((SENDS,)),
            pltpu.SemaphoreType.DMA((ARRIVALS,)),
            pltpu.SemaphoreType.DMA((18,)),
            pltpu.SemaphoreType.DMA((18,)),
        ],
        compiler_params=pltpu.CompilerParams(collective_id=0, has_side_effects=True, vmem_limit_bytes=63 * 2**20),
    )(*args)


def relay_kernel(*refs):
    given, taken, held, here, there = refs[:15], refs[15:31], refs[31:46], refs[46], refs[47]
    order = sorted(range(15), key=lambda i: -given[i].size)
    come = [pltpu.make_async_copy(given[i], held[i], here.at[i]) for i in range(15)]
    go = [pltpu.make_async_copy(held[i], taken[i], there.at[i]) for i in range(15)]
    go.append(pltpu.make_async_copy(held[11], taken[15], there.at[15]))
    for i in order:
        come[i].start()
    for i in order:
        come[i].wait()
        go[i].start()
        if i == 11:
            go[15].start()
    for x in go:
        x.wait()


def relay(arrays):
    anywhere = pl.BlockSpec(memory_space=pl.ANY)
    return pl.pallas_call(
        relay_kernel,
        out_shape=tuple(jax.ShapeDtypeStruct(x.shape, x.dtype) for x in (*arrays, arrays[11])),
        in_specs=[anywhere] * 15,
        out_specs=(anywhere,) * 16,
        scratch_shapes=[pltpu.VMEM(x.shape, x.dtype) for x in arrays]
        + [pltpu.SemaphoreType.DMA((15,)), pltpu.SemaphoreType.DMA((16,))],
        compiler_params=pltpu.CompilerParams(vmem_limit_bytes=62 * 2**20),
    )(*arrays)


def on_device(
    tokens, ln_gain, ln_bias, w_query, b_query, w_key, b_key, w_value, b_value, w_out, b_out,
    w_fc1, b_fc1, w_fc2, b_fc2, cotangent, lengths, dealing,
):
    cosine, sine = (
        np.ascontiguousarray(t.reshape(MAXLEN // BLOCK, 4, PART, 128).transpose(1, 0, 2, 3)).reshape(4, -1, 16, 128)
        for t in rope_tables()
    )
    out = call_block(
        dealing, lengths, tokens, cotangent, w_query.T, w_key.T, w_value.T, w_fc1, w_out, w_fc2,
        ln_gain[None], ln_bias[None], b_query[None], b_key[None], b_value[None], b_out.reshape(-1, 128),
        b_fc1.reshape(-1, 128), b_fc2.reshape(-1, 128),
        jnp.asarray(cosine), jnp.asarray(sine),
    )
    out = list(relay(out))
    for i in (4, 6, 8):
        out[i] = out[i].T
    for i in (2, 3, 5, 7, 9, 11, 13, 15):
        out[i] = out[i][0]
    return tuple(out)


def solution(mesh):
    rows, col, units = P("wide", "narrow"), P("narrow"), P("wide")
    weight, out = P("narrow", "wide"), P("wide", "narrow")
    placed = (
        rows, col, col, weight, units, weight, units, weight, units, out, col, weight, units, out, col, rows, P(), P(),
    )
    given = (
        rows, rows, col, col, weight, units, weight, units, weight, units, out, col, weight, units, out, col,
    )
    return jax.shard_map(on_device, mesh=mesh, in_specs=placed, out_specs=given, check_vma=False)
```

```python
import jax
import jax.numpy as jnp
import numpy as np
from jax import lax
from jax.experimental import pallas as pl
from jax.experimental.pallas import tpu as pltpu
from jax.sharding import PartitionSpec as P

MESH = pl.DeviceIdType.MESH
D = 2048
HEAD_DIM = 64
ROT = 32
BLOCK = 128
MAXLEN = 2048
NBLK = 32
PART = 32
ROWS = NBLK * PART
COLS = 512
UNITS = 256
EPS = 1e-05
SENDS, ARRIVALS = 17, 143
BF16 = jnp.bfloat16
F32 = jnp.float32


def rope_tables():
    half = ROT // 2
    inverse = (10000.0 ** (-(np.arange(half, dtype=np.float32) * np.float32(2.0) / np.float32(ROT)))).astype(np.float32)
    angles = (np.arange(MAXLEN, dtype=np.float32)[:, None] * inverse[None, :]).astype(np.float64)
    cosine = np.ones((MAXLEN, 128), np.float32)
    sine = np.zeros((MAXLEN, 128), np.float32)
    cosine[:, :half] = np.cos(angles)
    cosine[:, half:ROT] = np.cos(angles)
    sine[:, :half] = -np.sin(angles)
    sine[:, half:ROT] = np.sin(angles)
    return cosine, sine


class Net:
    def __init__(self, send, recv, anyone):
        self.send, self.recv, self.anyone = send, recv, anyone
        self.groups = self.slots = 0

    def group(self):
        self.groups += 1
        return self.groups - 1

    def slot(self):
        self.slots += 1
        return self.slots - 1

    def make(self, src, dst, device, group, slot):
        return pltpu.make_async_remote_copy(
            src_ref=src,
            dst_ref=dst,
            send_sem=self.send.at[group],
            recv_sem=self.recv.at[slot],
            device_id=device,
            device_id_type=MESH,
        )

    def copy(self, src, dst, device, group, slot):
        self.make(src, dst, device, group, slot).start()

    def arrived(self, ref, slot):
        self.make(ref, ref, self.anyone, 0, slot).wait_recv()

    def sent(self, ref, group):
        self.make(ref, ref, self.anyone, group, 0).wait_send()


class Ring:
    def __init__(self, net, group, me, device, unit, half):
        self.net, self.group, self.unit, self.half = net, group, unit, half
        self.me, self.right, self.left = me, (me + 1) % 4, (me + 3) % 4
        self.to_right, self.to_left = device(self.right), device(self.left)
        self.a, self.b, self.c = net.slot(), net.slot(), net.slot()

    def send(self, x, device, slot):
        self.net.copy(x, x, device, self.group, slot)

    def start(self):
        own = self.unit(self.me)
        self.send(own, self.to_right, self.a)
        self.send(own, self.to_left, self.b)

    def forward(self):
        self.net.arrived(self.unit(self.left), self.a)
        self.send(self.half(self.left, 0), self.to_right, self.c)
        self.net.arrived(self.unit(self.right), self.b)
        self.send(self.half(self.right, 1), self.to_left, self.c)

    def finish(self):
        self.net.arrived(self.unit((self.me + 2) % 4), self.c)


def coords():
    w, n = lax.axis_index("wide"), lax.axis_index("narrow")
    return w // 8, (w // 2) % 4, w % 2, n


def wide_of(y, z, c):
    return (y * 4 + z) * 2 + c


def aligned(x, m):
    return pl.multiple_of(x, m)


def slot_a(c, z, y):
    return aligned(((c * 4 + z) * 4 + y) * 16, 16)


def slot_b(c, y, z):
    return aligned((32 + (c * 4 + y) * 4 + z) * 16, 16)


class Gather2:
    def __init__(self, net, group, one, two, first, second, block, half):
        self.net, self.group, self.block, self.half = net, group, block, half
        self.one, self.two = one, two
        self.first = [first((one + j) % 4) for j in range(4)]
        self.second = [second((two + j) % 4) for j in range(4)]
        self.a, self.b, self.c = net.slot(), net.slot(), net.slot()
        self.p, self.q, self.r = ([net.slot() for _ in range(4)] for _ in range(3))

    def at(self, j, k):
        return (self.one + j) % 4, (self.two + k) % 4

    def move(self, x, device, slot):
        self.net.copy(x, x, device, self.group, slot)

    def send(self, j):
        x = self.block(*self.at(j, 0))
        self.move(x, self.second[1], self.p[j])
        self.move(x, self.second[3], self.q[j])

    def start(self):
        x = self.block(*self.at(0, 0))
        self.move(x, self.first[1], self.a)
        self.move(x, self.first[3], self.b)
        self.move(x, self.first[2], self.c)
        self.send(0)

    def near_one(self):
        self.net.arrived(self.block(*self.at(3, 0)), self.a)
        self.send(3)
        self.net.arrived(self.block(*self.at(1, 0)), self.b)
        self.send(1)

    def far_one(self):
        self.net.arrived(self.block(*self.at(2, 0)), self.c)
        self.send(2)

    def near_two(self, j):
        self.net.arrived(self.block(*self.at(j, 3)), self.p[j])
        self.move(self.half(*self.at(j, 3), 0), self.second[1], self.r[j])
        self.net.arrived(self.block(*self.at(j, 1)), self.q[j])
        self.move(self.half(*self.at(j, 1), 1), self.second[3], self.r[j])

    def far_two(self, j):
        self.net.arrived(self.block(*self.at(j, 2)), self.r[j])


class WideGather:
    def __init__(self, net, buf, y, z, c, n):
        self.net, self.buf, self.c = net, buf, c
        self.group, self.slot = net.group(), net.slot()

        def dev(y, z, c):
            return (wide_of(y, z, c), n)

        def block(start):
            return buf.at[pl.ds(start, 16)]

        def half(start, h):
            return buf.at[pl.ds(start, 16), pl.ds(h * 1024, 1024)]

        self.other = dev(y, z, 1 - c)
        self.slots = (slot_a, slot_b)
        self.parts = (
            Gather2(
                net, self.group, y, z, lambda i: dev(i, z, c), lambda i: dev(y, i, c),
                lambda i, k: block(slot_a(c, k, i)), lambda i, k, h: half(slot_a(c, k, i), h),
            ),
            Gather2(
                net, self.group, z, y, lambda i: dev(y, i, c), lambda i: dev(i, z, c),
                lambda i, k: block(slot_b(c, k, i)), lambda i, k, h: half(slot_b(c, k, i), h),
            ),
        )

    def cross(self, k):
        for part, slot in zip(self.parts, self.slots):
            x = self.buf.at[pl.ds(slot(self.c, (part.two + k) % 4, 0), 64)]
            self.net.copy(x, x, self.other, self.group, self.slot)

    def start(self):
        for x in self.parts:
            x.start()

    def near_one(self):
        for x in self.parts:
            x.near_one()

    def far_one(self):
        for x in self.parts:
            x.far_one()
        self.cross(0)

    def near_two(self, j):
        for x in self.parts:
            x.near_two(j)

    def cross_near(self):
        self.cross(3)
        self.cross(1)

    def far_two(self, j):
        for x in self.parts:
            x.far_two(j)
            b = x.block(*x.at(j, 2))
            self.net.copy(b, b, self.other, self.group, self.slot)

    def finish(self):
        self.net.arrived(self.buf.at[pl.ds(0, 512)], self.slot)

    def drain(self):
        self.net.sent(self.buf.at[pl.ds(0, 992)], self.group)


class Scatter:
    def __init__(self, net, group, me, device, part, passed, rh, got, rl, rr):
        self.net, self.group, self.part = net, group, part
        self.passed, self.rh, self.got, self.rl, self.rr = passed, rh, got, rl, rr
        self.me, self.right, self.left = me, (me + 1) % 4, (me + 3) % 4
        self.to_right, self.to_left = device(self.right), device(self.left)
        self.s, self.a = net.slot(), net.slot()

    def move(self, x, to, device, slot):
        self.net.copy(x, to, device, self.group, slot)

    def start(self):
        self.start_far()
        self.start_right()
        self.start_left()

    def start_far(self):
        far = (self.me + 2) % 4
        self.move(self.part(far, 0), self.rh[0], self.to_right, self.s)
        self.move(self.part(far, 1), self.rh[1], self.to_left, self.s)

    def start_right(self):
        self.move(self.part(self.right, 1), self.rl(1), self.to_right, self.a)

    def start_left(self):
        self.move(self.part(self.left, 0), self.rr(0), self.to_left, self.a)

    def step(self):
        self.net.arrived(self.passed, self.s)
        p = self.part(self.right, 0)
        p[...] = (p[...].astype(F32) + self.rh[0][...].astype(F32)).astype(BF16)
        self.move(p, self.rl(0), self.to_right, self.a)
        p = self.part(self.left, 1)
        p[...] = (p[...].astype(F32) + self.rh[1][...].astype(F32)).astype(BF16)
        self.move(p, self.rr(1), self.to_left, self.a)

    def finish(self):
        self.net.arrived(self.got, self.a)

    def half(self, h):
        return self.part(self.me, h)[...].astype(F32) + (self.rl(h)[...].astype(F32) + self.rr(h)[...].astype(F32))


class Direct:
    def __init__(self, net, group, me, device, part, got, base):
        self.net, self.group, self.me, self.part = net, group, me, part
        self.device, self.got, self.base, self.slot = device, got, base, net.slot()

    def send(self, j):
        i = (self.me + j) % 4
        x = self.part(i)
        self.net.copy(x, self.got.at[pl.ds(self.base + 16 * (j - 1), 16)], self.device(i), self.group, self.slot)

    def finish(self):
        self.net.arrived(self.got.at[pl.ds(self.base, 48)], self.slot)

    def result(self, cs):
        total = self.part(self.me)[:, cs].astype(F32)
        for j in range(3):
            total += self.got[self.base + 16 * j : self.base + 16 * j + 16, cs].astype(F32)
        return total


class WideScatter:
    def __init__(self, net, tile, out, got, acc, r1, r2, y, z, c, n):
        self.net, self.tile, self.out, self.got, self.acc, self.c = net, tile, out, got, acc, c
        self.group, self.slots = net.group(), (net.slot(), net.slot())

        def dev(y, z, c):
            return (wide_of(y, z, c), n)

        self.other = dev(y, z, 1 - c)

        def cols(ref, start, h):
            return ref.at[pl.ds(aligned(start, 16), 16), pl.ds(h * 1024, 1024)]

        def ring(me, device, part, ref, base):
            return Scatter(
                net, self.group, me, device, part,
                ref.at[pl.ds(base, 16)], (cols(ref, base, 0), cols(ref, base, 1)),
                ref.at[pl.ds(base + 16, 32)], lambda h: cols(ref, base + 16, h), lambda h: cols(ref, base + 32, h),
            )

        def first(base, one, two, device, k):
            return {
                j: ring(two, device, lambda i, h, j=j: cols(acc, base + i * 64 + (one + j) % 4 * 16, h), r1.at[k], j * 48)
                for j in (2, 1, 3, 0)
            }

        def second(base, one, two, device, k):
            return Direct(
                net, self.group, one, device,
                lambda i: acc.at[pl.ds(aligned(base + two * 64 + i * 16, 16), 16)], r2, k * 48,
            )

        def along_y(i):
            return dev(i, z, c)

        def along_z(i):
            return dev(y, i, c)

        self.one = (first(0, y, z, along_z, 0), first(256, z, y, along_y, 1))
        self.two = (second(0, y, z, along_y, 0), second(256, z, y, along_z, 1))

    def exchange(self):
        for p in range(2):
            mine = pl.ds(p * 256, 256)
            for i in range(4):
                cs = slice(i * COLS, (i + 1) * COLS)
                self.out[mine, cs] = self.tile(aligned(p * 512 + (1 - self.c) * 256, 256), cs).astype(BF16)
            self.net.copy(self.out.at[mine], self.got.at[mine], self.other, self.group, self.slots[p])

    def start(self):
        for p in range(2):
            mine = pl.ds(p * 256, 256)
            self.net.arrived(self.got.at[mine], self.slots[p])
            for i in range(4):
                cs = slice(i * COLS, (i + 1) * COLS)
                term = self.tile(aligned(p * 512 + self.c * 256, 256), cs)
                self.acc[mine, cs] = (term + self.got[mine, cs].astype(F32)).astype(BF16)
            for j in (2, 1, 3, 0):
                self.one[p][j].start_far()
            for j in (2, 1, 3, 0):
                self.one[p][j].start_right()
                self.one[p][j].start_left()

    def step(self, j):
        for x in self.one:
            x[j].step()

    def hand_on(self, j, also=None):
        for p, (x, t) in enumerate(zip(self.one, self.two)):
            r = x[j]
            r.finish()
            for h in range(2):
                v = r.half(h)
                r.part(r.me, h)[...] = v.astype(BF16)
                if also is not None:
                    also(p, (t.me + j) % 4, slice(h * 1024, (h + 1) * 1024), v)
            if j:
                t.send(j)

    def finish(self):
        for r in self.two:
            r.finish()

    def result(self, i, cs):
        return self.two[i].result(cs)

    def drain(self, ref):
        self.net.sent(ref.at[pl.ds(0, 992)], self.group)


def other_chips(y, z, c):
    for d in range(1, 16):
        yield wide_of((y + d // 4) % 4, (z + d % 4) % 4, c)


def greet(y, z, c, n):
    peers = [(wide_of((y + d) % 4, z, c), n) for d in (1, 3, 2)]
    peers += [(wide_of(y, (z + d) % 4, c), n) for d in (1, 3, 2)]
    peers += [(wide_of(y, z, 1 - c), n)]
    peers += [(wide_of(y, z, c), (n + d) % 4) for d in (1, 3, 2)]
    barrier = pltpu.get_barrier_semaphore()
    for p in peers:
        pl.semaphore_signal(barrier, inc=1, device_id=p, device_id_type=MESH)
    return lambda: pl.semaphore_wait(barrier, len(peers))


def repeat(count, step, body):
    def turn(i, _):
        for j in range(step):
            body(i * step + j)
        return 0

    lax.fori_loop(0, count // step, turn, 0)


def nt(a, b):
    return lax.dot_general(a, b, (((1,), (1,)), ((), ())), preferred_element_type=F32)


GELU_A = float(np.sqrt(2.0 / np.pi))
GELU_B = 0.044715


def dot(a, b):
    return jnp.dot(a, b, preferred_element_type=F32)


def lanes(shape):
    return lax.broadcasted_iota(jnp.int32, shape, len(shape) - 1)


def swap(x):
    return jnp.where(lanes(x.shape) < ROT // 2, pltpu.roll(x, 128 - ROT // 2, 1), pltpu.roll(x, ROT // 2, 1))


def block_kernel(
    dealing, lengths, i_tok, i_cot, i_wq, i_wk, i_wv, i_wu, i_wo, i_wd,
    i_gain, i_bias, i_bq, i_bk, i_bv, i_bo, i_bu, i_bd, cos_all, sin_all,
    o_res, o_ig, o_gain, o_bias, o_q, o_bq, o_k, o_bk, o_v, o_bv, o_o, o_bo, o_u, o_bu, o_f,
    tok, cot, wu, v_gain, v_bias, b_q, b_k, b_v, b_o, b_u, b_d,
    res, ig, grad_l, grad_u, grad_f, v_512, v_64, v_256,
    ln, g, w, wm, wmo, xs, gbs, xhat, cosine, sine, cosine_held, sine_held, slope, hb, dpre, kv, kk, xq, xd, od, dkvt, dkv, dkvp,
    rdkv, sum_f, sum_u, sum_l, r_f, r_u, r_l, out_1, got_1, acc_1, r1_1, r2_1, out_2, got_2, acc_2, r1_2, r2_2,
    trans, hidden, cmask, bsend, bfin, csend, clow, cfin, ssend, srecv, brecv, wrecv, nsum, hats, column, bias, index, there, kpos, send, recv, local, inward,
):
    y, z, c, n = coords()
    net = Net(send, recv, (wide_of(y, z, 1 - c), n))
    my_cols = pl.ds(aligned(n * COLS, COLS), COLS)
    me = wide_of(y, z, c)
    own_a, own_b = slot_a(c, z, y), slot_b(c, y, z)

    def to(m):
        return (me, m)

    def w_cols(i):
        return pl.ds(aligned(i * COLS, COLS), COLS)

    def share(i):
        return pl.ds(aligned(i * PART, PART), PART)

    loads = []

    def load(x, to):
        loads.append(pltpu.make_async_copy(x, to, inward.at[len(loads)]))
        loads[-1].start()

    load(i_tok, tok)
    load(i_wk, w.at[pl.ds(256, 64), my_cols])
    load(i_wv, w.at[pl.ds(320, 64), my_cols])
    load(i_wq, w.at[pl.ds(384, 64), my_cols])
    load(i_cot, cot)
    load(i_wu, wu)
    load(i_wo, wm.at[pl.ds(256, 64), my_cols])
    load(i_gain, v_gain)
    load(i_bias, v_bias)
    early = len(loads)
    load(i_wd, wm.at[pl.ds(0, 256), my_cols])
    for x, at in ((i_bq, b_q), (i_bk, b_k), (i_bv, b_v), (i_bo, b_o), (i_bu, b_u), (i_bd, b_d)):
        load(x, at)
    load(cos_all.at[n], cosine)
    load(sin_all.at[n], sine)
    all_greeted = greet(y, z, c, n)
    for x in loads[:early]:
        x.wait()
    w[0:256, my_cols] = wu[...].T
    for i in range(4):
        gbs[n, i : i + 1, :] = v_gain[:, i * 128 : i * 128 + 128]
        gbs[n, 4 + i : 5 + i, :] = v_bias[:, i * 128 : i * 128 + 128]
    xs[:, my_cols] = tok[share(n), :]
    row = lax.broadcasted_iota(jnp.int32, (BLOCK, COLS), 0)
    block = dealing[me]
    valid = block % (MAXLEN // BLOCK) * BLOCK + row < jnp.where(block < MAXLEN // BLOCK, lengths[0], lengths[1])
    cmask[...] = jnp.where(valid, cot[...], jnp.zeros_like(cot))
    mine = cmask[share(n), :]
    g[pl.ds(own_a, 16), my_cols] = mine[0:16]
    g[pl.ds(own_b, 16), my_cols] = mine[16:32]
    all_greeted()

    rings, turns = net.group(), net.group()
    tokens_in, gains_in, cot_in = net.slot(), net.slot(), net.slot()
    gains_out = net.group()
    for j in (1, 3, 2):
        m = (n + j) % 4
        net.copy(tok.at[share(m)], xs.at[:, my_cols], to(m), turns, tokens_in)
        net.copy(gbs.at[n], gbs.at[n], to(m), gains_out, gains_in)

    def x_ring(ref, start, count):
        half = count // 2
        return Ring(
            net, rings, n, to,
            lambda i: ref.at[pl.ds(start, count), w_cols(i)],
            lambda i, h: ref.at[pl.ds(start + h * half, half), w_cols(i)],
        )

    a_ring = x_ring(w, 256, 192)
    u_ring = x_ring(w, 0, 256)
    d_ring = x_ring(wm, 0, 256)
    o_ring = x_ring(wm, 256, 64)
    kv_ring = [
        Ring(
            net, rings, n, to,
            lambda i, s=s: kv.at[i, pl.ds(s * 32, 32)],
            lambda i, h, s=s: kv.at[i, pl.ds(s * 32 + h * 16, 16)],
        )
        for s in range(2)
    ]
    a_ring.start()
    for j in (1, 3, 2):
        m = (n + j) % 4
        for p, start in enumerate((own_a, own_b)):
            x = cmask.at[pl.ds(aligned(m * PART + p * 16, 16), 16)]
            net.copy(x, g.at[pl.ds(start, 16), my_cols], to(m), turns, cot_in)
    u_ring.start()
    o_ring.start()

    for x in loads[early:]:
        x.wait()
    at = lanes((8, 128))
    part = lax.broadcasted_iota(jnp.int32, (8, 128), 0)
    found = jnp.zeros((8, 128), jnp.int32)
    for b in range(NBLK):
        sy, sz, sc = b // 8, b // 2 % 4, b % 2
        found = jnp.where((part < 2) & (at == dealing[b]), jnp.where(part == 0, (sc * 4 + sz) * 4 + sy, 32 + (sc * 4 + sy) * 4 + sz), found)
        found = jnp.where((part == 2) & (at == (sc * 4 + sz) * 4 + sy), 2 * dealing[b], found)
        found = jnp.where((part == 2) & (at == 32 + (sc * 4 + sy) * 4 + sz), 2 * dealing[b] + 1, found)
        found = jnp.where((part == 3) & (at == (sc * 4 + sz) * 4 + sy), 2 * dealing[b] % 32, found)
        found = jnp.where((part == 3) & (at == 32 + (sc * 4 + sy) * 4 + sz), 2 * dealing[b] % 32 + 1, found)
    index[...] = found
    to_scalars = pltpu.make_async_copy(index, there, local.at[0])
    to_scalars.start()
    half = ROT // 2
    bias[:, 0:128] = b_u[0:1, :].astype(F32)
    bias[:, 128:256] = b_u[1:2, :].astype(F32)
    bias[:, 256:320] = b_k[...].astype(F32)
    bias[:, 320:384] = b_v[...].astype(F32)
    bias[:, 384:448] = b_q[...].astype(F32)
    bias[:, 448:464] = b_q[:, half:ROT].astype(F32)
    bias[:, 464:480] = b_q[:, 0:half].astype(F32)
    bias[:, 480:496] = b_k[:, half:ROT].astype(F32)
    bias[:, 496:512] = b_k[:, 0:half].astype(F32)
    for s in range(2):
        at = lanes((8, MAXLEN))
        kpos[s] = jnp.where(at < lengths[s], at, 1 << 20)
    wmo[0:64, :] = jnp.zeros((64, D), BF16)

    net.arrived(dpre.at[pl.ds(0, 96)], tokens_in)
    x = xs[...].astype(F32)
    mean = jnp.sum(x, 1, keepdims=True) / D
    var = jnp.sum(x * x, 1, keepdims=True) / D - mean * mean
    inv = lax.rsqrt(var + EPS)
    xhat[...] = (x - mean) * inv
    net.arrived(srecv.at[pl.ds(0, 3)], gains_in)
    for i in range(16):
        cs = slice(i * 128, (i + 1) * 128)
        low = (xhat[:, cs] * gbs[i // 4, i % 4 : i % 4 + 1, :] + gbs[i // 4, i % 4 + 4 : i % 4 + 5, :]).astype(BF16)
        ln[pl.ds(own_a, 16), cs] = low[0:16]
        ln[pl.ds(own_b, 16), cs] = low[16:32]

    lg = WideGather(net, ln, y, z, c, n)
    gg = WideGather(net, g, y, z, c, n)
    lg.start()
    to_scalars.wait()

    def hold(i):
        cosine_held[i] = cosine[there[3, i]]
        sine_held[i] = sine[there[3, i]]

    repeat(64, 8, hold)
    lg.near_one()
    a_ring.forward()
    d_ring.start()
    net.arrived(dpre.at[pl.ds(0, 96)], cot_in)
    lg.near_two(0)
    lg.far_one()
    gg.start()
    lg.near_two(3)
    lg.near_two(1)
    lg.near_two(2)
    lg.cross_near()
    gg.near_one()
    u_ring.forward()
    o_ring.forward()
    for j in (0, 3, 1, 2):
        lg.far_two(j)
    a_ring.finish()
    gg.near_two(0)
    gg.far_one()

    w[448:640, :] = w[256:448, :]
    w[640:656, :] = w[400:416, :]
    w[656:672, :] = w[384:400, :]
    w[672:688, :] = w[272:288, :]
    w[688:704, :] = w[256:272, :]

    lg.finish()
    x = (nt(ln[...], w[448:704, :]) + bias[:, 256:512]).reshape(64, 16, 256)
    a, b = x[:, :, 0:128], x[:, :, 128:256]
    kv[n] = (a * cosine_held[...] + pltpu.roll(b, 32, 2) * sine_held[...]).astype(BF16)
    kv_ring[0].start()
    kv_ring[1].start()
    x = (b * cosine_held[...] + pltpu.roll(b, 64, 2) * sine_held[...]) * (HEAD_DIM**-0.5)
    xq[...] = jnp.where(lanes((64, 16, 128)) < HEAD_DIM, x, 0.0).astype(BF16)
    gg.near_two(3)
    gg.near_two(1)
    gg.near_two(2)
    gg.cross_near()
    u_ring.finish()

    def units(i, _):
        r = pl.ds(aligned(i * 512, 512), 512)
        v = nt(ln[r, :], w[0:256, :]) + bias[:, 0:256]
        t = jnp.tanh(GELU_A * (v + GELU_B * (v * v * v)))
        hb[r, :] = (0.5 * v * (1.0 + t)).astype(BF16)
        slope[r, :] = 0.5 * (1.0 + t) + 0.5 * v * (1.0 - t * t) * (GELU_A * (1.0 + 3.0 * GELU_B * (v * v)))
        return 0

    lax.fori_loop(0, 2, units, 0)
    hidden[0:256, :] = hb[...].T
    hidden[256:288, :] = jnp.ones((32, ROWS), BF16)
    def scatter_cols(buf, count, r):
        half = count // 2
        return Scatter(
            net, net.group(), n, to,
            lambda i, h: buf.at[pl.ds(h * half, half), w_cols(i)],
            r.at[0], (r.at[0, pl.ds(0, half)], r.at[0, pl.ds(half, half)]),
            r.at[pl.ds(1, 2)], lambda h: r.at[1, pl.ds(h * half, half)], lambda h: r.at[2, pl.ds(h * half, half)],
        )

    f_sum = scatter_cols(sum_f, 288, r_f)
    u_sum = scatter_cols(sum_u, 256, r_u)
    l_sum = scatter_cols(sum_l, 256, r_l)

    def weight_f(i, _):
        cs = pl.ds(aligned(i * 1024, 1024), 1024)
        sum_f[:, cs] = dot(hidden[...], g[:, cs]).astype(BF16)
        return 0

    kv_ring[0].forward()
    o_ring.finish()
    wmo[64:128, :] = wm[256:320, :]
    for j in (0, 3, 1, 2):
        gg.far_two(j)
    kv_ring[1].forward()
    d_ring.forward()

    gg.finish()
    hats_out, hats_in = net.group(), net.slot()
    hats[y] = xhat[0:16, :]
    hats[4 + z] = xhat[16:32, :]
    for d in (1, 3, 2):
        net.copy(xhat.at[pl.ds(0, 16)], hats.at[y], (wide_of((y + d) % 4, z, c), n), hats_out, hats_in)
        net.copy(xhat.at[pl.ds(16, 16)], hats.at[4 + z], (wide_of(y, (z + d) % 4, c), n), hats_out, hats_in)
    lax.fori_loop(0, 2, weight_f, 0)

    def grad_o(i, _):
        r = pl.ds(aligned(i * 512, 512), 512)
        xd[pl.ds(i * 32, 32)] = nt(g[r, :], wmo[...]).astype(BF16).reshape(32, 16, 128)
        return 0

    lax.fori_loop(0, 2, grad_o, 0)

    def gather_keys(i):
        for m in range(4):
            for p in range(2):
                kk[pl.ds(aligned(i * BLOCK + m * PART + p * 16, 16), 16), :] = kv[m, there[p, i]]

    def attend(s, t):
        keys = 512 * (t + 1)
        held = [there[k % 2, s * 16 + t * 4 + k // 2] for k in range(8)]
        x = jnp.concatenate([xq[i] for i in held] + [xd[i] for i in held], 0)
        near = kk[pl.ds(s * MAXLEN, keys), :]
        both = nt(x, near)
        i = lax.broadcasted_iota(jnp.int32, (128, 1), 0)
        qpos = (4 * t + i // PART) * BLOCK + n * PART + i % PART
        scores = jnp.where(kpos[s, 0:1, 0:keys] <= qpos, both[0:128], -1e30)
        e = jnp.exp(scores - jnp.max(scores, 1, keepdims=True))
        p = e * (1.0 / jnp.sum(e, 1, keepdims=True))
        dp = both[128:256]
        ds = p * (dp - jnp.sum(p * dp, 1, keepdims=True))
        yy = jnp.concatenate([ds.astype(BF16), p.astype(BF16)], 0)
        back = dot(yy, near)
        back = jnp.where(lanes((128, 128)) < HEAD_DIM, back[0:128] * (HEAD_DIM**-0.5), back[128:256])
        od[pl.ds(s * 32 + t * 8, 8)] = back.reshape(8, 16, 128)
        grads = dot(x.T, yy)
        if t == 3:
            dkvt[s, :, 0:keys] = grads
        else:
            dkvt[s, :, 0:keys] += grads

    keys_out = net.group()

    def key_sum(s, part):
        def rows(start, count):
            return pl.ds(s * 512 + part * 256 + start, count)

        return Scatter(
            net, keys_out, n, to,
            lambda i, h: dkv.at[i, rows(h * 128, 128)],
            rdkv.at[0, rows(0, 256)], (rdkv.at[0, rows(0, 128)], rdkv.at[0, rows(128, 128)]),
            rdkv.at[pl.ds(1, 2), rows(0, 256)],
            lambda h: rdkv.at[1, rows(h * 128, 128)],
            lambda h: rdkv.at[2, rows(h * 128, 128)],
        )

    def turn_keys(s, h):
        for i in range(8 * h, 8 * h + 8):
            t = dkvt[s, :, i * BLOCK : (i + 1) * BLOCK].T.astype(BF16)
            for m in range(4):
                dkv[m, s * 512 + i * PART : s * 512 + (i + 1) * PART, :] = t[m * PART : (m + 1) * PART]

    kv_sum = [key_sum(0, 1), key_sum(0, 0), key_sum(1, 1), key_sum(1, 0)]
    kv_ring[0].finish()
    kv_ring[1].finish()
    f_sum.start()
    repeat(32, 4, gather_keys)
    attend(0, 3)
    attend(0, 2)
    turn_keys(0, 1)
    kv_sum[0].start()
    attend(0, 1)
    attend(0, 0)
    turn_keys(0, 0)
    kv_sum[1].start()
    attend(1, 3)
    attend(1, 2)
    turn_keys(1, 1)
    kv_sum[2].start()
    attend(1, 1)
    attend(1, 0)
    turn_keys(1, 0)
    kv_sum[3].start()

    def unrope(s):
        x = od[pl.ds(s * 32, 32)].reshape(512, 128)
        od[pl.ds(s * 32, 32)] = (x * cosine[...].reshape(512, 128) - swap(x) * sine[...].reshape(512, 128)).reshape(32, 16, 128)

    unrope(0)
    unrope(1)

    def place(i):
        dpre[pl.ds(aligned(i * 16, 16), 16), 384:512] = od[there[2, i]].astype(BF16)

    repeat(64, 8, place)

    def dln_tile(start, cs):
        r = pl.ds(start, 256)
        return dot(dpre[r, 0:448], w[0:448, cs])

    def branch_tile(start, cs):
        r = pl.ds(start, 256)
        return dot(hb[r, :], wm[0:256, cs]) + dot(dpre[r, 384:512], wmo[:, cs])

    branch = WideScatter(net, branch_tile, out_1, got_1, acc_1, r1_1, r2_1, y, z, c, n)
    dln = WideScatter(net, dln_tile, out_2, got_2, acc_2, r1_2, r2_2, y, z, c, n)
    d_ring.finish()
    branch.exchange()
    kv_sum[0].step()
    kv_sum[1].step()

    def grad_units(i, _):
        r = pl.ds(aligned(i * 512, 512), 512)
        dpre[r, 0:256] = (nt(g[r, :], wm[0:256, :]) * slope[r, :]).astype(BF16)
        return 0

    lax.fori_loop(0, 2, grad_units, 0)

    kv_sum[2].step()
    kv_sum[3].step()
    branch.start()
    trans[...] = dpre[:, 0:256].T

    def weight_u(i, _):
        cs = pl.ds(aligned(i * 1024, 1024), 1024)
        sum_u[:, cs] = dot(trans[...], ln[:, cs]).astype(BF16)
        return 0

    lax.fori_loop(0, 2, weight_u, 0)
    u_sum.start()
    def unrope_keys(s):
        r = pl.ds(s * 512, 512)
        x = dkv[n, r, :].astype(F32) + (rdkv[1, r, :].astype(F32) + rdkv[2, r, :].astype(F32))
        dkvp[pl.ds(s * 32, 32)] = (x * cosine[...].reshape(512, 128) - swap(x) * sine[...].reshape(512, 128)).reshape(32, 16, 128)

    kv_sum[0].finish()
    kv_sum[1].finish()
    unrope_keys(0)
    kv_sum[2].finish()
    kv_sum[3].finish()
    unrope_keys(1)

    def place_keys(i):
        dpre[pl.ds(aligned(i * 16, 16), 16), 256:384] = dkvp[there[2, i]].astype(BF16)

    repeat(64, 8, place_keys)
    dln.exchange()
    for j in (2, 1, 3, 0):
        branch.step(j)
    dln.start()
    trans[...] = dpre[:, 256:512].T

    def weight_l(i, _):
        cs = pl.ds(aligned(i * 1024, 1024), 1024)
        sum_l[0:192, cs] = dot(trans[0:192, :], ln[:, cs]).astype(BF16)
        sum_l[192:256, cs] = dot(trans[192:256, :], g[:, cs]).astype(BF16)
        return 0

    lax.fori_loop(0, 2, weight_l, 0)
    l_sum.start()
    f_sum.step()
    for j in (2, 1, 3, 0):
        dln.step(j)
    for j in (2, 1, 3, 0):
        branch.hand_on(j)
    u_sum.step()

    def norm_sums(p, i, cs, v):
        column[0:1, cs] += jnp.sum(v * hats[4 * p + i, :, cs], 0, keepdims=True)
        column[1:2, cs] += jnp.sum(v, 0, keepdims=True)

    column[...] = jnp.zeros((8, D), F32)
    net.arrived(hats.at[pl.ds(0, 6)], hats_in)
    for j in (2, 1, 3, 0):
        dln.hand_on(j, norm_sums)
    norm_out, norm_in, final_out, final_in, all_out, all_in = net.group(), net.slot(), net.group(), net.slot(), net.group(), net.slot()
    for m in range(4):
        for k in range(2):
            for i in range(4):
                ssend[m, 4 * k + i : 4 * k + i + 1, :] = column[k : k + 1, m * COLS + i * 128 : m * COLS + i * 128 + 128]
    chip = y * 4 + z
    wrecv[chip] = ssend[...]
    for p in other_chips(y, z, c):
        net.copy(ssend, wrecv.at[chip], (p, n), norm_out, norm_in)
    sums = jnp.sum(dpre[...].astype(F32), 0, keepdims=True)
    for i in range(4):
        brecv[n, i : i + 1, :] = sums[:, i * 128 : i * 128 + 128]
    small_out, small_in, branch_out, branch_in = net.group(), net.slot(), net.group(), net.slot()
    for j in (1, 3, 2):
        net.copy(brecv.at[n], brecv.at[n], to((n + j) % 4), small_out, small_in)
    l_sum.step()
    branch.finish()
    for i in range(2):
        for h in range(2):
            cs = slice(h * 1024, (h + 1) * 1024)
            bsend[i * 16 : (i + 1) * 16, cs] = branch.result(i, cs).astype(BF16)
    bfin[share(n), :] = bsend[:, my_cols]
    for j in (1, 3, 2):
        m = (n + j) % 4
        net.copy(bsend.at[:, w_cols(m)], bfin.at[share(n)], to(m), branch_out, branch_in)
    dln.finish()

    for i in range(2):
        for h in range(2):
            cs = slice(h * 1024, (h + 1) * 1024)
            csend[i * 16 : (i + 1) * 16, cs] = dln.result(i, cs)
    for i in range(16):
        cs = slice(i * 128, (i + 1) * 128)
        csend[:, cs] = csend[:, cs] * gbs[i // 4, i % 4 : i % 4 + 1, :]
    grad = csend[...]
    first = jnp.sum(grad, 1, keepdims=True) / D
    second = jnp.sum(grad * xhat[...], 1, keepdims=True) / D
    x = xs[...].astype(F32)
    mean = jnp.sum(x, 1, keepdims=True) / D
    var = jnp.sum(x * x, 1, keepdims=True) / D - mean * mean
    clow[...] = (lax.rsqrt(var + EPS) * (grad - first - xhat[...] * second)).astype(BF16)
    cfin[share(n), :] = clow[:, my_cols]
    for j in (1, 3, 2):
        m = (n + j) % 4
        net.copy(clow.at[:, w_cols(m)], cfin.at[share(n)], to(m), final_out, final_in)
    net.arrived(wrecv.at[pl.ds(0, 15)], norm_in)
    nsum[...] = jnp.sum(wrecv[...], 0)
    srecv[n * 2 + c] = nsum[n]
    for j in (1, 3, 2, 0):
        m = (n + j) % 4
        for d in (0, 1) if j else (1,):
            net.copy(nsum.at[m], srecv.at[n * 2 + c], (wide_of(y, z, (c + d) % 2), m), all_out, all_in)
    outs = []

    def give(x, to):
        outs.append(pltpu.make_async_copy(x, to, local.at[1 + len(outs)]))
        outs[-1].start()

    f_sum.finish()
    for h in range(2):
        grad_f[h * 144 : (h + 1) * 144, :] = f_sum.half(h)
    v_512[2] = grad_f[256:257, :]
    give(grad_f.at[pl.ds(0, 256)], o_f)
    give(v_512.at[2], o_bo)
    u_sum.finish()
    for h in range(2):
        grad_u[:, h * 128 : (h + 1) * 128] = u_sum.half(h).T
    give(grad_u, o_u)
    l_sum.finish()
    for h in range(2):
        grad_l[h * 128 : (h + 1) * 128, :] = l_sum.half(h)
    for i, x in enumerate((o_k, o_v, o_q, o_o)):
        give(grad_l.at[pl.ds(64 * i, 64)], x)
    net.arrived(dpre.at[pl.ds(0, 96)], branch_in)
    block = dealing[me]
    valid = block % (MAXLEN // BLOCK) * BLOCK + row < jnp.where(block < MAXLEN // BLOCK, lengths[0], lengths[1])
    valid = valid[:, 0:128]
    for i in range(4):
        cs = slice(i * 128, i * 128 + 128)
        base = bfin[:, cs].astype(F32) + (b_o[i : i + 1, :].astype(F32) + b_d[i : i + 1, :].astype(F32))
        res[:, cs] = (tok[:, cs].astype(F32) + jnp.where(valid, base, 0.0)).astype(BF16)
    give(res, o_res)
    net.arrived(srecv.at[pl.ds(0, 3)], small_in)
    sums = (brecv[0] + brecv[1]) + (brecv[2] + brecv[3])
    v_256[:, 0:128] = sums[0:1]
    v_256[:, 128:256] = sums[1:2]
    v_64[0] = sums[2:3, 0:64]
    v_64[1] = sums[2:3, 64:128]
    v_64[2] = sums[3:4, 0:64]
    give(v_256, o_bu)
    for i, x in enumerate((o_bk, o_bv, o_bq)):
        give(v_64.at[i], x)
    net.arrived(cfin.at[pl.ds(0, 96)], final_in)
    ig[...] = cot[...].astype(F32) + cfin[...].astype(F32)
    give(ig, o_ig)
    net.arrived(srecv.at[pl.ds(0, 7)], all_in)
    sums = jnp.sum(srecv[...], 0)
    for i in range(4):
        v_512[0, :, i * 128 : i * 128 + 128] = sums[i : i + 1]
        v_512[1, :, i * 128 : i * 128 + 128] = sums[4 + i : 5 + i]
    give(v_512.at[0], o_gain)
    give(v_512.at[1], o_bias)

    lg.drain()
    gg.drain()
    branch.drain(ln)
    dln.drain(ln)
    net.sent(ln.at[pl.ds(0, 768)], rings)
    net.sent(ln.at[pl.ds(0, 192)], keys_out)
    net.sent(dpre.at[pl.ds(0, 864)], f_sum.group)
    net.sent(dpre.at[pl.ds(0, 768)], u_sum.group)
    net.sent(dpre.at[pl.ds(0, 768)], l_sum.group)
    net.sent(dpre.at[pl.ds(0, 192)], turns)
    net.sent(srecv.at[pl.ds(0, 3)], gains_out)
    net.sent(srecv.at[pl.ds(0, 3)], small_out)
    net.sent(dpre.at[pl.ds(0, 96)], branch_out)
    net.sent(wrecv.at[pl.ds(0, 15)], norm_out)
    net.sent(cfin.at[pl.ds(0, 96)], final_out)
    net.sent(srecv.at[pl.ds(0, 7)], all_out)
    net.sent(hats.at[pl.ds(0, 6)], hats_out)
    for x in outs:
        x.wait()
    assert (net.groups, net.slots) == (SENDS, ARRIVALS), (net.groups, net.slots)


RESULTS = (
    (BLOCK, COLS), (1, COLS), (1, COLS), (64, COLS), (1, 64), (64, COLS), (1, 64), (64, COLS), (1, 64), (64, COLS), (1, COLS),
    (COLS, UNITS), (1, UNITS), (UNITS, COLS),
)


def call_block(*args):
    anywhere = pl.BlockSpec(memory_space=pl.ANY)
    shape = jax.ShapeDtypeStruct

    def buf(dtype, *size):
        return pltpu.VMEM(size, dtype)

    wide = [buf(BF16, 512, D), buf(BF16, 512, D), buf(BF16, 512, D), buf(BF16, 2, 192, D), buf(BF16, 96, D)]
    return pl.pallas_call(
        block_kernel,
        out_shape=(shape((BLOCK, COLS), BF16), *(shape(x, F32) for x in RESULTS)),
        in_specs=[pl.BlockSpec(memory_space=pltpu.SMEM)] * 2 + [anywhere] * 18,
        out_specs=(anywhere,) * 15,
        scratch_shapes=[
            buf(BF16, BLOCK, COLS),
            buf(BF16, BLOCK, COLS),
            buf(BF16, COLS, UNITS),
            buf(F32, 1, COLS),
            buf(F32, 1, COLS),
            buf(BF16, 1, 64),
            buf(BF16, 1, 64),
            buf(BF16, 1, 64),
            buf(BF16, 4, 128),
            buf(BF16, 2, 128),
            buf(BF16, 4, 128),
            buf(BF16, BLOCK, COLS),
            buf(F32, BLOCK, COLS),
            buf(F32, 256, COLS),
            buf(F32, COLS, UNITS),
            buf(F32, 288, COLS),
            buf(F32, 3, 1, COLS),
            buf(F32, 3, 1, 64),
            buf(F32, 1, UNITS),
            buf(BF16, ROWS, D),
            buf(BF16, ROWS, D),
            buf(BF16, 704, D),
            buf(BF16, 320, D),
            buf(BF16, 128, D),
            buf(BF16, PART, D),
            buf(F32, 4, 8, 128),
            buf(F32, PART, D),
            buf(F32, 32, 16, 128),
            buf(F32, 32, 16, 128),
            buf(F32, 64, 16, 128),
            buf(F32, 64, 16, 128),
            buf(F32, ROWS, UNITS),
            buf(BF16, ROWS, UNITS),
            buf(BF16, ROWS, 512),
            buf(BF16, 4, 64, 16, 128),
            buf(BF16, 2 * MAXLEN, 128),
            buf(BF16, 64, 16, 128),
            buf(BF16, 64, 16, 128),
            buf(F32, 64, 16, 128),
            buf(F32, 2, 128, MAXLEN),
            buf(BF16, 4, ROWS, 128),
            buf(F32, 64, 16, 128),
            buf(BF16, 3, ROWS, 128),
            buf(BF16, 288, D),
            buf(BF16, 256, D),
            buf(BF16, 256, D),
            buf(BF16, 3, 288, COLS),
            buf(BF16, 3, 256, COLS),
            buf(BF16, 3, 256, COLS),
            *wide,
            *wide,
            buf(BF16, 256, ROWS),
            buf(BF16, 288, ROWS),
            buf(BF16, BLOCK, COLS),
            buf(BF16, PART, D),
            buf(BF16, BLOCK, COLS),
            buf(F32, PART, D),
            buf(BF16, PART, D),
            buf(BF16, BLOCK, COLS),
            buf(F32, 4, 8, 128),
            buf(F32, 8, 8, 128),
            buf(F32, 4, 8, 128),
            buf(F32, 16, 4, 8, 128),
            buf(F32, 4, 8, 128),
            buf(F32, 8, 16, D),
            buf(F32, 8, D),
            buf(F32, 1, COLS),
            buf(jnp.int32, 8, 128),
            pltpu.SMEM((8, 128), jnp.int32),
            buf(jnp.int32, 2, 8, MAXLEN),
            pltpu.SemaphoreType.DMA((SENDS,)),
            pltpu.SemaphoreType.DMA((ARRIVALS,)),
            pltpu.SemaphoreType.DMA((18,)),
            pltpu.SemaphoreType.DMA((18,)),
        ],
        compiler_params=pltpu.CompilerParams(collective_id=0, has_side_effects=True, vmem_limit_bytes=63 * 2**20),
    )(*args)


def relay_kernel(*refs):
    given, taken, held, here, there = refs[:15], refs[15:31], refs[31:46], refs[46], refs[47]
    order = sorted(range(15), key=lambda i: -given[i].size)
    come = [pltpu.make_async_copy(given[i], held[i], here.at[i]) for i in range(15)]
    go = [pltpu.make_async_copy(held[i], taken[i], there.at[i]) for i in range(15)]
    go.append(pltpu.make_async_copy(held[11], taken[15], there.at[15]))
    for i in order:
        come[i].start()
    for i in order:
        come[i].wait()
        go[i].start()
        if i == 11:
            go[15].start()
    for x in go:
        x.wait()


def relay(arrays):
    anywhere = pl.BlockSpec(memory_space=pl.ANY)
    return pl.pallas_call(
        relay_kernel,
        out_shape=tuple(jax.ShapeDtypeStruct(x.shape, x.dtype) for x in (*arrays, arrays[11])),
        in_specs=[anywhere] * 15,
        out_specs=(anywhere,) * 16,
        scratch_shapes=[pltpu.VMEM(x.shape, x.dtype) for x in arrays]
        + [pltpu.SemaphoreType.DMA((15,)), pltpu.SemaphoreType.DMA((16,))],
        compiler_params=pltpu.CompilerParams(vmem_limit_bytes=62 * 2**20),
    )(*arrays)


def on_device(
    tokens, ln_gain, ln_bias, w_query, b_query, w_key, b_key, w_value, b_value, w_out, b_out,
    w_fc1, b_fc1, w_fc2, b_fc2, cotangent, lengths, dealing,
):
    cosine, sine = (
        np.ascontiguousarray(t.reshape(MAXLEN // BLOCK, 4, PART, 128).transpose(1, 0, 2, 3)).reshape(4, -1, 16, 128)
        for t in rope_tables()
    )
    out = call_block(
        dealing, lengths, tokens, cotangent, w_query.T, w_key.T, w_value.T, w_fc1, w_out, w_fc2,
        ln_gain[None], ln_bias[None], b_query[None], b_key[None], b_value[None], b_out.reshape(-1, 128),
        b_fc1.reshape(-1, 128), b_fc2.reshape(-1, 128),
        jnp.asarray(cosine), jnp.asarray(sine),
    )
    out = list(relay(out))
    for i in (4, 6, 8):
        out[i] = out[i].T
    for i in (2, 3, 5, 7, 9, 11, 13, 15):
        out[i] = out[i][0]
    return tuple(out)


def solution(mesh):
    rows, col, units = P("wide", "narrow"), P("narrow"), P("wide")
    weight, out = P("narrow", "wide"), P("wide", "narrow")
    placed = (
        rows, col, col, weight, units, weight, units, weight, units, out, col, weight, units, out, col, rows, P(), P(),
    )
    given = (
        rows, rows, col, col, weight, units, weight, units, weight, units, out, col, weight, units, out, col,
    )
    return jax.shard_map(on_device, mesh=mesh, in_specs=placed, out_specs=given, check_vma=False)
```
